128 devices in a mesh: seq: 32 (over z, x, core), head: 4 (over y).
Axes of the slice: x: 4, y: 4, z: 4, core: 2. Of those that a mesh axis runs over, the one named last changes fastest.
Arguments:
- query_heads: bfloat16 [4, 4, 64, 192], P(None, None, 'head'), may hold values from -6 to 6
- up_keys: bfloat16 [64, 128, 512], P('head'), may hold values from -0.5 to 0.5
- up_values: bfloat16 [64, 512, 128], P('head'), may hold values from -0.25 to 0.25
- latent_cache: bfloat16 [4, 262144, 576], P(None, ('seq', 'head')), may hold values from -120 to 120
- new_latent: bfloat16 [4, 4, 576], replicated, may hold values from -24 to 24
- context_lengths: int32 [4], replicated, may hold values from 32768 to 262144, as said below
- positions: int32 [4], replicated, may hold values from 0 to 262143
Outputs:
- attended: bfloat16 [4, 4, 64, 128], P(None, None, 'head')
The draws below stay inside these ranges and needn't reach their ends.
Inputs may be any that keep to these rules, and one draw needn't show every extreme that they name: `context_lengths`: some request uses all 262144 cached positions.
All inputs are finite; a program needn't handle non-finite values.
Results may differ from the reference program's by a relative error of at most 0.019.
The reference program's roundings to bfloat16 on the way count: a program that leaves them out, or rounds other values in their place, can miss the bound.
Values may be sent and summed in bfloat16 or wider, within the bound.
No kernel may reach another device: no remote copies, remote signals or barrier semaphores. Data moves between devices by JAX's collectives and lax.ppermute only.
A program may use at most 512 MiB of HBM per device.

```python
import jax
import jax.numpy as jnp
from jax import lax

HEADS = 64
NOPE = 128
ROPE = 64
KV = 512
VD = 128
BATCH = 4
STEPS = 4
CTX = 262144


def draw_latent_cache(key, part):
    key = jax.random.fold_in(key, 11)
    noise_key = jax.random.fold_in(key, 0)
    values = 2.0 * jnp.clip(jax.random.normal(noise_key, (BATCH, CTX, KV + ROPE), jnp.float32), -6.0, 6.0)
    return values.astype(jnp.bfloat16)


def draw_context_lengths(key, part):
    key = jax.random.fold_in(key, 23)
    length_key, longest_key = jax.random.split(key)
    lengths = jax.random.randint(length_key, (BATCH,), CTX // 8, CTX + 1, jnp.int32)
    longest = jax.random.randint(longest_key, (), 0, BATCH, jnp.int32)
    return jnp.where(jnp.arange(BATCH, dtype=jnp.int32) == longest, CTX, lengths).astype(jnp.int32)


def touch_ends(array, stream_key, smallest, largest):
    longest = array.shape.index(max(array.shape))
    spots = []
    for shift in (0, 1):
        where = [jax.random.randint(jax.random.fold_in(stream_key, axis), (), 0, length) for axis, length in enumerate(array.shape)]
        where[longest] = (where[longest] + shift) % array.shape[longest]
        spots.append(tuple(where))
    return array.at[spots[0]].set(smallest).at[spots[1]].set(largest)


def block_scale(key, extent, shards, low, top_value):
    def one(axis_at, shards_of):
        draws = jax.random.uniform(jax.random.fold_in(jax.random.fold_in(key, 6), axis_at), (shards_of,), jnp.float32, low / len(shards), top_value / len(shards))
        return jnp.repeat(jnp.exp(draws), extent[axis_at] // shards_of).reshape((-1,) + (1,) * (len(extent) - axis_at - 1))

    factor_of = one(*shards[0])
    for cut in shards[1:]:
        factor_of = factor_of * one(*cut)
    return factor_of


def noise(key, shape, scale, bound, pieces=(), kind=jnp.bfloat16):
    drawn = scale * jax.random.normal(key, shape, jnp.float32)
    if pieces:
        drawn = drawn * block_scale(key, shape, pieces, -0.22, 0.18)
    return jnp.clip(drawn, -bound, bound).astype(kind)


def setup_inputs(seed: int = 0) -> dict:
    keys = jax.random.split(jax.random.key(seed), 8)
    query_heads = noise(keys[0], (STEPS, BATCH, HEADS, NOPE + ROPE), 1.0, 6.0, ((2, 4),))
    up_keys = noise(keys[1], (HEADS, NOPE, KV), NOPE ** -0.5, 0.5, ((0, 4),))
    up_values = noise(keys[2], (HEADS, KV, VD), KV ** -0.5, 0.25, ((0, 4),))
    latent_cache = draw_latent_cache(jax.random.fold_in(keys[7], 71), 0)
    new_latent = noise(keys[4], (STEPS, BATCH, KV + ROPE), 4.0, 24.0)
    context_lengths = draw_context_lengths(jax.random.fold_in(keys[7], 71), 0)
    positions = touch_ends(jax.random.randint(keys[6], (BATCH,), 0, CTX), jax.random.fold_in(keys[6], 1), 0, CTX - 1).astype(jnp.int32)
    return {"query_heads": query_heads, "up_keys": up_keys, "up_values": up_values, "latent_cache": latent_cache, "new_latent": new_latent, "context_lengths": context_lengths, "positions": positions}


rope_base = 50000.0
masked_score = -1.0e30


def rotate(values, where_at):
    halfway = values.shape[-1] // 2
    counter = jnp.arange(halfway, dtype=jnp.float32)
    inverse = jnp.power(jnp.float32(rope_base), -2.0 * counter / values.shape[-1])
    angles = where_at.astype(jnp.float32)[..., None] * inverse
    cosine = jnp.cos(angles)
    sine_part = jnp.sin(angles)
    leading = values[..., :halfway]
    trailing = values[..., halfway:]
    return jnp.concatenate([leading * cosine - trailing * sine_part, trailing * cosine + leading * sine_part], axis=-1)


def build_new_keys(new_latent, pos_grid, latent_width):
    rotated = rotate(new_latent[..., latent_width:].astype(jnp.float32), pos_grid).astype(jnp.bfloat16)
    return jnp.concatenate([new_latent[..., :latent_width], rotated], axis=-1)


def reference(query_heads, up_keys, up_values, latent_cache, new_latent, context_lengths, positions):
    pos_grid = positions[None, :] + jnp.arange(STEPS, dtype=jnp.int32)[:, None]
    query_latent = jnp.einsum("sbhn,hnc->sbhc", query_heads[..., :NOPE].astype(jnp.float32), up_keys.astype(jnp.float32)).astype(jnp.bfloat16)
    query_rope = rotate(query_heads[..., NOPE:].astype(jnp.float32), pos_grid[:, :, None]).astype(jnp.bfloat16)
    queries = jnp.concatenate([query_latent, query_rope], axis=-1)
    new_keys = build_new_keys(new_latent, pos_grid, KV)
    softmax_scale = float(NOPE + ROPE) ** -0.5
    row_step = jnp.repeat(jnp.arange(STEPS, dtype=jnp.int32), HEADS)

    def one_request(request_item):
        query_block, cache_block, fresh_keys, length = request_item
        query_rows = query_block.reshape(STEPS * HEADS, KV + ROPE)
        all_keys = jnp.concatenate([cache_block, fresh_keys], axis=0)
        scores = jnp.dot(query_rows, all_keys.T, preferred_element_type=jnp.float32) * softmax_scale
        cache_visible = jnp.arange(CTX, dtype=jnp.int32) < length
        fresh_visible = jnp.arange(STEPS, dtype=jnp.int32)[None, :] <= row_step[:, None]
        visible = jnp.concatenate([jnp.broadcast_to(cache_visible[None, :], (STEPS * HEADS, CTX)), fresh_visible], axis=1)
        scores = jnp.where(visible, scores, masked_score)
        highest = jnp.max(scores, axis=1, keepdims=True)
        weights = jnp.where(visible, jnp.exp(scores - highest), 0.0)
        weight_sum = jnp.sum(weights, axis=1, keepdims=True)
        weighted = jnp.dot(weights.astype(jnp.bfloat16), all_keys[:, :KV], preferred_element_type=jnp.float32)
        return (weighted / weight_sum).reshape(STEPS, HEADS, KV)

    latent_out = lax.map(one_request, (jnp.swapaxes(queries, 0, 1), latent_cache, jnp.swapaxes(new_keys, 0, 1), context_lengths))
    return jnp.einsum("bshc,hcv->sbhv", latent_out.astype(jnp.float32), up_values.astype(jnp.float32), precision=lax.Precision.HIGHEST).astype(jnp.bfloat16)
```

```python
import functools

import jax
import jax.numpy as jnp
from jax import lax
from jax.experimental import pallas as pl
from jax.experimental.pallas import tpu as pltpu
from jax.sharding import Mesh, PartitionSpec as P

rope_base = 50000.0
masked_score = -1e30
lowest_max = -1e29
log2_e = 1.4426950408889634
bf16 = jnp.bfloat16
f32 = jnp.float32


def rope_tables(pos_grid, width):
    counter = jnp.arange(width // 2, dtype=f32)
    inverse = jnp.power(f32(rope_base), -2.0 * counter / width)
    angles = pos_grid.reshape(-1).astype(f32)[:, None] * inverse
    cosine = jnp.cos(angles)
    sine = jnp.sin(angles)
    return jnp.concatenate([cosine, cosine], -1), jnp.concatenate([-sine, sine], -1)


def swap_halves(values):
    half = values.shape[-1] // 2
    return jnp.concatenate([values[..., half:], values[..., :half]], axis=-1)


def queries_kernel(steps, requests, q_ref, up_ref, new_ref, cos_ref, sin_ref, out_ref, keys_ref, q_f32, lat):
    pairs, heads, _ = q_ref.shape
    nope, width = up_ref.shape[1], up_ref.shape[2]
    q_f32[...] = q_ref[:, :, :nope].astype(f32)
    for h in range(heads):
        lat[:, h, :] = jnp.dot(q_f32[:, h, :].astype(bf16), up_ref[h], preferred_element_type=f32)
    cos = cos_ref[...]
    sin = sin_ref[...]
    rope = q_ref[:, :, nope:].astype(f32)
    rope = (rope * cos[:, None, :] + swap_halves(rope) * sin[:, None, :]).astype(bf16)
    for s in range(steps):
        for b in range(requests):
            row = jnp.concatenate([lat[s * requests + b].astype(bf16), rope[s * requests + b]], axis=-1)
            for copy in range(out_ref.shape[0]):
                out_ref[copy, b, s * heads : (s + 1) * heads, :] = row
    new = new_ref[...]
    tail = new[:, width:].astype(f32)
    tail = (tail * cos + swap_halves(tail) * sin).astype(bf16)
    keys_ref[...] = jnp.concatenate([new[:, :width], tail], axis=-1)


def attention_kernel(
    scale, steps, heads, info_ref, q_ref, k_ref, new_ref, out_ref, stat_ref, scores, acc, top, total
):
    owners = q_ref.shape[0]
    rows = owners * q_ref.shape[2]
    cached = k_ref.shape[1]
    width = out_ref.shape[3]
    chunk = 512
    request = info_ref[0] + pl.program_id(0)
    limit = info_ref[3 + request] - info_ref[1]
    queries = q_ref[:, 0].reshape(rows, q_ref.shape[3])

    for c in range(0, cached, chunk):
        scores[:, c : c + chunk] = (
            lax.dot_general(
                queries, k_ref[0, c : c + chunk, :], (((1,), (1,)), ((), ())), preferred_element_type=f32
            )
            * scale
        )

    @pl.when(limit < cached)
    def _():
        column = lax.broadcasted_iota(jnp.int32, (rows, cached), 1)
        scores[...] = jnp.where(column < limit, scores[...], masked_score)

    highest = jnp.maximum(jnp.max(scores[...], axis=1, keepdims=True), lowest_max)
    weight_sum = jnp.zeros((rows, 1), f32)
    for c in range(0, cached, chunk):
        weights = jnp.exp2(scores[:, c : c + chunk] - highest)
        weight_sum += jnp.sum(weights, axis=1, keepdims=True)
        part = jnp.dot(weights.astype(bf16), k_ref[0, c : c + chunk, :width], preferred_element_type=f32)
        if c == 0:
            acc[...] = part
        else:
            acc[...] += part
    top[...] = jnp.broadcast_to(highest, top.shape)
    total[...] = jnp.broadcast_to(weight_sum, total.shape)

    @pl.when(info_ref[2] == request)
    def _():
        fresh = new_ref[0]
        new_scores = (
            lax.dot_general(queries, fresh, (((1,), (1,)), ((), ())), preferred_element_type=f32) * scale
        )
        count = fresh.shape[0]
        column = lax.broadcasted_iota(jnp.int32, (rows, count), 1)
        step = (lax.broadcasted_iota(jnp.int32, (rows, count), 0) // heads) % steps
        visible = (column <= step) & (column < steps)
        new_scores = jnp.where(visible, new_scores, masked_score)
        old = top[:, :1]
        peak = jnp.maximum(old, jnp.max(new_scores, axis=1, keepdims=True))
        carried = jnp.exp2(old - peak)
        new_weights = jnp.exp2(new_scores - peak)
        acc[...] = acc[...] * carried + jnp.dot(
            new_weights.astype(bf16), fresh[:, :width], preferred_element_type=f32
        )
        total[...] = total[...] * carried + jnp.sum(new_weights, axis=1, keepdims=True)
        top[...] = jnp.broadcast_to(peak, top.shape)

    out_ref[...] = acc[...].astype(bf16).reshape(out_ref.shape)
    lane = lax.broadcasted_iota(jnp.int32, top.shape, 1)
    stat_ref[...] = jnp.where(lane == 0, top[...], total[...]).reshape(stat_ref.shape)


def split_stats(peak, weight_sum, rows):
    lane = lax.broadcasted_iota(jnp.int32, (rows, 128), 1)
    first = peak.astype(bf16).astype(f32)
    rest = peak - first
    second = rest.astype(bf16).astype(f32)
    third = rest - second
    sum_first = weight_sum.astype(bf16).astype(f32)
    sum_second = weight_sum - sum_first
    out = jnp.where(lane == 0, first, 0.0)
    out = jnp.where(lane == 1, second, out)
    out = jnp.where(lane == 2, third, out)
    out = jnp.where(lane == 3, sum_first, out)
    return jnp.where(lane == 4, sum_second, out)


def pair_kernel(out_a, stat_a, out_b, stat_b, sent_ref):
    rows = sent_ref.shape[1]
    width = out_a.shape[3]
    sa = stat_a[...].reshape(rows, 128)
    sb = stat_b[...].reshape(rows, 128)
    top_a, sum_a = sa[:, :1], sa[:, 1:2]
    top_b, sum_b = sb[:, :1], sb[:, 1:2]
    peak = jnp.maximum(top_a, top_b)
    wa = jnp.exp2(top_a - peak)
    wb = jnp.exp2(top_b - peak)
    sent_ref[0, :, :width] = (
        out_a[...].reshape(rows, width).astype(f32) * wa + out_b[...].reshape(rows, width).astype(f32) * wb
    ).astype(bf16)
    sent_ref[0, :, width:] = split_stats(peak, sum_a * wa + sum_b * wb, rows).astype(bf16)


def project_kernel(heads, got_ref, up_ref, out_ref, mixed, projected):
    sources, rows, _ = got_ref.shape
    width = up_ref.shape[1]
    tops = []
    sums = []
    for i in range(sources):
        stat = got_ref[i, :, width:].astype(f32)
        tops.append(stat[:, 0:1] + stat[:, 1:2] + stat[:, 2:3])
        sums.append(stat[:, 3:4] + stat[:, 4:5])
    peak = functools.reduce(jnp.maximum, tops)
    weights = [jnp.exp2(t - peak) for t in tops]
    weight_sum = sum(w * s for w, s in zip(weights, sums))
    merged = sum(w * got_ref[i, :, :width].astype(f32) for i, w in enumerate(weights))
    mixed[...] = merged.reshape(mixed.shape)
    stats = split_stats(peak, weight_sum, rows).T[:16].astype(bf16)
    count = rows // heads
    for h in range(heads):
        part = mixed[:, h, :]
        high = part.astype(bf16)
        low = (part - high.astype(f32)).astype(bf16)
        both = jnp.dot(jnp.concatenate([high, low], axis=0), up_ref[h], preferred_element_type=f32)
        projected[:, h, :] = both[:count] + both[count:]
    values = projected[...].reshape(rows, projected.shape[2]).astype(bf16)
    for copy in range(out_ref.shape[0]):
        out_ref[copy, :rows, :] = values
        out_ref[copy, rows:, :] = stats


def finish_kernel(got_ref, out_ref):
    sources = got_ref.shape[0]
    rows = out_ref.shape[0]
    tops = []
    sums = []
    for i in range(sources):
        stat = got_ref[i, rows:, :].astype(f32)
        tops.append(stat[0:1] + stat[1:2] + stat[2:3])
        sums.append(stat[3:4] + stat[4:5])
    tops = jnp.concatenate(tops, axis=0)
    sums = jnp.concatenate(sums, axis=0)
    weights = jnp.exp2(tops - jnp.max(tops, axis=0, keepdims=True))
    weights = weights / jnp.sum(weights * sums, axis=0, keepdims=True)
    spread = jnp.concatenate([weights, jnp.zeros((128 - sources, weights.shape[1]), f32)], axis=0).T
    result = jnp.zeros(out_ref.shape, f32)
    for i in range(sources):
        result += got_ref[i, :rows, :].astype(f32) * spread[:rows, i : i + 1]
    out_ref[...] = result.astype(bf16)


def on_device(
    query_heads, up_keys, up_values, latent_cache, new_latent, context_lengths, positions
):
    steps, requests, heads, query_width = query_heads.shape
    nope = up_keys.shape[1]
    width = up_keys.shape[2]
    key_width = latent_cache.shape[2]
    rope = key_width - width
    value_width = up_values.shape[2]
    cached = latent_cache.shape[1]
    owners = lax.axis_size("head")
    plane = lax.axis_size("z") * lax.axis_size("x")
    pairs = steps * requests
    half = requests // 2
    scale = float(query_width) ** (-0.5) * log2_e

    core = lax.axis_index("core")
    slot = lax.axis_index(("z", "x", "core", "head"))

    pos_grid = positions[None, :] + jnp.arange(steps, dtype=jnp.int32)[:, None]
    cos, sin = rope_tables(pos_grid, rope)
    copies, new_keys = pl.pallas_call(
        functools.partial(queries_kernel, steps, requests),
        out_shape=(
            jax.ShapeDtypeStruct((owners, requests, steps * heads, key_width), bf16),
            jax.ShapeDtypeStruct((pairs, key_width), bf16),
        ),
        scratch_shapes=[
            pltpu.VMEM((pairs, heads, nope), f32),
            pltpu.VMEM((pairs, heads, width), f32),
        ],
        compiler_params=pltpu.CompilerParams(vmem_limit_bytes=32 * 2**20),
        name="queries",
    )(query_heads.reshape(pairs, heads, query_width), up_keys, new_latent.reshape(pairs, key_width), cos, sin)
    new_keys = jnp.swapaxes(new_keys.reshape(steps, requests, key_width), 0, 1)
    new_keys = jnp.pad(new_keys, ((0, 0), (0, 128 - steps), (0, 0)))
    queries = lax.all_to_all(copies, "head", 0, 0, tiled=True)

    slots = plane * 2 * owners
    share = slots // requests
    fresh_for = jnp.where(slot % share == 0, slot // share, -1).astype(jnp.int32)

    def attend(first):
        info = jnp.concatenate(
            [
                jnp.stack([first.astype(jnp.int32), slot.astype(jnp.int32) * cached, fresh_for]),
                context_lengths,
            ]
        )
        rows = owners * steps * heads
        return pl.pallas_call(
            functools.partial(attention_kernel, scale, steps, heads),
            grid_spec=pltpu.PrefetchScalarGridSpec(
                num_scalar_prefetch=1,
                grid=(half,),
                in_specs=[
                    pl.BlockSpec((owners, 1, steps * heads, key_width), lambda i, info: (0, info[0] + i, 0, 0)),
                    pl.BlockSpec((1, cached, key_width), lambda i, info: (info[0] + i, 0, 0)),
                    pl.BlockSpec((1, 128, key_width), lambda i, info: (info[0] + i, 0, 0)),
                ],
                out_specs=[
                    pl.BlockSpec((owners, 1, steps * heads, width), lambda i, info: (0, i, 0, 0)),
                    pl.BlockSpec((owners, 1, steps * heads, 128), lambda i, info: (0, i, 0, 0)),
                ],
                scratch_shapes=[
                    pltpu.VMEM((rows, cached), f32),
                    pltpu.VMEM((rows, width), f32),
                    pltpu.VMEM((rows, 128), f32),
                    pltpu.VMEM((rows, 128), f32),
                ],
            ),
            out_shape=(
                jax.ShapeDtypeStruct((owners, half, steps * heads, width), bf16),
                jax.ShapeDtypeStruct((owners, half, steps * heads, 128), f32),
            ),
            compiler_params=pltpu.CompilerParams(
                vmem_limit_bytes=40 * 2**20, dimension_semantics=("arbitrary",)
            ),
            cost_estimate=pl.CostEstimate(
                flops=2 * half * rows * cached * (key_width + width),
                bytes_accessed=half * cached * 640 * 2,
                transcendentals=half * rows * cached,
            ),
            name="attention",
        )(info, queries, latent_cache, new_keys)

    swap = [(0, 1), (1, 0)]
    out_other, stat_other = attend((1 - core) * half)
    out_a = lax.ppermute(out_other, "core", swap)
    stat_a = lax.ppermute(stat_other, "core", swap)
    out_b, stat_b = attend(core * half)

    chunk = half * steps * heads
    part_spec = pl.BlockSpec((1, half, steps * heads, width), lambda i: (i, 0, 0, 0))
    stat_spec = pl.BlockSpec((1, half, steps * heads, 128), lambda i: (i, 0, 0, 0))
    sent = pl.pallas_call(
        pair_kernel,
        grid=(owners,),
        in_specs=[part_spec, stat_spec, part_spec, stat_spec],
        out_specs=pl.BlockSpec((1, chunk, width + 128), lambda i: (i, 0, 0)),
        out_shape=jax.ShapeDtypeStruct((owners, chunk, width + 128), bf16),
        name="pair_merge",
    )(out_a, stat_a, out_b, stat_b)
    got = lax.all_to_all(sent, "head", 0, 0, tiled=True)

    projected = pl.pallas_call(
        functools.partial(project_kernel, heads),
        out_shape=jax.ShapeDtypeStruct((plane, chunk + 16, value_width), bf16),
        scratch_shapes=[
            pltpu.VMEM((chunk // heads, heads, width), f32),
            pltpu.VMEM((chunk // heads, heads, value_width), f32),
        ],
        compiler_params=pltpu.CompilerParams(vmem_limit_bytes=32 * 2**20),
        name="project",
    )(got, up_values)
    everyone = lax.all_to_all(projected, ("z", "x"), 0, 0, tiled=True)

    own = pl.pallas_call(
        finish_kernel,
        out_shape=jax.ShapeDtypeStruct((chunk, value_width), bf16),
        name="finish",
    )(everyone)
    theirs = lax.ppermute(own, "core", swap)
    both = jnp.where(core == 0, jnp.stack([own, theirs]), jnp.stack([theirs, own]))
    return jnp.swapaxes(both.reshape(requests, steps, heads, value_width), 0, 1)


def solution(mesh):
    fine = Mesh(mesh.devices.reshape(4, 4, 2, 4), ("z", "x", "core", "head"))
    in_specs = (
        P(None, None, "head", None),
        P("head", None, None),
        P("head", None, None),
        P(None, ("z", "x", "core", "head"), None),
        P(),
        P(),
        P(),
    )
    out_specs = P(None, None, "head", None)
    return jax.shard_map(
        on_device, mesh=fine, in_specs=in_specs, out_specs=out_specs, check_vma=False
    )
```

```python
import functools

import jax
import jax.numpy as jnp
from jax import lax
from jax.experimental import pallas as pl
from jax.experimental.pallas import tpu as pltpu
from jax.sharding import Mesh, PartitionSpec as P

rope_base = 50000.0
masked_score = -1e30
lowest_max = -1e29
log2_e = 1.4426950408889634
bf16 = jnp.bfloat16
f32 = jnp.float32


def swap_halves(values):
    half = values.shape[-1] // 2
    return jnp.concatenate([values[..., half:], values[..., :half]], axis=-1)


def rope_tables(positions_ref, steps, width):
    requests = positions_ref.shape[0]
    pairs = steps * requests
    half = width // 2
    row = lax.broadcasted_iota(jnp.int32, (pairs, width), 0)
    lane = lax.broadcasted_iota(jnp.int32, (pairs, width), 1)
    where_at = row // requests
    for b in range(requests):
        where_at += jnp.where(row % requests == b, positions_ref[b], 0)
    counter = lax.broadcasted_iota(jnp.int32, (1, width), 1) % half
    inverse = jnp.zeros((1, width), f32)
    for i in range(half):
        inverse = jnp.where(counter == i, f32(rope_base ** (-2.0 * i / width)), inverse)
    angles = where_at.astype(f32) * inverse
    return jnp.cos(angles), jnp.where(lane < half, -1.0, 1.0) * jnp.sin(angles)


def queries_kernel(steps, positions_ref, q_ref, up_ref, new_ref, out_ref, keys_ref, q_f32, lat):
    pairs, heads, _ = q_ref.shape
    requests = pairs // steps
    nope, width = up_ref.shape[1], up_ref.shape[2]
    q_f32[...] = q_ref[:, :, :nope].astype(f32)
    for h in range(heads):
        lat[:, h, :] = jnp.dot(q_f32[:, h, :].astype(bf16), up_ref[h], preferred_element_type=f32)
    cos, sin = rope_tables(positions_ref, steps, new_ref.shape[1] - width)
    rope = q_ref[:, :, nope:].astype(f32)
    rope = (rope * cos[:, None, :] + swap_halves(rope) * sin[:, None, :]).astype(bf16)
    for s in range(steps):
        for b in range(requests):
            row = jnp.concatenate([lat[s * requests + b].astype(bf16), rope[s * requests + b]], axis=-1)
            for copy in range(out_ref.shape[0]):
                out_ref[copy, b, s * heads : (s + 1) * heads, :] = row
    new = new_ref[...]
    tail = new[:, width:].astype(f32)
    tail = (tail * cos + swap_halves(tail) * sin).astype(bf16)
    keys_ref[...] = jnp.concatenate([new[:, :width], tail], axis=-1)


def attention_kernel(
    scale, steps, heads, info_ref, q_ref, k_ref, new_ref, out_ref, stat_ref, acc, *scores
):
    owners, requests = q_ref.shape[:2]
    rows = owners * q_ref.shape[2]
    key_width, cached = k_ref.shape[1:]
    width = out_ref.shape[3]
    chunk = 1024
    count = out_ref.shape[1]
    lane = lax.broadcasted_iota(jnp.int32, (rows, 128), 1)

    tops = []
    for i in range(count):
        request = info_ref[0] + i
        limit = info_ref[3 + request] - info_ref[1]
        queries = q_ref[:, request].reshape(rows, key_width)
        top = jnp.full((rows, 128), lowest_max, f32)
        for c in range(0, cached, chunk):
            part = jnp.dot(queries, k_ref[request, :, c : c + chunk], preferred_element_type=f32) * scale
            column = lax.broadcasted_iota(jnp.int32, (1, chunk), 1) + c
            part = jnp.where(column < limit, part, masked_score)
            scores[i][:, c : c + chunk] = part
            for at in range(0, chunk, 128):
                top = jnp.maximum(top, part[:, at : at + 128])
        tops.append(jnp.max(top, axis=1, keepdims=True))

    for i in range(count):
        request = info_ref[0] + i
        total = jnp.zeros((rows, 128), f32)
        for c in range(0, cached, chunk):
            weights = jnp.exp2(scores[i][:, c : c + chunk] - tops[i])
            for at in range(0, chunk, 128):
                total = total + weights[:, at : at + 128]
            part = lax.dot_general(
                weights.astype(bf16),
                k_ref[request, :width, c : c + chunk],
                (((1,), (1,)), ((), ())),
                preferred_element_type=f32,
            )
            mixed = part if c == 0 else mixed + part
        total = jnp.sum(total, axis=1, keepdims=True)
        out_ref[:, i] = mixed.astype(bf16).reshape(owners, -1, width)
        stat_ref[:, i] = jnp.where(lane == 0, tops[i], total).reshape(owners, -1, 128)

        @pl.when(info_ref[2] == request)
        def _():
            acc[...] = mixed

    for i in range(count):
        request = info_ref[0] + i

        @pl.when(info_ref[2] == request)
        def _():
            queries = q_ref[:, request].reshape(rows, key_width)
            fresh = new_ref[...]
            new_scores = (
                lax.dot_general(queries, fresh, (((1,), (1,)), ((), ())), preferred_element_type=f32) * scale
            )
            shape = (rows, fresh.shape[0])
            key = lax.broadcasted_iota(jnp.int32, shape, 1)
            step = (lax.broadcasted_iota(jnp.int32, shape, 0) // heads) % steps
            visible = (key % requests == request) & (key // requests <= step)
            new_scores = jnp.where(visible, new_scores, masked_score)
            old = stat_ref[:, i].reshape(rows, 128)
            top, total = old[:, :1], old[:, 1:2]
            peak = jnp.maximum(top, jnp.max(new_scores, axis=1, keepdims=True))
            carried = jnp.exp2(top - peak)
            new_weights = jnp.exp2(new_scores - peak)
            mixed = acc[...] * carried + jnp.dot(
                new_weights.astype(bf16), fresh[:, :width], preferred_element_type=f32
            )
            total = total * carried + jnp.sum(new_weights, axis=1, keepdims=True)
            out_ref[:, i] = mixed.astype(bf16).reshape(owners, -1, width)
            stat_ref[:, i] = jnp.where(lane == 0, peak, total).reshape(owners, -1, 128)


def split_stats(peak, weight_sum, rows):
    lane = lax.broadcasted_iota(jnp.int32, (rows, 128), 1)
    first = peak.astype(bf16).astype(f32)
    rest = peak - first
    second = rest.astype(bf16).astype(f32)
    third = rest - second
    sum_first = weight_sum.astype(bf16).astype(f32)
    sum_second = weight_sum - sum_first
    out = jnp.where(lane == 0, first, 0.0)
    out = jnp.where(lane == 1, second, out)
    out = jnp.where(lane == 2, third, out)
    out = jnp.where(lane == 3, sum_first, out)
    return jnp.where(lane == 4, sum_second, out)


def pair_kernel(out_a, stat_a, out_b, stat_b, sent_ref):
    owners, rows, _ = sent_ref.shape
    width = out_a.shape[3]
    for owner in range(owners):
        sa = stat_a[owner].reshape(rows, 128)
        sb = stat_b[owner].reshape(rows, 128)
        top_a, sum_a = sa[:, :1], sa[:, 1:2]
        top_b, sum_b = sb[:, :1], sb[:, 1:2]
        peak = jnp.maximum(top_a, top_b)
        wa = jnp.exp2(top_a - peak)
        wb = jnp.exp2(top_b - peak)
        part_a = out_a[owner].reshape(rows, width).astype(f32)
        part_b = out_b[owner].reshape(rows, width).astype(f32)
        sent_ref[owner, :, :width] = (part_a * wa + part_b * wb).astype(bf16)
        sent_ref[owner, :, width:] = split_stats(peak, sum_a * wa + sum_b * wb, rows).astype(bf16)


def project_kernel(heads, got_ref, up_ref, out_ref, mixed, projected):
    sources, rows, _ = got_ref.shape
    width = up_ref.shape[1]
    tops = []
    sums = []
    for i in range(sources):
        stat = got_ref[i, :, width:].astype(f32)
        tops.append(stat[:, 0:1] + stat[:, 1:2] + stat[:, 2:3])
        sums.append(stat[:, 3:4] + stat[:, 4:5])
    peak = functools.reduce(jnp.maximum, tops)
    weights = [jnp.exp2(t - peak) for t in tops]
    weight_sum = sum(w * s for w, s in zip(weights, sums))
    merged = sum(w * got_ref[i, :, :width].astype(f32) for i, w in enumerate(weights))
    mixed[...] = merged.reshape(mixed.shape)
    stats = split_stats(peak, weight_sum, rows).T[:16].astype(bf16)
    count = rows // heads
    for h in range(heads):
        part = mixed[:, h, :]
        high = part.astype(bf16)
        low = (part - high.astype(f32)).astype(bf16)
        both = jnp.dot(jnp.concatenate([high, low], axis=0), up_ref[h], preferred_element_type=f32)
        projected[:, h, :] = both[:count] + both[count:]
    values = projected[...].reshape(rows, projected.shape[2]).astype(bf16)
    for copy in range(out_ref.shape[0]):
        out_ref[copy, :rows, :] = values
        out_ref[copy, rows:, :] = stats


def finish_kernel(got_ref, out_ref):
    sources = got_ref.shape[0]
    rows = out_ref.shape[0] * out_ref.shape[1] * out_ref.shape[2]
    tops = []
    sums = []
    for i in range(sources):
        stat = got_ref[i, rows:, :].astype(f32)
        tops.append(stat[0:1] + stat[1:2] + stat[2:3])
        sums.append(stat[3:4] + stat[4:5])
    tops = jnp.concatenate(tops, axis=0)
    sums = jnp.concatenate(sums, axis=0)
    weights = jnp.exp2(tops - jnp.max(tops, axis=0, keepdims=True))
    weights = weights / jnp.sum(weights * sums, axis=0, keepdims=True)
    spread = jnp.concatenate([weights, jnp.zeros((128 - sources, weights.shape[1]), f32)], axis=0).T
    result = jnp.zeros((rows, got_ref.shape[2]), f32)
    for i in range(sources):
        result += got_ref[i, :rows, :].astype(f32) * spread[:rows, i : i + 1]
    half, steps = out_ref.shape[1], out_ref.shape[0]
    result = result.astype(bf16).reshape(half, steps, *out_ref.shape[2:])
    for b in range(half):
        out_ref[:, b] = result[b]


def place_kernel(info_ref, own_ref, other_ref, out_ref):
    half = own_ref.shape[1]
    first = info_ref[0]
    out_ref[:, pl.ds(first, half)] = own_ref[...]
    out_ref[:, pl.ds(half - first, half)] = other_ref[...]


def on_device(
    query_heads, up_keys, up_values, latent_cache, new_latent, context_lengths, positions
):
    steps, requests, heads, query_width = query_heads.shape
    nope = up_keys.shape[1]
    width = up_keys.shape[2]
    key_width = latent_cache.shape[2]
    rope = key_width - width
    value_width = up_values.shape[2]
    cached = latent_cache.shape[1]
    owners = lax.axis_size("head")
    plane = lax.axis_size("z") * lax.axis_size("x")
    pairs = steps * requests
    half = requests // 2
    scale = float(query_width) ** (-0.5) * log2_e

    core = lax.axis_index("core")
    slot = lax.axis_index(("z", "x", "core", "head"))

    vmem = pl.BlockSpec(memory_space=pltpu.VMEM)
    smem = pl.BlockSpec(memory_space=pltpu.SMEM)
    small = pltpu.CompilerParams(vmem_limit_bytes=12 * 2**20)
    copies, new_keys = pl.pallas_call(
        functools.partial(queries_kernel, steps),
        in_specs=[smem, vmem, vmem, vmem],
        out_specs=[vmem, vmem],
        out_shape=(
            jax.ShapeDtypeStruct((owners, requests, steps * heads, key_width), bf16),
            jax.ShapeDtypeStruct((pairs, key_width), bf16),
        ),
        scratch_shapes=[
            pltpu.VMEM((pairs, heads, nope), f32),
            pltpu.VMEM((pairs, heads, width), f32),
        ],
        compiler_params=small,
        name="queries",
    )(positions, query_heads.reshape(pairs, heads, query_width), up_keys, new_latent.reshape(pairs, key_width))
    queries = lax.all_to_all(copies, "head", 0, 0, tiled=True)
    cache = jnp.swapaxes(latent_cache, 1, 2)

    slots = plane * 2 * owners
    share = slots // requests
    fresh_for = jnp.where(slot % share == 0, slot // share, -1).astype(jnp.int32)

    def attend(first):
        info = jnp.concatenate(
            [
                jnp.stack([first.astype(jnp.int32), slot.astype(jnp.int32) * cached, fresh_for]),
                context_lengths,
            ]
        )
        rows = owners * steps * heads
        return pl.pallas_call(
            functools.partial(attention_kernel, scale, steps, heads),
            in_specs=[smem, vmem, vmem, vmem],
            out_specs=[vmem, vmem],
            scratch_shapes=[pltpu.VMEM((rows, width), f32)] + [pltpu.VMEM((rows, cached), f32)] * half,
            out_shape=(
                jax.ShapeDtypeStruct((owners, half, steps * heads, width), bf16),
                jax.ShapeDtypeStruct((owners, half, steps * heads, 128), f32),
            ),
            compiler_params=pltpu.CompilerParams(vmem_limit_bytes=20 * 2**20),
            cost_estimate=pl.CostEstimate(
                flops=2 * half * rows * cached * (key_width + width),
                bytes_accessed=half * cached * key_width * 2,
                transcendentals=half * rows * cached,
            ),
            name="attention",
        )(info, queries, cache, new_keys)

    swap = [(0, 1), (1, 0)]
    out_other, stat_other = attend((1 - core) * half)
    out_a = lax.ppermute(out_other, "core", swap)
    stat_a = lax.ppermute(stat_other, "core", swap)
    out_b, stat_b = attend(core * half)

    chunk = half * steps * heads
    sent = pl.pallas_call(
        pair_kernel,
        in_specs=[vmem] * 4,
        out_specs=vmem,
        out_shape=jax.ShapeDtypeStruct((owners, chunk, width + 128), bf16),
        compiler_params=small,
        name="pair_merge",
    )(out_a, stat_a, out_b, stat_b)
    got = lax.all_to_all(sent, "head", 0, 0, tiled=True)

    projected = pl.pallas_call(
        functools.partial(project_kernel, heads),
        in_specs=[vmem] * 2,
        out_specs=vmem,
        out_shape=jax.ShapeDtypeStruct((plane, chunk + 16, value_width), bf16),
        scratch_shapes=[
            pltpu.VMEM((chunk // heads, heads, width), f32),
            pltpu.VMEM((chunk // heads, heads, value_width), f32),
        ],
        compiler_params=small,
        name="project",
    )(got, up_values)
    everyone = lax.all_to_all(projected, ("z", "x"), 0, 0, tiled=True)

    own = pl.pallas_call(
        finish_kernel,
        in_specs=[vmem],
        out_specs=vmem,
        out_shape=jax.ShapeDtypeStruct((steps, half, heads, value_width), bf16),
        compiler_params=small,
        name="finish",
    )(everyone)
    theirs = lax.ppermute(own, "core", swap)
    return pl.pallas_call(
        place_kernel,
        in_specs=[smem, vmem, vmem],
        out_specs=vmem,
        out_shape=jax.ShapeDtypeStruct((steps, requests, heads, value_width), bf16),
        compiler_params=small,
        name="place",
    )((core * half).astype(jnp.int32).reshape(1), own, theirs)


def solution(mesh):
    fine = Mesh(mesh.devices.reshape(4, 4, 2, 4), ("z", "x", "core", "head"))
    in_specs = (
        P(None, None, "head", None),
        P("head", None, None),
        P("head", None, None),
        P(None, ("z", "x", "core", "head"), None),
        P(),
        P(),
        P(),
    )
    out_specs = P(None, None, "head", None)
    return jax.shard_map(
        on_device, mesh=fine, in_specs=in_specs, out_specs=out_specs, check_vma=False
    )
```

```python
import functools

import jax
import jax.numpy as jnp
from jax import lax
from jax.experimental import pallas as pl
from jax.experimental.pallas import tpu as pltpu
from jax.sharding import Mesh, PartitionSpec as P

rope_base = 50000.0
masked_score = -1e30
lowest_max = -1e29
log2_e = 1.4426950408889634
bf16 = jnp.bfloat16
f32 = jnp.float32


def swap_halves(values):
    half = values.shape[-1] // 2
    return jnp.concatenate([values[..., half:], values[..., :half]], axis=-1)


def rope_tables(positions_ref, steps, width):
    requests = positions_ref.shape[0]
    pairs = steps * requests
    half = width // 2
    row = lax.broadcasted_iota(jnp.int32, (pairs, width), 0)
    lane = lax.broadcasted_iota(jnp.int32, (pairs, width), 1)
    where_at = row // requests
    for b in range(requests):
        where_at += jnp.where(row % requests == b, positions_ref[b], 0)
    counter = lax.broadcasted_iota(jnp.int32, (1, width), 1) % half
    inverse = jnp.zeros((1, width), f32)
    for i in range(half):
        inverse = jnp.where(counter == i, f32(rope_base ** (-2.0 * i / width)), inverse)
    angles = where_at.astype(f32) * inverse
    return jnp.cos(angles), jnp.where(lane < half, -1.0, 1.0) * jnp.sin(angles)


def queries_kernel(
    steps, info_ref, positions_hbm, q_hbm, up_hbm, new_hbm, own_ref, sent_ref, keys_ref, positions, q, up, new, lat, sems
):
    pairs, heads, _ = q.shape
    requests = pairs // steps
    nope, width = up.shape[1], up.shape[2]
    key_width = new.shape[2]
    fetches = [
        pltpu.make_async_copy(positions_hbm, positions, sems.at[0]),
        pltpu.make_async_copy(q_hbm, q, sems.at[1]),
        pltpu.make_async_copy(new_hbm, new, sems.at[2]),
    ]
    groups = 4
    share = heads // groups
    for g in range(groups):
        at = pl.ds(g * share, share)
        fetches.append(pltpu.make_async_copy(up_hbm.at[at], up.at[at], sems.at[3 + g]))
    for fetch in fetches:
        fetch.start()
    own_ref[:, :, key_width:] = jnp.zeros(own_ref.shape[:2] + (own_ref.shape[2] - key_width,), bf16)
    fetches[0].wait()
    cos, sin = rope_tables(positions, steps, key_width - width)
    fetches[1].wait()
    rope = q[:, :, nope:].astype(f32)
    rope = (rope * cos[:, None, :] + swap_halves(rope) * sin[:, None, :]).astype(bf16)
    for s in range(steps):
        for b in range(requests):
            own_ref[b, s * heads : (s + 1) * heads, width:key_width] = rope[s * requests + b]
    fetches[2].wait()
    for t in range(steps):
        at = slice(t * requests, (t + 1) * requests)
        tail = new[t, :, width:].astype(f32)
        tail = tail * cos[at] + swap_halves(tail) * sin[at]
        keys_ref[t] = jnp.concatenate([new[t, :, :width], tail.astype(bf16)], axis=-1)
    q_f32 = q[:, :, :nope].astype(f32)
    for h in range(heads):
        if h % share == 0:
            fetches[3 + h // share].wait()
        lat[:, h, :] = jnp.dot(q_f32[:, h, :].astype(bf16), up[h], preferred_element_type=f32)
    for s in range(steps):
        for b in range(requests):
            own_ref[b, s * heads : (s + 1) * heads, :width] = lat[s * requests + b].astype(bf16)
    sent_ref[...] = own_ref[pl.ds(info_ref[0], sent_ref.shape[0])]


def stage_kernel(cache_hbm, out_ref, sems):
    copies = []
    for i in range(out_ref.shape[0]):
        copies.append(pltpu.make_async_copy(cache_hbm.at[i], out_ref.at[i], sems.at[i]))
    for copy in copies:
        copy.start()
    for copy in copies:
        copy.wait()


def attention_kernel(
    scale, steps, heads, info_ref, own_ref, q1_ref, q2_ref, q3_ref, k_ref, new_ref, out_ref, stat_ref, q_ref, acc, *scores
):
    owners = q_ref.shape[1]
    requests = own_ref.shape[0]
    rows = owners * q_ref.shape[2]
    key_width, cached = k_ref.shape[1:]
    q_ref[:, 0] = own_ref[pl.ds(info_ref[0], q_ref.shape[0])]
    q_ref[:, 1] = q1_ref[...]
    q_ref[:, 2] = q2_ref[...]
    q_ref[:, 3] = q3_ref[...]
    width = out_ref.shape[3]
    chunk = 1024
    count = out_ref.shape[1]
    lane = lax.broadcasted_iota(jnp.int32, (rows, 128), 1)

    tops = []
    for i in range(count):
        request = info_ref[0] + i
        limit = info_ref[3 + request] - info_ref[1]
        queries = q_ref[i].reshape(rows, -1)[:, :key_width]
        top = jnp.full((rows, 128), lowest_max, f32)
        for c in range(0, cached, chunk):
            part = jnp.dot(queries, k_ref[request, :, c : c + chunk], preferred_element_type=f32) * scale
            column = lax.broadcasted_iota(jnp.int32, (1, chunk), 1) + c
            part = jnp.where(column < limit, part, masked_score)
            scores[i][:, c : c + chunk] = part
            for at in range(0, chunk, 128):
                top = jnp.maximum(top, part[:, at : at + 128])
        tops.append(jnp.max(top, axis=1, keepdims=True))

    for i in range(count):
        request = info_ref[0] + i
        total = jnp.zeros((rows, 128), f32)
        for c in range(0, cached, chunk):
            weights = jnp.exp2(scores[i][:, c : c + chunk] - tops[i])
            for at in range(0, chunk, 128):
                total = total + weights[:, at : at + 128]
            part = lax.dot_general(
                weights.astype(bf16),
                k_ref[request, :width, c : c + chunk],
                (((1,), (1,)), ((), ())),
                preferred_element_type=f32,
            )
            mixed = part if c == 0 else mixed + part
        total = jnp.sum(total, axis=1, keepdims=True)
        out_ref[:, i] = mixed.astype(bf16).reshape(owners, -1, width)
        stat_ref[:, i] = jnp.where(lane == 0, tops[i], total).reshape(owners, -1, 128)

        @pl.when(info_ref[2] == request)
        def _():
            acc[...] = mixed

    for i in range(count):
        request = info_ref[0] + i

        @pl.when(info_ref[2] == request)
        def _():
            queries = q_ref[i].reshape(rows, -1)[:, :key_width]
            fresh = new_ref[...]
            new_scores = (
                lax.dot_general(queries, fresh, (((1,), (1,)), ((), ())), preferred_element_type=f32) * scale
            )
            shape = (rows, fresh.shape[0])
            key = lax.broadcasted_iota(jnp.int32, shape, 1)
            step = (lax.broadcasted_iota(jnp.int32, shape, 0) // heads) % steps
            visible = (key % requests == request) & (key // requests <= step)
            new_scores = jnp.where(visible, new_scores, masked_score)
            old = stat_ref[:, i].reshape(rows, 128)
            top, total = old[:, :1], old[:, 1:2]
            peak = jnp.maximum(top, jnp.max(new_scores, axis=1, keepdims=True))
            carried = jnp.exp2(top - peak)
            new_weights = jnp.exp2(new_scores - peak)
            mixed = acc[...] * carried + jnp.dot(
                new_weights.astype(bf16), fresh[:, :width], preferred_element_type=f32
            )
            total = total * carried + jnp.sum(new_weights, axis=1, keepdims=True)
            out_ref[:, i] = mixed.astype(bf16).reshape(owners, -1, width)
            stat_ref[:, i] = jnp.where(lane == 0, peak, total).reshape(owners, -1, 128)


def split_stats(peak, weight_sum, rows):
    lane = lax.broadcasted_iota(jnp.int32, (rows, 128), 1)
    first = peak.astype(bf16).astype(f32)
    rest = peak - first
    second = rest.astype(bf16).astype(f32)
    third = rest - second
    sum_first = weight_sum.astype(bf16).astype(f32)
    sum_second = weight_sum - sum_first
    out = jnp.where(lane == 0, first, 0.0)
    out = jnp.where(lane == 1, second, out)
    out = jnp.where(lane == 2, third, out)
    out = jnp.where(lane == 3, sum_first, out)
    return jnp.where(lane == 4, sum_second, out)


def pair_kernel(out_a, stat_a, out_b, stat_b, *sent_refs):
    rows = sent_refs[0].shape[0]
    width = out_a.shape[3]
    for owner, sent_ref in enumerate(sent_refs):
        sa = stat_a[owner].reshape(rows, 128)
        sb = stat_b[owner].reshape(rows, 128)
        top_a, sum_a = sa[:, :1], sa[:, 1:2]
        top_b, sum_b = sb[:, :1], sb[:, 1:2]
        peak = jnp.maximum(top_a, top_b)
        wa = jnp.exp2(top_a - peak)
        wb = jnp.exp2(top_b - peak)
        part_a = out_a[owner].reshape(rows, width).astype(f32)
        part_b = out_b[owner].reshape(rows, width).astype(f32)
        sent_ref[:, :width] = (part_a * wa + part_b * wb).astype(bf16)
        sent_ref[:, width:] = split_stats(peak, sum_a * wa + sum_b * wb, rows).astype(bf16)


def project_kernel(heads, own_ref, got1_ref, got2_ref, got3_ref, up_ref, out_ref, mixed, projected):
    parts = (own_ref, got1_ref, got2_ref, got3_ref)
    rows = own_ref.shape[0]
    width = up_ref.shape[1]
    tops = []
    sums = []
    for part in parts:
        stat = part[:, width:].astype(f32)
        tops.append(stat[:, 0:1] + stat[:, 1:2] + stat[:, 2:3])
        sums.append(stat[:, 3:4] + stat[:, 4:5])
    peak = functools.reduce(jnp.maximum, tops)
    weights = [jnp.exp2(t - peak) for t in tops]
    weight_sum = sum(w * s for w, s in zip(weights, sums))
    merged = sum(w * part[:, :width].astype(f32) for w, part in zip(weights, parts))
    mixed[...] = merged.reshape(mixed.shape)
    stats = split_stats(peak, weight_sum, rows).T[:16].astype(bf16)
    count = rows // heads
    for h in range(heads):
        part = mixed[:, h, :]
        high = part.astype(bf16)
        low = (part - high.astype(f32)).astype(bf16)
        both = jnp.dot(jnp.concatenate([high, low], axis=0), up_ref[h], preferred_element_type=f32)
        projected[:, h, :] = both[:count] + both[count:]
    values = projected[...].reshape(rows, projected.shape[2]).astype(bf16)
    for copy in range(out_ref.shape[0]):
        out_ref[copy, :rows, :] = values
        out_ref[copy, rows:, :] = stats


def finish_kernel(got_ref, out_ref):
    sources = got_ref.shape[0]
    rows = out_ref.shape[0] * out_ref.shape[1] * out_ref.shape[2]
    tops = []
    sums = []
    for i in range(sources):
        stat = got_ref[i, rows:, :].astype(f32)
        tops.append(stat[0:1] + stat[1:2] + stat[2:3])
        sums.append(stat[3:4] + stat[4:5])
    tops = jnp.concatenate(tops, axis=0)
    sums = jnp.concatenate(sums, axis=0)
    weights = jnp.exp2(tops - jnp.max(tops, axis=0, keepdims=True))
    weights = weights / jnp.sum(weights * sums, axis=0, keepdims=True)
    spread = jnp.concatenate([weights, jnp.zeros((128 - sources, weights.shape[1]), f32)], axis=0).T
    result = jnp.zeros((rows, got_ref.shape[2]), f32)
    for i in range(sources):
        result += got_ref[i, :rows, :].astype(f32) * spread[:rows, i : i + 1]
    half, steps = out_ref.shape[1], out_ref.shape[0]
    result = result.astype(bf16).reshape(half, steps, *out_ref.shape[2:])
    for b in range(half):
        out_ref[:, b] = result[b]


def place_kernel(info_ref, own_ref, other_ref, out_ref):
    half = own_ref.shape[1]
    first = info_ref[0]
    out_ref[:, pl.ds(first, half)] = own_ref[...]
    out_ref[:, pl.ds(half - first, half)] = other_ref[...]


def on_device(
    query_heads, up_keys, up_values, latent_cache, new_latent, context_lengths, positions
):
    steps, requests, heads, query_width = query_heads.shape
    nope = up_keys.shape[1]
    width = up_keys.shape[2]
    key_width = latent_cache.shape[2]
    rope = key_width - width
    value_width = up_values.shape[2]
    cached = latent_cache.shape[1]
    owners = lax.axis_size("head")
    plane = lax.axis_size("z") * lax.axis_size("x")
    pairs = steps * requests
    half = requests // 2
    scale = float(query_width) ** (-0.5) * log2_e

    core = lax.axis_index("core")
    slot = lax.axis_index(("z", "x", "core", "head"))

    vmem = pl.BlockSpec(memory_space=pltpu.VMEM)
    smem = pl.BlockSpec(memory_space=pltpu.SMEM)
    small = pltpu.CompilerParams(vmem_limit_bytes=12 * 2**20)
    anywhere = pl.BlockSpec(memory_space=pl.ANY)
    wide = 640
    other_first = ((1 - core) * half).astype(jnp.int32)
    own_queries, sent_queries, new_keys = pl.pallas_call(
        functools.partial(queries_kernel, steps),
        in_specs=[smem] + [anywhere] * 4,
        out_specs=[vmem, vmem, vmem],
        out_shape=(
            jax.ShapeDtypeStruct((requests, steps * heads, wide), bf16),
            jax.ShapeDtypeStruct((half, steps * heads, wide), bf16),
            jax.ShapeDtypeStruct((steps, requests, key_width), bf16),
        ),
        scratch_shapes=[
            pltpu.SMEM((requests,), jnp.int32),
            pltpu.VMEM((pairs, heads, query_width), bf16),
            pltpu.VMEM(up_keys.shape, bf16),
            pltpu.VMEM(new_latent.shape, bf16),
            pltpu.VMEM((pairs, heads, width), f32),
            pltpu.SemaphoreType.DMA((7,)),
        ],
        compiler_params=pltpu.CompilerParams(vmem_limit_bytes=56 * 2**20),
        name="queries",
    )(other_first.reshape(1), positions, query_heads.reshape(pairs, heads, query_width), up_keys, new_latent)
    new_keys = new_keys.reshape(pairs, key_width)

    def over_head(array, k):
        return lax.ppermute(array, "head", [(i, i ^ k) for i in range(owners)])

    swap = [(0, 1), (1, 0)]
    partners = (1, 3, 2)
    got = [over_head(sent_queries, k) for k in partners]
    cache = pl.pallas_call(
        stage_kernel,
        in_specs=[anywhere],
        out_specs=vmem,
        out_shape=jax.ShapeDtypeStruct((requests, key_width, cached), bf16),
        scratch_shapes=[pltpu.SemaphoreType.DMA((requests,))],
        compiler_params=pltpu.CompilerParams(vmem_limit_bytes=16 * 2**20),
        cost_estimate=pl.CostEstimate(flops=0, bytes_accessed=2 * requests * key_width * cached, transcendentals=0),
        name="stage",
    )(jnp.swapaxes(latent_cache, 1, 2))
    passed = [lax.ppermute(g, "core", swap) for g in got]

    slots = plane * 2 * owners
    share = slots // requests
    fresh_for = jnp.where(slot % share == 0, slot // share, -1).astype(jnp.int32)

    def attend(first, got):
        info = jnp.concatenate(
            [
                jnp.stack([first.astype(jnp.int32), slot.astype(jnp.int32) * cached, fresh_for]),
                context_lengths,
            ]
        )
        rows = owners * steps * heads
        return pl.pallas_call(
            functools.partial(attention_kernel, scale, steps, heads),
            in_specs=[smem] + [vmem] * 6,
            out_specs=[vmem, vmem],
            scratch_shapes=[pltpu.VMEM((half, owners, steps * heads, wide), bf16), pltpu.VMEM((rows, width), f32)]
            + [pltpu.VMEM((rows, cached), f32)] * half,
            out_shape=(
                jax.ShapeDtypeStruct((owners, half, steps * heads, width), bf16),
                jax.ShapeDtypeStruct((owners, half, steps * heads, 128), f32),
            ),
            compiler_params=pltpu.CompilerParams(vmem_limit_bytes=20 * 2**20),
            cost_estimate=pl.CostEstimate(
                flops=2 * half * rows * cached * (key_width + width),
                bytes_accessed=half * cached * key_width * 2,
                transcendentals=half * rows * cached,
            ),
            name="attention",
        )(info, own_queries, *got, cache, new_keys)

    out_other, stat_other = attend(other_first, got)
    out_a = lax.ppermute(out_other, "core", swap)
    stat_a = lax.ppermute(stat_other, "core", swap)
    out_b, stat_b = attend(core * half, passed)

    chunk = half * steps * heads
    sent = pl.pallas_call(
        pair_kernel,
        in_specs=[vmem] * 4,
        out_specs=[vmem] * owners,
        out_shape=[jax.ShapeDtypeStruct((chunk, width + 128), bf16)] * owners,
        compiler_params=small,
        name="pair_merge",
    )(out_a, stat_a, out_b, stat_b)
    arrived = [over_head(array, k) for array, k in zip(sent[1:], partners)]

    projected = pl.pallas_call(
        functools.partial(project_kernel, heads),
        in_specs=[vmem] * 5,
        out_specs=vmem,
        out_shape=jax.ShapeDtypeStruct((plane, chunk + 16, value_width), bf16),
        scratch_shapes=[
            pltpu.VMEM((chunk // heads, heads, width), f32),
            pltpu.VMEM((chunk // heads, heads, value_width), f32),
        ],
        compiler_params=small,
        name="project",
    )(sent[0], *arrived, up_values)
    everyone = lax.all_to_all(projected, ("z", "x"), 0, 0, tiled=True)

    own = pl.pallas_call(
        finish_kernel,
        in_specs=[vmem],
        out_specs=vmem,
        out_shape=jax.ShapeDtypeStruct((steps, half, heads, value_width), bf16),
        compiler_params=small,
        name="finish",
    )(everyone)
    theirs = lax.ppermute(own, "core", swap)
    return pl.pallas_call(
        place_kernel,
        in_specs=[smem, vmem, vmem],
        out_specs=vmem,
        out_shape=jax.ShapeDtypeStruct((steps, requests, heads, value_width), bf16),
        compiler_params=small,
        name="place",
    )((core * half).astype(jnp.int32).reshape(1), own, theirs)


def solution(mesh):
    fine = Mesh(mesh.devices.reshape(4, 4, 2, 4), ("z", "x", "core", "head"))
    in_specs = (
        P(None, None, "head", None),
        P("head", None, None),
        P("head", None, None),
        P(None, ("z", "x", "core", "head"), None),
        P(),
        P(),
        P(),
    )
    out_specs = P(None, None, "head", None)
    return jax.shard_map(
        on_device, mesh=fine, in_specs=in_specs, out_specs=out_specs, check_vma=False
    )
```

```python
import functools

import jax
import jax.numpy as jnp
from jax import lax
from jax.experimental import pallas as pl
from jax.experimental.pallas import tpu as pltpu
from jax.sharding import Mesh, PartitionSpec as P

rope_base = 50000.0
masked_score = -1e30
lowest_max = -1e29
log2_e = 1.4426950408889634
bf16 = jnp.bfloat16
f32 = jnp.float32


def swap_halves(values):
    half = values.shape[-1] // 2
    return jnp.concatenate([values[..., half:], values[..., :half]], axis=-1)


def rope_tables(positions_ref, steps, width):
    requests = positions_ref.shape[0]
    pairs = steps * requests
    half = width // 2
    row = lax.broadcasted_iota(jnp.int32, (pairs, width), 0)
    lane = lax.broadcasted_iota(jnp.int32, (pairs, width), 1)
    where_at = row // requests
    for b in range(requests):
        where_at += jnp.where(row % requests == b, positions_ref[b], 0)
    counter = lax.broadcasted_iota(jnp.int32, (1, width), 1) % half
    inverse = jnp.zeros((1, width), f32)
    for i in range(half):
        inverse = jnp.where(counter == i, f32(rope_base ** (-2.0 * i / width)), inverse)
    angles = where_at.astype(f32) * inverse
    return jnp.cos(angles), jnp.where(lane < half, -1.0, 1.0) * jnp.sin(angles)


def queries_kernel(
    steps, info_ref, positions_hbm, q_hbm, up_hbm, new_hbm, own_ref, sent_ref, keys_ref, positions, q, up, new, lat, sems
):
    pairs, heads, _ = q.shape
    requests = pairs // steps
    nope, width = up.shape[1], up.shape[2]
    key_width = new.shape[2]
    fetches = [
        pltpu.make_async_copy(positions_hbm, positions, sems.at[0]),
        pltpu.make_async_copy(q_hbm, q, sems.at[1]),
        pltpu.make_async_copy(new_hbm, new, sems.at[2]),
    ]
    groups = 4
    share = heads // groups
    for g in range(groups):
        at = pl.ds(g * share, share)
        fetches.append(pltpu.make_async_copy(up_hbm.at[at], up.at[at], sems.at[3 + g]))
    for fetch in fetches:
        fetch.start()
    own_ref[:, :, key_width:] = jnp.zeros(own_ref.shape[:2] + (own_ref.shape[2] - key_width,), bf16)
    fetches[0].wait()
    cos, sin = rope_tables(positions, steps, key_width - width)
    fetches[1].wait()
    rope = q[:, :, nope:].astype(f32)
    rope = (rope * cos[:, None, :] + swap_halves(rope) * sin[:, None, :]).astype(bf16)
    for s in range(steps):
        for b in range(requests):
            own_ref[b, s * heads : (s + 1) * heads, width:key_width] = rope[s * requests + b]
    fetches[2].wait()
    rows = jnp.concatenate([new[t].astype(f32) for t in range(steps)], axis=0)
    tail = rows[:, width:]
    tail = tail * cos + swap_halves(tail) * sin
    keys_ref[...] = jnp.concatenate([rows[:, :width], tail], axis=-1).astype(bf16)
    q_f32 = q[:, :, :nope].astype(f32)
    for h in range(heads):
        if h % share == 0:
            fetches[3 + h // share].wait()
        lat[:, h, :] = jnp.dot(q_f32[:, h, :].astype(bf16), up[h], preferred_element_type=f32)
    for s in range(steps):
        for b in range(requests):
            own_ref[b, s * heads : (s + 1) * heads, :width] = lat[s * requests + b].astype(bf16)
    sent_ref[...] = own_ref[pl.ds(info_ref[0], sent_ref.shape[0])]


def split_stats(peak, weight_sum, rows):
    lane = lax.broadcasted_iota(jnp.int32, (rows, 128), 1)
    first = peak.astype(bf16).astype(f32)
    rest = peak - first
    second = rest.astype(bf16).astype(f32)
    third = rest - second
    sum_first = weight_sum.astype(bf16).astype(f32)
    sum_second = weight_sum - sum_first
    out = jnp.where(lane == 0, first, 0.0)
    out = jnp.where(lane == 1, second, out)
    out = jnp.where(lane == 2, third, out)
    out = jnp.where(lane == 3, sum_first, out)
    return jnp.where(lane == 4, sum_second, out)


def attention_kernel(
    scale, info_ref, own_ref, q1_ref, q2_ref, q3_ref, cache_hbm, out_ref, q_ref, k_ref, sems, *scores
):
    count, owners, share, _ = q_ref.shape
    rows = owners * share
    key_width, cached = k_ref.shape[1:]
    width = out_ref.shape[2] - 128
    pieces = sems.shape[1]
    piece = cached // pieces
    chunk = 1024
    first = info_ref[0]
    fetches = []
    for i in range(count):
        for p in range(pieces):
            at = pl.ds(p * piece, piece)
            fetches.append(
                pltpu.make_async_copy(cache_hbm.at[first + i, :, at], k_ref.at[i, :, at], sems.at[i, p])
            )
    for fetch in fetches:
        fetch.start()

    q_ref[:, 0] = own_ref[pl.ds(first, count)]
    q_ref[:, 1] = q1_ref[...]
    q_ref[:, 2] = q2_ref[...]
    q_ref[:, 3] = q3_ref[...]

    tops = []
    for i in range(count):
        limit = info_ref[2 + first + i] - info_ref[1]
        queries = q_ref[i].reshape(rows, -1)[:, :key_width]
        top = jnp.full((rows, 128), lowest_max, f32)
        step = piece if i == 0 else cached
        for c in range(0, cached, step):
            for p in range(c // piece, (c + step) // piece):
                fetches[i * pieces + p].wait()
            part = jnp.dot(queries, k_ref[i, :, c : c + step], preferred_element_type=f32) * scale
            column = lax.broadcasted_iota(jnp.int32, (1, step), 1) + c
            part = jnp.where(column < limit, part, masked_score)
            scores[i][:, c : c + step] = part
            for at in range(0, step, 128):
                top = jnp.maximum(top, part[:, at : at + 128])
        tops.append(jnp.max(top, axis=1, keepdims=True))

    for i in range(count):
        total = jnp.zeros((rows, 128), f32)
        for c in range(0, cached, chunk):
            weights = jnp.exp2(scores[i][:, c : c + chunk] - tops[i])
            for at in range(0, chunk, 128):
                total = total + weights[:, at : at + 128]
            part = lax.dot_general(
                weights.astype(bf16),
                k_ref[i, :width, c : c + chunk],
                (((1,), (1,)), ((), ())),
                preferred_element_type=f32,
            )
            mixed = part if c == 0 else mixed + part
        total = jnp.sum(total, axis=1, keepdims=True)
        at = slice(i * share, (i + 1) * share)
        out_ref[:, at, :width] = mixed.astype(bf16).reshape(owners, share, width)
        out_ref[:, at, width:] = split_stats(tops[i], total, rows).astype(bf16).reshape(owners, share, 128)


def fresh_kernel(scale, steps, heads, info_ref, own_ref, new_ref, out_ref):
    requests, share, _ = own_ref.shape
    key_width = new_ref.shape[1]
    width = out_ref.shape[1] - 128
    fresh = new_ref[...]
    shape = (share, fresh.shape[0])
    key = lax.broadcasted_iota(jnp.int32, shape, 1)
    step = (lax.broadcasted_iota(jnp.int32, shape, 0) // heads) % steps
    counted = info_ref[1] == 1
    for i in range(out_ref.shape[0] // share):
        request = info_ref[0] + i
        scores = (
            lax.dot_general(
                own_ref[request][:, :key_width], fresh, (((1,), (1,)), ((), ())), preferred_element_type=f32
            )
            * scale
        )
        visible = (key % requests == request) & (key // requests <= step) & counted
        scores = jnp.where(visible, scores, masked_score)
        top = jnp.maximum(jnp.max(scores, axis=1, keepdims=True), lowest_max)
        weights = jnp.exp2(scores - top)
        total = jnp.sum(weights, axis=1, keepdims=True)
        mixed = jnp.dot(weights.astype(bf16), fresh[:, :width], preferred_element_type=f32)
        at = slice(i * share, (i + 1) * share)
        out_ref[at, :width] = mixed.astype(bf16)
        out_ref[at, width:] = split_stats(top, total, share).astype(bf16)


def merge_parts(parts, width):
    tops = []
    sums = []
    for part in parts:
        stat = part[:, width:].astype(f32)
        tops.append(stat[:, 0:1] + stat[:, 1:2] + stat[:, 2:3])
        sums.append(stat[:, 3:4] + stat[:, 4:5])
    peak = functools.reduce(jnp.maximum, tops)
    weights = [jnp.exp2(t - peak) for t in tops]
    weight_sum = sum(w * s for w, s in zip(weights, sums))
    merged = sum(w * part[:, :width].astype(f32) for w, part in zip(weights, parts))
    return merged, peak, weight_sum


def pair_kernel(a_ref, b_ref, *sent_refs):
    rows = sent_refs[0].shape[0]
    width = a_ref.shape[2] - 128
    for owner, sent_ref in enumerate(sent_refs):
        merged, peak, weight_sum = merge_parts((a_ref[owner], b_ref[owner]), width)
        sent_ref[:, :width] = merged.astype(bf16)
        sent_ref[:, width:] = split_stats(peak, weight_sum, rows).astype(bf16)


def project_kernel(heads, *refs):
    *parts, up_ref, out_ref, mixed, projected = refs
    rows = parts[0].shape[0]
    merged, peak, weight_sum = merge_parts([part[...] for part in parts], up_ref.shape[1])
    mixed[...] = merged.reshape(mixed.shape)
    stats = split_stats(peak, weight_sum, rows).T[:16].astype(bf16)
    count = rows // heads
    for h in range(heads):
        part = mixed[:, h, :]
        high = part.astype(bf16)
        low = (part - high.astype(f32)).astype(bf16)
        both = jnp.dot(jnp.concatenate([high, low], axis=0), up_ref[h], preferred_element_type=f32)
        projected[:, h, :] = both[:count] + both[count:]
    values = projected[...].reshape(rows, projected.shape[2]).astype(bf16)
    out_ref[:rows, :] = values
    out_ref[rows:, :] = stats


def merge_rows(parts, rows):
    tops = []
    sums = []
    for part in parts:
        stat = part[rows:, :].astype(f32)
        tops.append(stat[0:1] + stat[1:2] + stat[2:3])
        sums.append(stat[3:4] + stat[4:5])
    tops = jnp.concatenate(tops, axis=0)
    peak = jnp.max(tops, axis=0, keepdims=True)
    weights = jnp.exp2(tops - peak)
    weight_sum = jnp.sum(weights * jnp.concatenate(sums, axis=0), axis=0, keepdims=True)
    return weights, peak, weight_sum


def weigh(parts, weights, rows):
    spread = jnp.concatenate([weights, jnp.zeros((128 - len(parts), weights.shape[1]), f32)], axis=0).T
    return sum(part[:rows, :].astype(f32) * spread[:rows, i : i + 1] for i, part in enumerate(parts))


def middle_kernel(*refs):
    *parts, out_ref = refs
    parts = [part[...] for part in parts]
    rows = out_ref.shape[0] - 16
    weights, peak, weight_sum = merge_rows(parts, rows)
    out_ref[:rows, :] = weigh(parts, weights, rows).astype(bf16)
    line = lax.broadcasted_iota(jnp.int32, (16, weights.shape[1]), 0)
    first = peak.astype(bf16).astype(f32)
    second = (peak - first).astype(bf16).astype(f32)
    sum_first = weight_sum.astype(bf16).astype(f32)
    stats = jnp.where(line == 0, first, 0.0)
    stats = jnp.where(line == 1, second, stats)
    stats = jnp.where(line == 2, peak - first - second, stats)
    stats = jnp.where(line == 3, sum_first, stats)
    out_ref[rows:, :] = jnp.where(line == 4, weight_sum - sum_first, stats).astype(bf16)


def finish_kernel(*refs):
    *parts, out_ref = refs
    parts = [part[...] for part in parts]
    steps, half = out_ref.shape[:2]
    rows = steps * half * out_ref.shape[2]
    weights, _, weight_sum = merge_rows(parts, rows)
    result = weigh(parts, weights / weight_sum, rows)
    result = result.astype(bf16).reshape(half, steps, *out_ref.shape[2:])
    for b in range(half):
        out_ref[:, b] = result[b]


def place_kernel(info_ref, own_ref, other_ref, out_ref):
    half = own_ref.shape[1]
    first = info_ref[0]
    out_ref[:, pl.ds(first, half)] = own_ref[...]
    out_ref[:, pl.ds(half - first, half)] = other_ref[...]


def on_device(
    query_heads, up_keys, up_values, latent_cache, new_latent, context_lengths, positions
):
    steps, requests, heads, query_width = query_heads.shape
    nope = up_keys.shape[1]
    width = up_keys.shape[2]
    key_width = latent_cache.shape[2]
    rope = key_width - width
    value_width = up_values.shape[2]
    cached = latent_cache.shape[1]
    owners = lax.axis_size("head")
    plane = lax.axis_size("z") * lax.axis_size("x")
    pairs = steps * requests
    half = requests // 2
    scale = float(query_width) ** (-0.5) * log2_e

    core = lax.axis_index("core")
    slot = lax.axis_index(("z", "x", "core", "head"))

    vmem = pl.BlockSpec(memory_space=pltpu.VMEM)
    smem = pl.BlockSpec(memory_space=pltpu.SMEM)
    small = pltpu.CompilerParams(vmem_limit_bytes=12 * 2**20)
    anywhere = pl.BlockSpec(memory_space=pltpu.HBM)
    wide = 640
    in_hbm = functools.partial(pltpu.with_memory_space_constraint, memory_space=pltpu.HBM)
    other_first = ((1 - core) * half).astype(jnp.int32)
    own_queries, sent_queries, new_keys = pl.pallas_call(
        functools.partial(queries_kernel, steps),
        in_specs=[smem] + [anywhere] * 4,
        out_specs=[vmem, vmem, vmem],
        out_shape=(
            jax.ShapeDtypeStruct((requests, steps * heads, wide), bf16),
            jax.ShapeDtypeStruct((half, steps * heads, wide), bf16),
            jax.ShapeDtypeStruct((pairs, key_width), bf16),
        ),
        scratch_shapes=[
            pltpu.SMEM((requests,), jnp.int32),
            pltpu.VMEM((pairs, heads, query_width), bf16),
            pltpu.VMEM(up_keys.shape, bf16),
            pltpu.VMEM(new_latent.shape, bf16),
            pltpu.VMEM((pairs, heads, width), f32),
            pltpu.SemaphoreType.DMA((7,)),
        ],
        compiler_params=pltpu.CompilerParams(vmem_limit_bytes=24 * 2**20),
        name="queries",
    )(
        other_first.reshape(1),
        in_hbm(positions),
        in_hbm(query_heads.reshape(pairs, heads, query_width)),
        in_hbm(up_keys),
        in_hbm(new_latent),
    )

    def over_head(array, k):
        return lax.ppermute(array, "head", [(i, i ^ k) for i in range(owners)])

    swap = [(0, 1), (1, 0)]
    partners = (1, 3, 2)
    got = [over_head(sent_queries, k) for k in partners]
    own_first = (core * half).astype(jnp.int32)
    chunk = half * steps * heads
    at_origin = (lax.axis_index(("z", "x")) == 0).astype(jnp.int32)
    fresh = pl.pallas_call(
        functools.partial(fresh_kernel, scale, steps, heads),
        in_specs=[smem, vmem, vmem],
        out_specs=vmem,
        out_shape=jax.ShapeDtypeStruct((chunk, width + 128), bf16),
        compiler_params=small,
        cost_estimate=pl.CostEstimate(flops=10**9, bytes_accessed=4 * 10**6, transcendentals=0),
        name="fresh",
    )(jnp.stack([own_first, at_origin]), own_queries, new_keys)
    cache = in_hbm(jnp.swapaxes(latent_cache, 1, 2))
    passed = [lax.ppermute(g, "core", swap) for g in got]

    rows = owners * steps * heads

    def attend(first, got):
        info = jnp.concatenate([jnp.stack([first, slot.astype(jnp.int32) * cached]), context_lengths])
        return pl.pallas_call(
            functools.partial(attention_kernel, scale),
            in_specs=[smem] + [vmem] * 4 + [anywhere],
            out_specs=vmem,
            scratch_shapes=[
                pltpu.VMEM((half, owners, steps * heads, wide), bf16),
                pltpu.VMEM((half, key_width, cached), bf16),
                pltpu.SemaphoreType.DMA((half, 4)),
            ]
            + [pltpu.VMEM((rows, cached), f32)] * half,
            out_shape=jax.ShapeDtypeStruct((owners, chunk, width + 128), bf16),
            compiler_params=pltpu.CompilerParams(vmem_limit_bytes=24 * 2**20),
            cost_estimate=pl.CostEstimate(
                flops=2 * half * rows * cached * (key_width + width),
                bytes_accessed=half * cached * key_width * 2,
                transcendentals=half * rows * cached,
            ),
            name="attention",
        )(info, own_queries, *got, cache)

    other_part = lax.ppermute(attend(other_first, got), "core", swap)
    own_part = attend(own_first, passed)
    sent = pl.pallas_call(
        pair_kernel,
        in_specs=[vmem] * 2,
        out_specs=[vmem] * owners,
        out_shape=[jax.ShapeDtypeStruct((chunk, width + 128), bf16)] * owners,
        compiler_params=small,
        name="pair_merge",
    )(other_part, own_part)
    arrived = [over_head(array, k) for array, k in zip(sent[1:], partners)]
    part = pl.pallas_call(
        functools.partial(project_kernel, heads),
        in_specs=[vmem] * 6,
        out_specs=vmem,
        out_shape=jax.ShapeDtypeStruct((chunk + 16, value_width), bf16),
        scratch_shapes=[
            pltpu.VMEM((chunk // heads, heads, width), f32),
            pltpu.VMEM((chunk // heads, heads, value_width), f32),
        ],
        compiler_params=small,
        name="project",
    )(sent[0], *arrived, fresh, up_values)

    def over_plane(array, k):
        return lax.ppermute(array, ("z", "x"), [(i, i ^ k) for i in range(plane)])

    part = pl.pallas_call(
        middle_kernel,
        in_specs=[vmem] * 4,
        out_specs=vmem,
        out_shape=jax.ShapeDtypeStruct(part.shape, bf16),
        compiler_params=small,
        name="middle_merge",
    )(part, *[over_plane(part, k) for k in (1, 4, 5)])
    own = pl.pallas_call(
        finish_kernel,
        in_specs=[vmem] * 4,
        out_specs=vmem,
        out_shape=jax.ShapeDtypeStruct((steps, half, heads, value_width), bf16),
        compiler_params=small,
        name="finish",
    )(part, *[over_plane(part, k) for k in (3, 12, 15)])
    theirs = lax.ppermute(own, "core", swap)
    return pl.pallas_call(
        place_kernel,
        in_specs=[smem, vmem, vmem],
        out_specs=vmem,
        out_shape=jax.ShapeDtypeStruct((steps, requests, heads, value_width), bf16),
        compiler_params=small,
        name="place",
    )(own_first.reshape(1), own, theirs)


def solution(mesh):
    fine = Mesh(mesh.devices.reshape(4, 4, 2, 4), ("z", "x", "core", "head"))
    in_specs = (
        P(None, None, "head", None),
        P("head", None, None),
        P("head", None, None),
        P(None, ("z", "x", "core", "head"), None),
        P(),
        P(),
        P(),
    )
    out_specs = P(None, None, "head", None)
    return jax.shard_map(
        on_device, mesh=fine, in_specs=in_specs, out_specs=out_specs, check_vma=False
    )
```

```python
import functools

import jax
import jax.numpy as jnp
from jax import lax
from jax.experimental import pallas as pl
from jax.experimental.pallas import tpu as pltpu
from jax.sharding import Mesh, PartitionSpec as P

rope_base = 50000.0
masked_score = -1e30
lowest_max = -1e29
log2_e = 1.4426950408889634
bf16 = jnp.bfloat16
f32 = jnp.float32


def swap_halves(values):
    half = values.shape[-1] // 2
    return jnp.concatenate([values[..., half:], values[..., :half]], axis=-1)


def rope_tables(positions_ref, steps, width):
    requests = positions_ref.shape[0]
    pairs = steps * requests
    half = width // 2
    row = lax.broadcasted_iota(jnp.int32, (pairs, width), 0)
    lane = lax.broadcasted_iota(jnp.int32, (pairs, width), 1)
    where_at = row // requests
    for b in range(requests):
        where_at += jnp.where(row % requests == b, positions_ref[b], 0)
    counter = lax.broadcasted_iota(jnp.int32, (1, width), 1) % half
    inverse = jnp.zeros((1, width), f32)
    for i in range(half):
        inverse = jnp.where(counter == i, f32(rope_base ** (-2.0 * i / width)), inverse)
    angles = where_at.astype(f32) * inverse
    return jnp.cos(angles), jnp.where(lane < half, -1.0, 1.0) * jnp.sin(angles)


def queries_kernel(
    steps, info_ref, positions_hbm, q_hbm, up_hbm, new_hbm, own_ref, sent_ref, keys_ref, positions, q, up, new, lat, sems
):
    pairs, heads, _ = q.shape
    requests = pairs // steps
    nope, width = up.shape[1], up.shape[2]
    key_width = new.shape[2]
    fetches = [
        pltpu.make_async_copy(positions_hbm, positions, sems.at[0]),
        pltpu.make_async_copy(q_hbm, q, sems.at[1]),
        pltpu.make_async_copy(new_hbm, new, sems.at[2]),
    ]
    groups = 4
    share = heads // groups
    for g in range(groups):
        at = pl.ds(g * share, share)
        fetches.append(pltpu.make_async_copy(up_hbm.at[at], up.at[at], sems.at[3 + g]))
    for fetch in fetches:
        fetch.start()
    own_ref[:, :, key_width:] = jnp.zeros(own_ref.shape[:2] + (own_ref.shape[2] - key_width,), bf16)
    fetches[0].wait()
    cos, sin = rope_tables(positions, steps, key_width - width)
    fetches[1].wait()
    rope = q[:, :, nope:].astype(f32)
    rope = (rope * cos[:, None, :] + swap_halves(rope) * sin[:, None, :]).astype(bf16)
    for s in range(steps):
        for b in range(requests):
            own_ref[b, s * heads : (s + 1) * heads, width:key_width] = rope[s * requests + b]
    fetches[2].wait()
    rows = jnp.concatenate([new[t].astype(f32) for t in range(steps)], axis=0)
    tail = rows[:, width:]
    tail = tail * cos + swap_halves(tail) * sin
    keys_ref[...] = jnp.concatenate([rows[:, :width], tail], axis=-1).astype(bf16)
    q_f32 = q[:, :, :nope].astype(f32)
    for h in range(heads):
        if h % share == 0:
            fetches[3 + h // share].wait()
        lat[:, h, :] = jnp.dot(q_f32[:, h, :].astype(bf16), up[h], preferred_element_type=f32)
    for s in range(steps):
        for b in range(requests):
            own_ref[b, s * heads : (s + 1) * heads, :width] = lat[s * requests + b].astype(bf16)
    sent_ref[...] = own_ref[pl.ds(info_ref[0], sent_ref.shape[0])]


def split_stats(peak, weight_sum, rows):
    lane = lax.broadcasted_iota(jnp.int32, (rows, 128), 1)
    first = peak.astype(bf16).astype(f32)
    rest = peak - first
    second = rest.astype(bf16).astype(f32)
    third = rest - second
    sum_first = weight_sum.astype(bf16).astype(f32)
    sum_second = weight_sum - sum_first
    out = jnp.where(lane == 0, first, 0.0)
    out = jnp.where(lane == 1, second, out)
    out = jnp.where(lane == 2, third, out)
    out = jnp.where(lane == 3, sum_first, out)
    return jnp.where(lane == 4, sum_second, out)


def stage_kernel(cache_hbm, out_ref, sems):
    copies = []
    for i in range(out_ref.shape[0]):
        copies.append(pltpu.make_async_copy(cache_hbm.at[i], out_ref.at[i], sems.at[i]))
    for copy in copies:
        copy.start()
    for copy in copies:
        copy.wait()


def attention_kernel(scale, info_ref, own_ref, q1_ref, q2_ref, q3_ref, k_ref, out_ref, q_ref, *scores):
    count, owners, share, _ = q_ref.shape
    rows = owners * share
    key_width, cached = k_ref.shape[1:]
    width = out_ref.shape[2] - 128
    chunk = 1024
    first = info_ref[0]
    q_ref[:, 0] = own_ref[pl.ds(first, count)]
    q_ref[:, 1] = q1_ref[...]
    q_ref[:, 2] = q2_ref[...]
    q_ref[:, 3] = q3_ref[...]

    tops = []
    for i in range(count):
        limit = info_ref[2 + first + i] - info_ref[1]
        queries = q_ref[i].reshape(rows, -1)[:, :key_width]
        top = jnp.full((rows, 128), lowest_max, f32)
        for c in range(0, cached, chunk):
            keys = k_ref[first + i, :, c : c + chunk]
            part = jnp.dot(queries, keys, preferred_element_type=f32) * scale
            column = lax.broadcasted_iota(jnp.int32, (1, chunk), 1) + c
            part = jnp.where(column < limit, part, masked_score)
            scores[i][:, c : c + chunk] = part
            for at in range(0, chunk, 128):
                top = jnp.maximum(top, part[:, at : at + 128])
        tops.append(jnp.max(top, axis=1, keepdims=True))

    for i in range(count):
        total = jnp.zeros((rows, 128), f32)
        for c in range(0, cached, chunk):
            weights = jnp.exp2(scores[i][:, c : c + chunk] - tops[i])
            for at in range(0, chunk, 128):
                total = total + weights[:, at : at + 128]
            part = lax.dot_general(
                weights.astype(bf16),
                k_ref[first + i, :width, c : c + chunk],
                (((1,), (1,)), ((), ())),
                preferred_element_type=f32,
            )
            mixed = part if c == 0 else mixed + part
        total = jnp.sum(total, axis=1, keepdims=True)
        at = slice(i * share, (i + 1) * share)
        out_ref[:, at, :width] = mixed.astype(bf16).reshape(owners, share, width)
        out_ref[:, at, width:] = split_stats(tops[i], total, rows).astype(bf16).reshape(owners, share, 128)


def fresh_kernel(scale, steps, heads, info_ref, own_ref, new_ref, out_ref):
    requests, share, _ = own_ref.shape
    key_width = new_ref.shape[1]
    width = out_ref.shape[1] - 128
    fresh = new_ref[...]
    shape = (share, fresh.shape[0])
    key = lax.broadcasted_iota(jnp.int32, shape, 1)
    step = (lax.broadcasted_iota(jnp.int32, shape, 0) // heads) % steps
    counted = info_ref[1] == 1
    for i in range(out_ref.shape[0] // share):
        request = info_ref[0] + i
        scores = (
            lax.dot_general(
                own_ref[request][:, :key_width], fresh, (((1,), (1,)), ((), ())), preferred_element_type=f32
            )
            * scale
        )
        visible = (key % requests == request) & (key // requests <= step) & counted
        scores = jnp.where(visible, scores, masked_score)
        top = jnp.maximum(jnp.max(scores, axis=1, keepdims=True), lowest_max)
        weights = jnp.exp2(scores - top)
        total = jnp.sum(weights, axis=1, keepdims=True)
        mixed = jnp.dot(weights.astype(bf16), fresh[:, :width], preferred_element_type=f32)
        at = slice(i * share, (i + 1) * share)
        out_ref[at, :width] = mixed.astype(bf16)
        out_ref[at, width:] = split_stats(top, total, share).astype(bf16)


def merge_parts(parts, width):
    tops = []
    sums = []
    for part in parts:
        stat = part[:, width:].astype(f32)
        tops.append(stat[:, 0:1] + stat[:, 1:2] + stat[:, 2:3])
        sums.append(stat[:, 3:4] + stat[:, 4:5])
    peak = functools.reduce(jnp.maximum, tops)
    weights = [jnp.exp2(t - peak) for t in tops]
    weight_sum = sum(w * s for w, s in zip(weights, sums))
    merged = sum(w * part[:, :width].astype(f32) for w, part in zip(weights, parts))
    return merged, peak, weight_sum


def pair_kernel(a_ref, b_ref, *sent_refs):
    rows = sent_refs[0].shape[0]
    width = a_ref.shape[2] - 128
    for owner, sent_ref in enumerate(sent_refs):
        merged, peak, weight_sum = merge_parts((a_ref[owner], b_ref[owner]), width)
        sent_ref[:, :width] = merged.astype(bf16)
        sent_ref[:, width:] = split_stats(peak, weight_sum, rows).astype(bf16)


def project_kernel(heads, *refs):
    *parts, up_ref, out_ref, mixed, projected = refs
    rows = parts[0].shape[0]
    merged, peak, weight_sum = merge_parts([part[...] for part in parts], up_ref.shape[1])
    mixed[...] = merged.reshape(mixed.shape)
    stats = split_stats(peak, weight_sum, rows).T[:16].astype(bf16)
    count = rows // heads
    for h in range(heads):
        part = mixed[:, h, :]
        high = part.astype(bf16)
        low = (part - high.astype(f32)).astype(bf16)
        both = jnp.dot(jnp.concatenate([high, low], axis=0), up_ref[h], preferred_element_type=f32)
        projected[:, h, :] = both[:count] + both[count:]
    values = projected[...].reshape(rows, projected.shape[2]).astype(bf16)
    out_ref[:rows, :] = values
    out_ref[rows:, :] = stats


def merge_rows(parts, rows):
    tops = []
    sums = []
    for part in parts:
        stat = part[rows:, :].astype(f32)
        tops.append(stat[0:1] + stat[1:2] + stat[2:3])
        sums.append(stat[3:4] + stat[4:5])
    tops = jnp.concatenate(tops, axis=0)
    peak = jnp.max(tops, axis=0, keepdims=True)
    weights = jnp.exp2(tops - peak)
    weight_sum = jnp.sum(weights * jnp.concatenate(sums, axis=0), axis=0, keepdims=True)
    return weights, peak, weight_sum


def weigh(parts, weights, rows):
    spread = jnp.concatenate([weights, jnp.zeros((128 - len(parts), weights.shape[1]), f32)], axis=0).T
    return sum(part[:rows, :].astype(f32) * spread[:rows, i : i + 1] for i, part in enumerate(parts))


def middle_kernel(*refs):
    *parts, out_ref = refs
    parts = [part[...] for part in parts]
    rows = out_ref.shape[0] - 16
    weights, peak, weight_sum = merge_rows(parts, rows)
    out_ref[:rows, :] = weigh(parts, weights, rows).astype(bf16)
    line = lax.broadcasted_iota(jnp.int32, (16, weights.shape[1]), 0)
    first = peak.astype(bf16).astype(f32)
    second = (peak - first).astype(bf16).astype(f32)
    sum_first = weight_sum.astype(bf16).astype(f32)
    stats = jnp.where(line == 0, first, 0.0)
    stats = jnp.where(line == 1, second, stats)
    stats = jnp.where(line == 2, peak - first - second, stats)
    stats = jnp.where(line == 3, sum_first, stats)
    out_ref[rows:, :] = jnp.where(line == 4, weight_sum - sum_first, stats).astype(bf16)


def finish_kernel(*refs):
    *parts, out_ref = refs
    parts = [part[...] for part in parts]
    steps, half = out_ref.shape[:2]
    rows = steps * half * out_ref.shape[2]
    weights, _, weight_sum = merge_rows(parts, rows)
    result = weigh(parts, weights / weight_sum, rows)
    result = result.astype(bf16).reshape(half, steps, *out_ref.shape[2:])
    for b in range(half):
        out_ref[:, b] = result[b]


def place_kernel(info_ref, own_ref, other_ref, out_ref):
    half = own_ref.shape[1]
    first = info_ref[0]
    out_ref[:, pl.ds(first, half)] = own_ref[...]
    out_ref[:, pl.ds(half - first, half)] = other_ref[...]


def on_device(
    query_heads, up_keys, up_values, latent_cache, new_latent, context_lengths, positions
):
    steps, requests, heads, query_width = query_heads.shape
    nope = up_keys.shape[1]
    width = up_keys.shape[2]
    key_width = latent_cache.shape[2]
    rope = key_width - width
    value_width = up_values.shape[2]
    cached = latent_cache.shape[1]
    owners = lax.axis_size("head")
    plane = lax.axis_size("z") * lax.axis_size("x")
    pairs = steps * requests
    half = requests // 2
    scale = float(query_width) ** (-0.5) * log2_e

    core = lax.axis_index("core")
    slot = lax.axis_index(("z", "x", "core", "head"))

    vmem = pl.BlockSpec(memory_space=pltpu.VMEM)
    smem = pl.BlockSpec(memory_space=pltpu.SMEM)
    small = pltpu.CompilerParams(vmem_limit_bytes=12 * 2**20)
    anywhere = pl.BlockSpec(memory_space=pltpu.HBM)
    wide = 640
    in_hbm = functools.partial(pltpu.with_memory_space_constraint, memory_space=pltpu.HBM)
    other_first = ((1 - core) * half).astype(jnp.int32)
    own_queries, sent_queries, new_keys = pl.pallas_call(
        functools.partial(queries_kernel, steps),
        in_specs=[smem] + [anywhere] * 4,
        out_specs=[vmem, vmem, vmem],
        out_shape=(
            jax.ShapeDtypeStruct((requests, steps * heads, wide), bf16),
            jax.ShapeDtypeStruct((half, steps * heads, wide), bf16),
            jax.ShapeDtypeStruct((pairs, key_width), bf16),
        ),
        scratch_shapes=[
            pltpu.SMEM((requests,), jnp.int32),
            pltpu.VMEM((pairs, heads, query_width), bf16),
            pltpu.VMEM(up_keys.shape, bf16),
            pltpu.VMEM(new_latent.shape, bf16),
            pltpu.VMEM((pairs, heads, width), f32),
            pltpu.SemaphoreType.DMA((7,)),
        ],
        compiler_params=pltpu.CompilerParams(vmem_limit_bytes=24 * 2**20),
        name="queries",
    )(
        other_first.reshape(1),
        in_hbm(positions),
        in_hbm(query_heads.reshape(pairs, heads, query_width)),
        in_hbm(up_keys),
        in_hbm(new_latent),
    )

    def over_head(array, k):
        return lax.ppermute(array, "head", [(i, i ^ k) for i in range(owners)])

    swap = [(0, 1), (1, 0)]
    partners = (1, 3, 2)
    got = [over_head(sent_queries, k) for k in partners]
    own_first = (core * half).astype(jnp.int32)
    chunk = half * steps * heads
    at_origin = (lax.axis_index(("z", "x")) == 0).astype(jnp.int32)
    fresh = pl.pallas_call(
        functools.partial(fresh_kernel, scale, steps, heads),
        in_specs=[smem, vmem, vmem],
        out_specs=vmem,
        out_shape=jax.ShapeDtypeStruct((chunk, width + 128), bf16),
        compiler_params=small,
        cost_estimate=pl.CostEstimate(flops=10**9, bytes_accessed=4 * 10**6, transcendentals=0),
        name="fresh",
    )(jnp.stack([own_first, at_origin]), own_queries, new_keys)
    cache = pl.pallas_call(
        stage_kernel,
        in_specs=[anywhere],
        out_specs=vmem,
        out_shape=pltpu.VMEM((requests, key_width, cached), bf16),
        scratch_shapes=[pltpu.SemaphoreType.DMA((requests,))],
        compiler_params=small,
        cost_estimate=pl.CostEstimate(flops=0, bytes_accessed=2 * requests * key_width * cached, transcendentals=0),
        name="stage",
    )(in_hbm(jnp.swapaxes(latent_cache, 1, 2)))
    cache = pltpu.with_memory_space_constraint(cache, memory_space=pltpu.VMEM)
    got[2], cache = lax.optimization_barrier((got[2], cache))
    passed = [lax.ppermute(g, "core", swap) for g in got]
    got, passed = lax.optimization_barrier((got, passed))

    rows = owners * steps * heads

    def attend(first, got):
        info = jnp.concatenate([jnp.stack([first, slot.astype(jnp.int32) * cached]), context_lengths])
        return pl.pallas_call(
            functools.partial(attention_kernel, scale),
            in_specs=[smem] + [vmem] * 5,
            out_specs=vmem,
            scratch_shapes=[
                pltpu.VMEM((half, owners, steps * heads, wide), bf16),
            ]
            + [pltpu.VMEM((rows, cached), f32)] * half,
            out_shape=jax.ShapeDtypeStruct((owners, chunk, width + 128), bf16),
            compiler_params=pltpu.CompilerParams(vmem_limit_bytes=24 * 2**20),
            cost_estimate=pl.CostEstimate(
                flops=2 * half * rows * cached * (key_width + width),
                bytes_accessed=half * cached * key_width * 2,
                transcendentals=half * rows * cached,
            ),
            name="attention",
        )(info, own_queries, *got, cache)

    other_part = lax.ppermute(attend(other_first, got), "core", swap)
    own_part = attend(own_first, passed)
    sent = pl.pallas_call(
        pair_kernel,
        in_specs=[vmem] * 2,
        out_specs=[vmem] * owners,
        out_shape=[jax.ShapeDtypeStruct((chunk, width + 128), bf16)] * owners,
        compiler_params=small,
        name="pair_merge",
    )(other_part, own_part)
    arrived = [over_head(array, k) for array, k in zip(sent[1:], partners)]
    part = pl.pallas_call(
        functools.partial(project_kernel, heads),
        in_specs=[vmem] * 6,
        out_specs=vmem,
        out_shape=jax.ShapeDtypeStruct((chunk + 16, value_width), bf16),
        scratch_shapes=[
            pltpu.VMEM((chunk // heads, heads, width), f32),
            pltpu.VMEM((chunk // heads, heads, value_width), f32),
        ],
        compiler_params=small,
        name="project",
    )(sent[0], *arrived, fresh, up_values)

    def over_plane(array, k):
        return lax.ppermute(array, ("z", "x"), [(i, i ^ k) for i in range(plane)])

    part = pl.pallas_call(
        middle_kernel,
        in_specs=[vmem] * 4,
        out_specs=vmem,
        out_shape=jax.ShapeDtypeStruct(part.shape, bf16),
        compiler_params=small,
        name="middle_merge",
    )(part, *[over_plane(part, k) for k in (1, 4, 5)])
    own = pl.pallas_call(
        finish_kernel,
        in_specs=[vmem] * 4,
        out_specs=vmem,
        out_shape=jax.ShapeDtypeStruct((steps, half, heads, value_width), bf16),
        compiler_params=small,
        name="finish",
    )(part, *[over_plane(part, k) for k in (3, 12, 15)])
    theirs = lax.ppermute(own, "core", swap)
    return pl.pallas_call(
        place_kernel,
        in_specs=[smem, vmem, vmem],
        out_specs=vmem,
        out_shape=jax.ShapeDtypeStruct((steps, requests, heads, value_width), bf16),
        compiler_params=small,
        name="place",
    )(own_first.reshape(1), own, theirs)


def solution(mesh):
    fine = Mesh(mesh.devices.reshape(4, 4, 2, 4), ("z", "x", "core", "head"))
    in_specs = (
        P(None, None, "head", None),
        P("head", None, None),
        P("head", None, None),
        P(None, ("z", "x", "core", "head"), None),
        P(),
        P(),
        P(),
    )
    out_specs = P(None, None, "head", None)
    return jax.shard_map(
        on_device, mesh=fine, in_specs=in_specs, out_specs=out_specs, check_vma=False
    )
```

```python
import functools

import jax
import jax.numpy as jnp
from jax import lax
from jax.experimental import pallas as pl
from jax.experimental.pallas import tpu as pltpu
from jax.sharding import Mesh, PartitionSpec as P

rope_base = 50000.0
masked_score = -1e30
lowest_max = -1e29
log2_e = 1.4426950408889634
bf16 = jnp.bfloat16
f32 = jnp.float32


def swap_halves(values):
    half = values.shape[-1] // 2
    return jnp.concatenate([values[..., half:], values[..., :half]], axis=-1)


def rope_tables(positions_ref, steps, width):
    requests = positions_ref.shape[0]
    pairs = steps * requests
    half = width // 2
    row = lax.broadcasted_iota(jnp.int32, (pairs, width), 0)
    lane = lax.broadcasted_iota(jnp.int32, (pairs, width), 1)
    where_at = row // requests
    for b in range(requests):
        where_at += jnp.where(row % requests == b, positions_ref[b], 0)
    counter = lax.broadcasted_iota(jnp.int32, (1, width), 1) % half
    inverse = jnp.zeros((1, width), f32)
    for i in range(half):
        inverse = jnp.where(counter == i, f32(rope_base ** (-2.0 * i / width)), inverse)
    angles = where_at.astype(f32) * inverse
    return jnp.cos(angles), jnp.where(lane < half, -1.0, 1.0) * jnp.sin(angles)


def queries_kernel(
    steps, info_ref, positions_hbm, q_hbm, up_hbm, new_hbm, own_ref, sent_ref, keys_ref, positions, q, up, new, lat, sems
):
    pairs, heads, _ = q.shape
    requests = pairs // steps
    nope, width = up.shape[1], up.shape[2]
    key_width = new.shape[2]
    fetches = [
        pltpu.make_async_copy(positions_hbm, positions, sems.at[0]),
        pltpu.make_async_copy(q_hbm, q, sems.at[1]),
        pltpu.make_async_copy(new_hbm, new, sems.at[2]),
    ]
    groups = 4
    share = heads // groups
    for g in range(groups):
        at = pl.ds(g * share, share)
        fetches.append(pltpu.make_async_copy(up_hbm.at[at], up.at[at], sems.at[3 + g]))
    for fetch in fetches:
        fetch.start()
    own_ref[:, :, key_width:] = jnp.zeros(own_ref.shape[:2] + (own_ref.shape[2] - key_width,), bf16)
    fetches[0].wait()
    cos, sin = rope_tables(positions, steps, key_width - width)
    fetches[1].wait()
    rope = q[:, :, nope:].astype(f32)
    rope = (rope * cos[:, None, :] + swap_halves(rope) * sin[:, None, :]).astype(bf16)
    for s in range(steps):
        for b in range(requests):
            own_ref[b, s * heads : (s + 1) * heads, width:key_width] = rope[s * requests + b]
    fetches[2].wait()
    rows = jnp.concatenate([new[t].astype(f32) for t in range(steps)], axis=0)
    tail = rows[:, width:]
    tail = tail * cos + swap_halves(tail) * sin
    keys_ref[...] = jnp.concatenate([rows[:, :width], tail], axis=-1).astype(bf16)
    q_f32 = q[:, :, :nope].astype(f32)
    for h in range(heads):
        if h % share == 0:
            fetches[3 + h // share].wait()
        lat[:, h, :] = jnp.dot(q_f32[:, h, :].astype(bf16), up[h], preferred_element_type=f32)
    for s in range(steps):
        for b in range(requests):
            own_ref[b, s * heads : (s + 1) * heads, :width] = lat[s * requests + b].astype(bf16)
    sent_ref[...] = own_ref[pl.ds(info_ref[0], sent_ref.shape[0])]


def split_stats(peak, weight_sum, rows):
    lane = lax.broadcasted_iota(jnp.int32, (rows, 128), 1)
    first = peak.astype(bf16).astype(f32)
    rest = peak - first
    second = rest.astype(bf16).astype(f32)
    third = rest - second
    sum_first = weight_sum.astype(bf16).astype(f32)
    sum_second = weight_sum - sum_first
    out = jnp.where(lane == 0, first, 0.0)
    out = jnp.where(lane == 1, second, out)
    out = jnp.where(lane == 2, third, out)
    out = jnp.where(lane == 3, sum_first, out)
    return jnp.where(lane == 4, sum_second, out)


def stage_kernel(info_ref, cache_hbm, out_ref, sems):
    copies = []
    for i in range(out_ref.shape[0]):
        copies.append(pltpu.make_async_copy(cache_hbm.at[info_ref[0] + i], out_ref.at[i], sems.at[i]))
    for copy in copies:
        copy.start()
    for copy in copies:
        copy.wait()


def first_attention_kernel(
    scale, info_ref, own_ref, q1_ref, q2_ref, q3_ref, k_ref, cache_hbm, out_ref, next_ref, q_ref, sems, *scores
):
    copies = []
    for i in range(next_ref.shape[0]):
        source = cache_hbm.at[info_ref[1] + i]
        copies.append(pltpu.make_async_copy(source, next_ref.at[i], sems.at[i]))
    for copy in copies:
        copy.start()
    attention_kernel(scale, 0, info_ref, own_ref, q1_ref, q2_ref, q3_ref, k_ref, out_ref, q_ref, *scores)
    for copy in copies:
        copy.wait()


def attention_kernel(scale, which, info_ref, own_ref, q1_ref, q2_ref, q3_ref, k_ref, out_ref, q_ref, *scores):
    count, owners, share, _ = q_ref.shape
    rows = owners * share
    key_width, cached = k_ref.shape[1:]
    width = out_ref.shape[2] - 128
    chunk = 1024
    first = info_ref[which]
    q_ref[:, 0] = own_ref[pl.ds(first, count)]
    q_ref[:, 1] = q1_ref[...]
    q_ref[:, 2] = q2_ref[...]
    q_ref[:, 3] = q3_ref[...]

    tops = []
    for i in range(count):
        limit = info_ref[4 + first + i] - info_ref[2]
        queries = q_ref[i].reshape(rows, -1)[:, :key_width]
        top = jnp.full((rows, 128), lowest_max, f32)
        for c in range(0, cached, chunk):
            keys = k_ref[i, :, c : c + chunk]
            part = jnp.dot(queries, keys, preferred_element_type=f32) * scale
            column = lax.broadcasted_iota(jnp.int32, (1, chunk), 1) + c
            part = jnp.where(column < limit, part, masked_score)
            scores[i][:, c : c + chunk] = part
            for at in range(0, chunk, 128):
                top = jnp.maximum(top, part[:, at : at + 128])
        tops.append(jnp.max(top, axis=1, keepdims=True))

    for i in range(count):
        total = jnp.zeros((rows, 128), f32)
        for c in range(0, cached, chunk):
            weights = jnp.exp2(scores[i][:, c : c + chunk] - tops[i])
            for at in range(0, chunk, 128):
                total = total + weights[:, at : at + 128]
            part = lax.dot_general(
                weights.astype(bf16),
                k_ref[i, :width, c : c + chunk],
                (((1,), (1,)), ((), ())),
                preferred_element_type=f32,
            )
            mixed = part if c == 0 else mixed + part
        total = jnp.sum(total, axis=1, keepdims=True)
        at = slice(i * share, (i + 1) * share)
        out_ref[:, at, :width] = mixed.astype(bf16).reshape(owners, share, width)
        out_ref[:, at, width:] = split_stats(tops[i], total, rows).astype(bf16).reshape(owners, share, 128)


def fresh_kernel(scale, steps, heads, info_ref, own_ref, new_ref, out_ref):
    requests, share, _ = own_ref.shape
    key_width = new_ref.shape[1]
    width = out_ref.shape[1] - 128
    fresh = new_ref[...]
    shape = (share, fresh.shape[0])
    key = lax.broadcasted_iota(jnp.int32, shape, 1)
    step = (lax.broadcasted_iota(jnp.int32, shape, 0) // heads) % steps
    counted = info_ref[3] == 1
    for i in range(out_ref.shape[0] // share):
        request = info_ref[1] + i
        scores = (
            lax.dot_general(
                own_ref[request][:, :key_width], fresh, (((1,), (1,)), ((), ())), preferred_element_type=f32
            )
            * scale
        )
        visible = (key % requests == request) & (key // requests <= step) & counted
        scores = jnp.where(visible, scores, masked_score)
        top = jnp.maximum(jnp.max(scores, axis=1, keepdims=True), lowest_max)
        weights = jnp.exp2(scores - top)
        total = jnp.sum(weights, axis=1, keepdims=True)
        mixed = jnp.dot(weights.astype(bf16), fresh[:, :width], preferred_element_type=f32)
        at = slice(i * share, (i + 1) * share)
        out_ref[at, :width] = mixed.astype(bf16)
        out_ref[at, width:] = split_stats(top, total, share).astype(bf16)


def merge_parts(parts, width):
    tops = []
    sums = []
    for part in parts:
        stat = part[:, width:].astype(f32)
        tops.append(stat[:, 0:1] + stat[:, 1:2] + stat[:, 2:3])
        sums.append(stat[:, 3:4] + stat[:, 4:5])
    peak = functools.reduce(jnp.maximum, tops)
    weights = [jnp.exp2(t - peak) for t in tops]
    weight_sum = sum(w * s for w, s in zip(weights, sums))
    merged = sum(w * part[:, :width].astype(f32) for w, part in zip(weights, parts))
    return merged, peak, weight_sum


def pair_kernel(a_ref, b_ref, *sent_refs):
    rows = sent_refs[0].shape[0]
    width = a_ref.shape[2] - 128
    for owner, sent_ref in enumerate(sent_refs):
        merged, peak, weight_sum = merge_parts((a_ref[owner], b_ref[owner]), width)
        sent_ref[:, :width] = merged.astype(bf16)
        sent_ref[:, width:] = split_stats(peak, weight_sum, rows).astype(bf16)


def project_kernel(heads, *refs):
    *parts, up_ref, out_ref, mixed, projected = refs
    rows = parts[0].shape[0]
    merged, peak, weight_sum = merge_parts([part[...] for part in parts], up_ref.shape[1])
    mixed[...] = merged.reshape(mixed.shape)
    stats = split_stats(peak, weight_sum, rows).T[:16].astype(bf16)
    count = rows // heads
    for h in range(heads):
        part = mixed[:, h, :]
        high = part.astype(bf16)
        low = (part - high.astype(f32)).astype(bf16)
        both = jnp.dot(jnp.concatenate([high, low], axis=0), up_ref[h], preferred_element_type=f32)
        projected[:, h, :] = both[:count] + both[count:]
    values = projected[...].reshape(rows, projected.shape[2]).astype(bf16)
    out_ref[:rows, :] = values
    out_ref[rows:, :] = stats


def merge_rows(parts, rows):
    tops = []
    sums = []
    for part in parts:
        stat = part[rows:, :].astype(f32)
        tops.append(stat[0:1] + stat[1:2] + stat[2:3])
        sums.append(stat[3:4] + stat[4:5])
    tops = jnp.concatenate(tops, axis=0)
    peak = jnp.max(tops, axis=0, keepdims=True)
    weights = jnp.exp2(tops - peak)
    weight_sum = jnp.sum(weights * jnp.concatenate(sums, axis=0), axis=0, keepdims=True)
    return weights, peak, weight_sum


def weigh(parts, weights, rows):
    spread = jnp.concatenate([weights, jnp.zeros((128 - len(parts), weights.shape[1]), f32)], axis=0).T
    return sum(part[:rows, :].astype(f32) * spread[:rows, i : i + 1] for i, part in enumerate(parts))


def middle_kernel(*refs):
    *parts, out_ref = refs
    parts = [part[...] for part in parts]
    rows = out_ref.shape[0] - 16
    weights, peak, weight_sum = merge_rows(parts, rows)
    out_ref[:rows, :] = weigh(parts, weights, rows).astype(bf16)
    line = lax.broadcasted_iota(jnp.int32, (16, weights.shape[1]), 0)
    first = peak.astype(bf16).astype(f32)
    second = (peak - first).astype(bf16).astype(f32)
    sum_first = weight_sum.astype(bf16).astype(f32)
    stats = jnp.where(line == 0, first, 0.0)
    stats = jnp.where(line == 1, second, stats)
    stats = jnp.where(line == 2, peak - first - second, stats)
    stats = jnp.where(line == 3, sum_first, stats)
    out_ref[rows:, :] = jnp.where(line == 4, weight_sum - sum_first, stats).astype(bf16)


def finish_kernel(*refs):
    *parts, out_ref = refs
    parts = [part[...] for part in parts]
    steps, half = out_ref.shape[:2]
    rows = steps * half * out_ref.shape[2]
    weights, _, weight_sum = merge_rows(parts, rows)
    result = weigh(parts, weights / weight_sum, rows)
    result = result.astype(bf16).reshape(half, steps, *out_ref.shape[2:])
    for b in range(half):
        out_ref[:, b] = result[b]


def place_kernel(info_ref, own_ref, other_ref, out_ref):
    half = own_ref.shape[1]
    first = info_ref[1]
    out_ref[:, pl.ds(first, half)] = own_ref[...]
    out_ref[:, pl.ds(half - first, half)] = other_ref[...]


def on_device(
    query_heads, up_keys, up_values, latent_cache, new_latent, context_lengths, positions
):
    steps, requests, heads, query_width = query_heads.shape
    nope = up_keys.shape[1]
    width = up_keys.shape[2]
    key_width = latent_cache.shape[2]
    rope = key_width - width
    value_width = up_values.shape[2]
    cached = latent_cache.shape[1]
    owners = lax.axis_size("head")
    plane = lax.axis_size("z") * lax.axis_size("x")
    pairs = steps * requests
    half = requests // 2
    scale = float(query_width) ** (-0.5) * log2_e

    core = lax.axis_index("core")
    slot = lax.axis_index(("z", "x", "core", "head"))

    vmem = pl.BlockSpec(memory_space=pltpu.VMEM)
    smem = pl.BlockSpec(memory_space=pltpu.SMEM)
    small = pltpu.CompilerParams(vmem_limit_bytes=12 * 2**20)
    anywhere = pl.BlockSpec(memory_space=pltpu.HBM)
    wide = 640
    in_hbm = functools.partial(pltpu.with_memory_space_constraint, memory_space=pltpu.HBM)
    own_first = core * half
    at_origin = lax.axis_index(("z", "x")) == 0
    info = jnp.stack([half - own_first, own_first, slot * cached, at_origin])
    info = jnp.concatenate([info.astype(jnp.int32), context_lengths])
    chunk = half * steps * heads
    own_queries, sent_queries, new_keys = pl.pallas_call(
        functools.partial(queries_kernel, steps),
        in_specs=[smem] + [anywhere] * 4,
        out_specs=[vmem, vmem, vmem],
        out_shape=(
            jax.ShapeDtypeStruct((requests, steps * heads, wide), bf16),
            jax.ShapeDtypeStruct((half, steps * heads, wide), bf16),
            jax.ShapeDtypeStruct((pairs, key_width), bf16),
        ),
        scratch_shapes=[
            pltpu.SMEM((requests,), jnp.int32),
            pltpu.VMEM((pairs, heads, query_width), bf16),
            pltpu.VMEM(up_keys.shape, bf16),
            pltpu.VMEM(new_latent.shape, bf16),
            pltpu.VMEM((pairs, heads, width), f32),
            pltpu.SemaphoreType.DMA((7,)),
        ],
        compiler_params=pltpu.CompilerParams(vmem_limit_bytes=24 * 2**20),
        name="queries",
    )(
        info,
        in_hbm(positions),
        in_hbm(query_heads.reshape(pairs, heads, query_width)),
        in_hbm(up_keys),
        in_hbm(new_latent),
    )

    def over_head(array, k):
        return lax.ppermute(array, "head", [(i, i ^ k) for i in range(owners)])

    swap = [(0, 1), (1, 0)]
    partners = (1, 3, 2)
    got = [over_head(sent_queries, k) for k in partners]
    fresh = pl.pallas_call(
        functools.partial(fresh_kernel, scale, steps, heads),
        in_specs=[smem, vmem, vmem],
        out_specs=vmem,
        out_shape=jax.ShapeDtypeStruct((chunk, width + 128), bf16),
        compiler_params=small,
        cost_estimate=pl.CostEstimate(flops=10**9, bytes_accessed=4 * 10**6, transcendentals=0),
        name="fresh",
    )(info, own_queries, new_keys)
    cache = in_hbm(jnp.swapaxes(latent_cache, 1, 2))
    staged_shape = pltpu.VMEM((half, key_width, cached), bf16)
    in_vmem = functools.partial(pltpu.with_memory_space_constraint, memory_space=pltpu.VMEM)
    staged = pl.pallas_call(
        stage_kernel,
        in_specs=[smem, anywhere],
        out_specs=vmem,
        out_shape=staged_shape,
        scratch_shapes=[pltpu.SemaphoreType.DMA((half,))],
        compiler_params=small,
        cost_estimate=pl.CostEstimate(flops=0, bytes_accessed=2 * half * key_width * cached, transcendentals=0),
        name="stage",
    )(info, cache)
    got[2], staged = lax.optimization_barrier((got[2], staged))
    passed = [lax.ppermute(g, "core", swap) for g in got]
    got, passed = lax.optimization_barrier((got, passed))

    rows = owners * steps * heads

    def attend(got, keys, is_first):
        part_shape = jax.ShapeDtypeStruct((owners, chunk, width + 128), bf16)
        scratch = [pltpu.VMEM((half, owners, steps * heads, wide), bf16)]
        scores = [pltpu.VMEM((rows, cached), f32)] * half
        return pl.pallas_call(
            functools.partial(first_attention_kernel, scale)
            if is_first
            else functools.partial(attention_kernel, scale, 1),
            in_specs=[smem] + [vmem] * 5 + [anywhere] * is_first,
            out_specs=[vmem] * 2 if is_first else vmem,
            scratch_shapes=scratch + [pltpu.SemaphoreType.DMA((half,))] * is_first + scores,
            out_shape=[part_shape, staged_shape] if is_first else part_shape,
            compiler_params=pltpu.CompilerParams(vmem_limit_bytes=18 * 2**20),
            cost_estimate=pl.CostEstimate(
                flops=2 * half * rows * cached * (key_width + width),
                bytes_accessed=half * cached * key_width * 2,
                transcendentals=half * rows * cached,
            ),
            name="attention",
        )(info, own_queries, *got, in_vmem(keys), *[cache] * is_first)

    other_part, staged = attend(got, staged, True)
    other_part = lax.ppermute(other_part, "core", swap)
    own_part = attend(passed, staged, False)
    sent = pl.pallas_call(
        pair_kernel,
        in_specs=[vmem] * 2,
        out_specs=[vmem] * owners,
        out_shape=[jax.ShapeDtypeStruct((chunk, width + 128), bf16)] * owners,
        compiler_params=small,
        name="pair_merge",
    )(other_part, own_part)
    arrived = [over_head(array, k) for array, k in zip(sent[1:], partners)]
    part = pl.pallas_call(
        functools.partial(project_kernel, heads),
        in_specs=[vmem] * 6,
        out_specs=vmem,
        out_shape=jax.ShapeDtypeStruct((chunk + 16, value_width), bf16),
        scratch_shapes=[
            pltpu.VMEM((chunk // heads, heads, width), f32),
            pltpu.VMEM((chunk // heads, heads, value_width), f32),
        ],
        compiler_params=small,
        name="project",
    )(sent[0], *arrived, fresh, up_values)

    def over_plane(array, k):
        return lax.ppermute(array, ("z", "x"), [(i, i ^ k) for i in range(plane)])

    part = pl.pallas_call(
        middle_kernel,
        in_specs=[vmem] * 4,
        out_specs=vmem,
        out_shape=jax.ShapeDtypeStruct(part.shape, bf16),
        compiler_params=small,
        name="middle_merge",
    )(part, *[over_plane(part, k) for k in (1, 4, 5)])
    own = pl.pallas_call(
        finish_kernel,
        in_specs=[vmem] * 4,
        out_specs=vmem,
        out_shape=jax.ShapeDtypeStruct((steps, half, heads, value_width), bf16),
        compiler_params=small,
        name="finish",
    )(part, *[over_plane(part, k) for k in (3, 12, 15)])
    theirs = lax.ppermute(own, "core", swap)
    return pl.pallas_call(
        place_kernel,
        in_specs=[smem, vmem, vmem],
        out_specs=vmem,
        out_shape=jax.ShapeDtypeStruct((steps, requests, heads, value_width), bf16),
        compiler_params=small,
        name="place",
    )(info, own, theirs)


def solution(mesh):
    fine = Mesh(mesh.devices.reshape(4, 4, 2, 4), ("z", "x", "core", "head"))
    in_specs = (
        P(None, None, "head", None),
        P("head", None, None),
        P("head", None, None),
        P(None, ("z", "x", "core", "head"), None),
        P(),
        P(),
        P(),
    )
    out_specs = P(None, None, "head", None)
    return jax.shard_map(
        on_device, mesh=fine, in_specs=in_specs, out_specs=out_specs, check_vma=False
    )
```

```python
import functools

import jax
import jax.numpy as jnp
from jax import lax
from jax.experimental import pallas as pl
from jax.experimental.pallas import tpu as pltpu
from jax.sharding import Mesh, PartitionSpec as P

rope_base = 50000.0
masked_score = -1e30
lowest_max = -1e29
log2_e = 1.4426950408889634
bf16 = jnp.bfloat16
f32 = jnp.float32


def swap_halves(values):
    half = values.shape[-1] // 2
    return jnp.concatenate([values[..., half:], values[..., :half]], axis=-1)


def rope_tables(positions_ref, steps, width):
    requests = positions_ref.shape[0]
    pairs = steps * requests
    half = width // 2
    row = lax.broadcasted_iota(jnp.int32, (pairs, width), 0)
    lane = lax.broadcasted_iota(jnp.int32, (pairs, width), 1)
    where_at = row // requests
    for b in range(requests):
        where_at += jnp.where(row % requests == b, positions_ref[b], 0)
    counter = lax.broadcasted_iota(jnp.int32, (1, width), 1) % half
    inverse = jnp.zeros((1, width), f32)
    for i in range(half):
        inverse = jnp.where(counter == i, f32(rope_base ** (-2.0 * i / width)), inverse)
    angles = where_at.astype(f32) * inverse
    return jnp.cos(angles), jnp.where(lane < half, -1.0, 1.0) * jnp.sin(angles)


def queries_kernel(
    steps,
    info_ref,
    row_ref,
    positions_hbm,
    lengths_hbm,
    q_hbm,
    up_hbm,
    new_hbm,
    own_ref,
    sent_ref,
    keys_ref,
    limits_ref,
    positions,
    lengths,
    q,
    up,
    new,
    lat,
    sems,
):
    pairs, heads, _ = q.shape
    requests = pairs // steps
    nope, width = up.shape[1], up.shape[2]
    key_width = new.shape[2]
    fetches = [
        pltpu.make_async_copy(positions_hbm, positions, sems.at[0]),
        pltpu.make_async_copy(q_hbm, q, sems.at[1]),
        pltpu.make_async_copy(new_hbm, new, sems.at[2]),
        pltpu.make_async_copy(lengths_hbm, lengths, sems.at[3]),
    ]
    groups = 4
    share = heads // groups
    for g in range(groups):
        at = pl.ds(g * share, share)
        fetches.append(pltpu.make_async_copy(up_hbm.at[at], up.at[at], sems.at[4 + g]))
    for fetch in fetches:
        fetch.start()
    own_ref[:, :, key_width:] = jnp.zeros(own_ref.shape[:2] + (own_ref.shape[2] - key_width,), bf16)
    fetches[0].wait()
    cos, sin = rope_tables(positions, steps, key_width - width)
    fetches[1].wait()
    rope = q[:, :, nope:].astype(f32)
    rope = (rope * cos[:, None, :] + swap_halves(rope) * sin[:, None, :]).astype(bf16)
    for s in range(steps):
        for b in range(requests):
            own_ref[b, s * heads : (s + 1) * heads, width:key_width] = rope[s * requests + b]
    fetches[3].wait()
    line = lax.broadcasted_iota(jnp.int32, limits_ref.shape, 0)
    limits = jnp.zeros(limits_ref.shape, jnp.int32)
    for b in range(requests):
        limits = jnp.where(line == b, lengths[b] - row_ref[0], limits)
    limits_ref[...] = limits
    fetches[2].wait()
    rows = jnp.concatenate([new[t].astype(f32) for t in range(steps)], axis=0)
    tail = rows[:, width:]
    tail = tail * cos + swap_halves(tail) * sin
    keys_ref[...] = jnp.concatenate([rows[:, :width], tail], axis=-1).astype(bf16)
    q_f32 = q[:, :, :nope].astype(f32)
    for h in range(heads):
        if h % share == 0:
            fetches[4 + h // share].wait()
        lat[:, h, :] = jnp.dot(q_f32[:, h, :].astype(bf16), up[h], preferred_element_type=f32)
    for s in range(steps):
        for b in range(requests):
            own_ref[b, s * heads : (s + 1) * heads, :width] = lat[s * requests + b].astype(bf16)
    sent_ref[...] = own_ref[pl.ds(info_ref[0], sent_ref.shape[0])]


def split_stats(peak, weight_sum, rows):
    lane = lax.broadcasted_iota(jnp.int32, (rows, 128), 1)
    first = peak.astype(bf16).astype(f32)
    rest = peak - first
    second = rest.astype(bf16).astype(f32)
    third = rest - second
    sum_first = weight_sum.astype(bf16).astype(f32)
    sum_second = weight_sum - sum_first
    out = jnp.where(lane == 0, first, 0.0)
    out = jnp.where(lane == 1, second, out)
    out = jnp.where(lane == 2, third, out)
    out = jnp.where(lane == 3, sum_first, out)
    return jnp.where(lane == 4, sum_second, out)


def stage_kernel(info_ref, cache_hbm, out_ref, sems):
    copies = []
    for i in range(out_ref.shape[0]):
        copies.append(pltpu.make_async_copy(cache_hbm.at[info_ref[0] + i], out_ref.at[i], sems.at[i]))
    for copy in copies:
        copy.start()
    for copy in copies:
        copy.wait()


def attention_kernel(scale, info_ref, limits_ref, own_ref, q1_ref, q2_ref, q3_ref, k_ref, out_ref, q_ref, *scores):
    count, owners, share, _ = q_ref.shape
    rows = owners * share
    key_width, cached = k_ref.shape[1:]
    width = out_ref.shape[2] - 128
    chunk = 1024
    first = info_ref[0]
    base = first if k_ref.shape[0] > count else 0
    q_ref[:, 0] = own_ref[pl.ds(first, count)]
    q_ref[:, 1] = q1_ref[...]
    q_ref[:, 2] = q2_ref[...]
    q_ref[:, 3] = q3_ref[...]

    tops = []
    for i in range(count):
        limit = limits_ref[pl.ds(first + i, 1), :1]
        queries = q_ref[i].reshape(rows, -1)[:, :key_width]
        top = jnp.full((rows, 128), lowest_max, f32)
        for c in range(0, cached, chunk):
            keys = k_ref[base + i, :, c : c + chunk]
            part = jnp.dot(queries, keys, preferred_element_type=f32) * scale
            column = lax.broadcasted_iota(jnp.int32, (1, chunk), 1) + c
            part = jnp.where(column < limit, part, masked_score)
            scores[i][:, c : c + chunk] = part
            for at in range(0, chunk, 128):
                top = jnp.maximum(top, part[:, at : at + 128])
        tops.append(jnp.max(top, axis=1, keepdims=True))

    for i in range(count):
        total = jnp.zeros((rows, 128), f32)
        for c in range(0, cached, chunk):
            weights = jnp.exp2(scores[i][:, c : c + chunk] - tops[i])
            for at in range(0, chunk, 128):
                total = total + weights[:, at : at + 128]
            part = lax.dot_general(
                weights.astype(bf16),
                k_ref[base + i, :width, c : c + chunk],
                (((1,), (1,)), ((), ())),
                preferred_element_type=f32,
            )
            mixed = part if c == 0 else mixed + part
        total = jnp.sum(total, axis=1, keepdims=True)
        at = slice(i * share, (i + 1) * share)
        out_ref[:, at, :width] = mixed.astype(bf16).reshape(owners, share, width)
        out_ref[:, at, width:] = split_stats(tops[i], total, rows).astype(bf16).reshape(owners, share, 128)


def fresh_kernel(scale, steps, heads, info_ref, place_ref, own_ref, new_ref, out_ref):
    requests, share, _ = own_ref.shape
    key_width = new_ref.shape[1]
    width = out_ref.shape[1] - 128
    fresh = new_ref[...]
    shape = (share, fresh.shape[0])
    key = lax.broadcasted_iota(jnp.int32, shape, 1)
    step = (lax.broadcasted_iota(jnp.int32, shape, 0) // heads) % steps
    counted = place_ref[0] == 0
    for i in range(out_ref.shape[0] // share):
        request = info_ref[0] + i
        scores = (
            lax.dot_general(
                own_ref[request][:, :key_width], fresh, (((1,), (1,)), ((), ())), preferred_element_type=f32
            )
            * scale
        )
        visible = (key % requests == request) & (key // requests <= step) & counted
        scores = jnp.where(visible, scores, masked_score)
        top = jnp.maximum(jnp.max(scores, axis=1, keepdims=True), lowest_max)
        weights = jnp.exp2(scores - top)
        total = jnp.sum(weights, axis=1, keepdims=True)
        mixed = jnp.dot(weights.astype(bf16), fresh[:, :width], preferred_element_type=f32)
        at = slice(i * share, (i + 1) * share)
        out_ref[at, :width] = mixed.astype(bf16)
        out_ref[at, width:] = split_stats(top, total, share).astype(bf16)


def merge_parts(parts, width):
    tops = []
    sums = []
    for part in parts:
        stat = part[:, width:].astype(f32)
        tops.append(stat[:, 0:1] + stat[:, 1:2] + stat[:, 2:3])
        sums.append(stat[:, 3:4] + stat[:, 4:5])
    peak = functools.reduce(jnp.maximum, tops)
    weights = [jnp.exp2(t - peak) for t in tops]
    weight_sum = sum(w * s for w, s in zip(weights, sums))
    merged = sum(w * part[:, :width].astype(f32) for w, part in zip(weights, parts))
    return merged, peak, weight_sum


def pair_kernel(a_ref, b_ref, *sent_refs):
    rows = sent_refs[0].shape[0]
    width = a_ref.shape[2] - 128
    for owner, sent_ref in enumerate(sent_refs):
        merged, peak, weight_sum = merge_parts((a_ref[owner], b_ref[owner]), width)
        sent_ref[:, :width] = merged.astype(bf16)
        sent_ref[:, width:] = split_stats(peak, weight_sum, rows).astype(bf16)


def project_kernel(heads, *refs):
    *parts, up_ref, out_ref, mixed, projected = refs
    rows = parts[0].shape[0]
    merged, peak, weight_sum = merge_parts([part[...] for part in parts], up_ref.shape[1])
    mixed[...] = merged.reshape(mixed.shape)
    stats = split_stats(peak, weight_sum, rows).T[:16].astype(bf16)
    count = rows // heads
    for h in range(heads):
        part = mixed[:, h, :]
        high = part.astype(bf16)
        low = (part - high.astype(f32)).astype(bf16)
        both = jnp.dot(jnp.concatenate([high, low], axis=0), up_ref[h], preferred_element_type=f32)
        projected[:, h, :] = both[:count] + both[count:]
    values = projected[...].reshape(rows, projected.shape[2]).astype(bf16)
    out_ref[:rows, :] = values
    out_ref[rows:, :] = stats


def merge_rows(parts, rows):
    tops = []
    sums = []
    for part in parts:
        stat = part[rows:, :].astype(f32)
        tops.append(stat[0:1] + stat[1:2] + stat[2:3])
        sums.append(stat[3:4] + stat[4:5])
    tops = jnp.concatenate(tops, axis=0)
    peak = jnp.max(tops, axis=0, keepdims=True)
    weights = jnp.exp2(tops - peak)
    weight_sum = jnp.sum(weights * jnp.concatenate(sums, axis=0), axis=0, keepdims=True)
    return weights, peak, weight_sum


def weigh(parts, weights, rows):
    spread = jnp.concatenate([weights, jnp.zeros((128 - len(parts), weights.shape[1]), f32)], axis=0).T
    return sum(part[:rows, :].astype(f32) * spread[:rows, i : i + 1] for i, part in enumerate(parts))


def middle_kernel(*refs):
    *parts, out_ref = refs
    parts = [part[...] for part in parts]
    rows = out_ref.shape[0] - 16
    weights, peak, weight_sum = merge_rows(parts, rows)
    out_ref[:rows, :] = weigh(parts, weights, rows).astype(bf16)
    line = lax.broadcasted_iota(jnp.int32, (16, weights.shape[1]), 0)
    first = peak.astype(bf16).astype(f32)
    second = (peak - first).astype(bf16).astype(f32)
    sum_first = weight_sum.astype(bf16).astype(f32)
    stats = jnp.where(line == 0, first, 0.0)
    stats = jnp.where(line == 1, second, stats)
    stats = jnp.where(line == 2, peak - first - second, stats)
    stats = jnp.where(line == 3, sum_first, stats)
    out_ref[rows:, :] = jnp.where(line == 4, weight_sum - sum_first, stats).astype(bf16)


def finish_kernel(*refs):
    *parts, out_ref = refs
    parts = [part[...] for part in parts]
    steps, half = out_ref.shape[:2]
    rows = steps * half * out_ref.shape[2]
    weights, _, weight_sum = merge_rows(parts, rows)
    result = weigh(parts, weights / weight_sum, rows)
    result = result.astype(bf16).reshape(half, steps, *out_ref.shape[2:])
    for b in range(half):
        out_ref[:, b] = result[b]


def place_kernel(info_ref, own_ref, other_ref, out_ref):
    half = own_ref.shape[1]
    first = info_ref[0]
    out_ref[:, pl.ds(first, half)] = own_ref[...]
    out_ref[:, pl.ds(half - first, half)] = other_ref[...]


def on_device(
    query_heads, up_keys, up_values, latent_cache, new_latent, context_lengths, positions
):
    steps, requests, heads, query_width = query_heads.shape
    nope = up_keys.shape[1]
    width = up_keys.shape[2]
    key_width = latent_cache.shape[2]
    rope = key_width - width
    value_width = up_values.shape[2]
    cached = latent_cache.shape[1]
    owners = lax.axis_size("head")
    plane = lax.axis_size("z") * lax.axis_size("x")
    pairs = steps * requests
    half = requests // 2
    scale = float(query_width) ** (-0.5) * log2_e

    core = lax.axis_index("core")
    slot = lax.axis_index(("z", "x", "core", "head"))

    vmem = pl.BlockSpec(memory_space=pltpu.VMEM)
    smem = pl.BlockSpec(memory_space=pltpu.SMEM)
    small = pltpu.CompilerParams(vmem_limit_bytes=12 * 2**20)
    anywhere = pl.BlockSpec(memory_space=pltpu.HBM)
    wide = 640
    in_hbm = functools.partial(pltpu.with_memory_space_constraint, memory_space=pltpu.HBM)
    core32 = core.astype(jnp.int32)
    own_first = (core32 * half).reshape(1)
    other_first = (half - core32 * half).reshape(1)
    first_row = (slot.astype(jnp.int32) * cached).reshape(1)
    place = lax.axis_index(("z", "x")).astype(jnp.int32).reshape(1)
    chunk = half * steps * heads
    own_queries, sent_queries, new_keys, limits = pl.pallas_call(
        functools.partial(queries_kernel, steps),
        in_specs=[smem] * 2 + [anywhere] * 5,
        out_specs=[vmem] * 4,
        out_shape=(
            jax.ShapeDtypeStruct((requests, steps * heads, wide), bf16),
            jax.ShapeDtypeStruct((half, steps * heads, wide), bf16),
            jax.ShapeDtypeStruct((pairs, key_width), bf16),
            jax.ShapeDtypeStruct((8, 128), jnp.int32),
        ),
        scratch_shapes=[
            pltpu.SMEM((requests,), jnp.int32),
            pltpu.SMEM((requests,), jnp.int32),
            pltpu.VMEM((pairs, heads, query_width), bf16),
            pltpu.VMEM(up_keys.shape, bf16),
            pltpu.VMEM(new_latent.shape, bf16),
            pltpu.VMEM((pairs, heads, width), f32),
            pltpu.SemaphoreType.DMA((8,)),
        ],
        compiler_params=pltpu.CompilerParams(vmem_limit_bytes=24 * 2**20),
        name="queries",
    )(
        other_first,
        first_row,
        in_hbm(positions),
        in_hbm(context_lengths),
        in_hbm(query_heads.reshape(pairs, heads, query_width)),
        in_hbm(up_keys),
        in_hbm(new_latent),
    )

    def over_head(array, k):
        return lax.ppermute(array, "head", [(i, i ^ k) for i in range(owners)])

    swap = [(0, 1), (1, 0)]
    partners = (1, 3, 2)
    got = [over_head(sent_queries, k) for k in partners]
    fresh = pl.pallas_call(
        functools.partial(fresh_kernel, scale, steps, heads),
        in_specs=[smem, smem, vmem, vmem],
        out_specs=vmem,
        out_shape=jax.ShapeDtypeStruct((chunk, width + 128), bf16),
        compiler_params=small,
        cost_estimate=pl.CostEstimate(flops=10**9, bytes_accessed=4 * 10**6, transcendentals=0),
        name="fresh",
    )(own_first, place, own_queries, new_keys)
    cache = jnp.swapaxes(latent_cache, 1, 2)
    staged_shape = pltpu.VMEM((half, key_width, cached), bf16)
    in_vmem = functools.partial(pltpu.with_memory_space_constraint, memory_space=pltpu.VMEM)
    staged = pl.pallas_call(
        stage_kernel,
        in_specs=[smem, anywhere],
        out_specs=vmem,
        out_shape=staged_shape,
        scratch_shapes=[pltpu.SemaphoreType.DMA((half,))],
        compiler_params=small,
        cost_estimate=pl.CostEstimate(flops=0, bytes_accessed=2 * half * key_width * cached, transcendentals=0),
        name="stage",
    )(other_first, in_hbm(cache))
    got[2], staged = lax.optimization_barrier((got[2], staged))
    passed = [lax.ppermute(g, "core", swap) for g in got]
    got, passed = lax.optimization_barrier((got, passed))

    rows = owners * steps * heads

    def attend(first, got, keys):
        return pl.pallas_call(
            functools.partial(attention_kernel, scale),
            in_specs=[smem] + [vmem] * 6,
            out_specs=vmem,
            scratch_shapes=[pltpu.VMEM((half, owners, steps * heads, wide), bf16)]
            + [pltpu.VMEM((rows, cached), f32)] * half,
            out_shape=jax.ShapeDtypeStruct((owners, chunk, width + 128), bf16),
            compiler_params=pltpu.CompilerParams(vmem_limit_bytes=18 * 2**20),
            cost_estimate=pl.CostEstimate(
                flops=2 * half * rows * cached * (key_width + width),
                bytes_accessed=half * cached * key_width * 2,
                transcendentals=half * rows * cached,
            ),
            name="attention",
        )(first, limits, own_queries, *got, keys)

    other_part = lax.ppermute(attend(other_first, got, in_vmem(staged)), "core", swap)
    own_part = attend(own_first, passed, cache)
    sent = pl.pallas_call(
        pair_kernel,
        in_specs=[vmem] * 2,
        out_specs=[vmem] * owners,
        out_shape=[jax.ShapeDtypeStruct((chunk, width + 128), bf16)] * owners,
        compiler_params=small,
        name="pair_merge",
    )(other_part, own_part)
    arrived = [over_head(array, k) for array, k in zip(sent[1:], partners)]
    part = pl.pallas_call(
        functools.partial(project_kernel, heads),
        in_specs=[vmem] * 6,
        out_specs=vmem,
        out_shape=jax.ShapeDtypeStruct((chunk + 16, value_width), bf16),
        scratch_shapes=[
            pltpu.VMEM((chunk // heads, heads, width), f32),
            pltpu.VMEM((chunk // heads, heads, value_width), f32),
        ],
        compiler_params=small,
        name="project",
    )(sent[0], *arrived, fresh, up_values)

    def over_plane(array, k):
        return lax.ppermute(array, ("z", "x"), [(i, i ^ k) for i in range(plane)])

    part = pl.pallas_call(
        middle_kernel,
        in_specs=[vmem] * 4,
        out_specs=vmem,
        out_shape=jax.ShapeDtypeStruct(part.shape, bf16),
        compiler_params=small,
        name="middle_merge",
    )(part, *[over_plane(part, k) for k in (5, 4, 1)])
    own = pl.pallas_call(
        finish_kernel,
        in_specs=[vmem] * 4,
        out_specs=vmem,
        out_shape=jax.ShapeDtypeStruct((steps, half, heads, value_width), bf16),
        compiler_params=small,
        name="finish",
    )(part, *[over_plane(part, k) for k in (15, 12, 3)])
    theirs = lax.ppermute(own, "core", swap)
    return pl.pallas_call(
        place_kernel,
        in_specs=[smem, vmem, vmem],
        out_specs=vmem,
        out_shape=jax.ShapeDtypeStruct((steps, requests, heads, value_width), bf16),
        compiler_params=small,
        name="place",
    )(own_first, own, theirs)


def solution(mesh):
    fine = Mesh(mesh.devices.reshape(4, 4, 2, 4), ("z", "x", "core", "head"))
    in_specs = (
        P(None, None, "head", None),
        P("head", None, None),
        P("head", None, None),
        P(None, ("z", "x", "core", "head"), None),
        P(),
        P(),
        P(),
    )
    out_specs = P(None, None, "head", None)
    return jax.shard_map(
        on_device, mesh=fine, in_specs=in_specs, out_specs=out_specs, check_vma=False
    )
```

```python
import functools

import jax
import jax.numpy as jnp
from jax import lax
from jax.experimental import pallas as pl
from jax.experimental.pallas import tpu as pltpu
from jax.sharding import Mesh, PartitionSpec as P

rope_base = 50000.0
masked_score = -1e30
lowest_max = -1e29
log2_e = 1.4426950408889634
bf16 = jnp.bfloat16
f32 = jnp.float32


def swap_halves(values):
    half = values.shape[-1] // 2
    return jnp.concatenate([values[..., half:], values[..., :half]], axis=-1)


def rope_tables(positions_ref, steps, width):
    requests = positions_ref.shape[0]
    pairs = steps * requests
    half = width // 2
    row = lax.broadcasted_iota(jnp.int32, (pairs, width), 0)
    lane = lax.broadcasted_iota(jnp.int32, (pairs, width), 1)
    where_at = row // requests
    for b in range(requests):
        where_at += jnp.where(row % requests == b, positions_ref[b], 0)
    counter = lax.broadcasted_iota(jnp.int32, (1, width), 1) % half
    inverse = jnp.zeros((1, width), f32)
    for i in range(half):
        inverse = jnp.where(counter == i, f32(rope_base ** (-2.0 * i / width)), inverse)
    angles = where_at.astype(f32) * inverse
    return jnp.cos(angles), jnp.where(lane < half, -1.0, 1.0) * jnp.sin(angles)


def queries_kernel(
    steps,
    info_ref,
    row_ref,
    positions_hbm,
    lengths_hbm,
    q_hbm,
    up_hbm,
    new_hbm,
    own_ref,
    sent_ref,
    keys_ref,
    limits_ref,
    positions,
    lengths,
    q,
    up,
    new,
    lat,
    sems,
):
    pairs, heads, _ = q.shape
    requests = pairs // steps
    nope, width = up.shape[1], up.shape[2]
    key_width = new.shape[2]
    fetches = [
        pltpu.make_async_copy(positions_hbm, positions, sems.at[0]),
        pltpu.make_async_copy(q_hbm, q, sems.at[1]),
        pltpu.make_async_copy(new_hbm, new, sems.at[2]),
        pltpu.make_async_copy(lengths_hbm, lengths, sems.at[3]),
    ]
    groups = 4
    share = heads // groups
    for g in range(groups):
        at = pl.ds(g * share, share)
        fetches.append(pltpu.make_async_copy(up_hbm.at[at], up.at[at], sems.at[4 + g]))
    for fetch in fetches:
        fetch.start()
    own_ref[:, :, key_width:] = jnp.zeros(own_ref.shape[:2] + (own_ref.shape[2] - key_width,), bf16)
    fetches[0].wait()
    cos, sin = rope_tables(positions, steps, key_width - width)
    fetches[1].wait()
    rope = q[:, :, nope:].astype(f32)
    rope = (rope * cos[:, None, :] + swap_halves(rope) * sin[:, None, :]).astype(bf16)
    for s in range(steps):
        for b in range(requests):
            own_ref[b, s * heads : (s + 1) * heads, width:key_width] = rope[s * requests + b]
    fetches[3].wait()
    line = lax.broadcasted_iota(jnp.int32, limits_ref.shape, 0)
    limits = jnp.zeros(limits_ref.shape, jnp.int32)
    for b in range(requests):
        limits = jnp.where(line == b, lengths[b] - row_ref[0], limits)
    limits_ref[...] = limits
    fetches[2].wait()
    rows = jnp.concatenate([new[t].astype(f32) for t in range(steps)], axis=0)
    tail = rows[:, width:]
    tail = tail * cos + swap_halves(tail) * sin
    keys_ref[...] = jnp.concatenate([rows[:, :width], tail], axis=-1).astype(bf16)
    q_f32 = q[:, :, :nope].astype(f32)
    for h in range(heads):
        if h % share == 0:
            fetches[4 + h // share].wait()
        lat[:, h, :] = jnp.dot(q_f32[:, h, :].astype(bf16), up[h], preferred_element_type=f32)
    for s in range(steps):
        for b in range(requests):
            own_ref[b, s * heads : (s + 1) * heads, :width] = lat[s * requests + b].astype(bf16)
    sent_ref[...] = own_ref[pl.ds(info_ref[0], sent_ref.shape[0])]


def split_stats(peak, weight_sum, rows):
    lane = lax.broadcasted_iota(jnp.int32, (rows, 128), 1)
    first = peak.astype(bf16).astype(f32)
    rest = peak - first
    second = rest.astype(bf16).astype(f32)
    third = rest - second
    sum_first = weight_sum.astype(bf16).astype(f32)
    sum_second = weight_sum - sum_first
    out = jnp.where(lane == 0, first, 0.0)
    out = jnp.where(lane == 1, second, out)
    out = jnp.where(lane == 2, third, out)
    out = jnp.where(lane == 3, sum_first, out)
    return jnp.where(lane == 4, sum_second, out)


def stage_kernel(info_ref, cache_hbm, out_ref, sems):
    copies = []
    for i in range(out_ref.shape[0]):
        copies.append(pltpu.make_async_copy(cache_hbm.at[info_ref[0] + i], out_ref.at[i], sems.at[i]))
    for copy in copies:
        copy.start()
    for copy in copies:
        copy.wait()


def attention_kernel(
    scale, info_ref, core_ref, limits_ref, own_ref, near_ref, passed_ref, far_ref, k_ref, out_ref, q_ref, *scores
):
    count, owners, share, _ = q_ref.shape
    rows = owners * share
    key_width, cached = k_ref.shape[1:]
    width = out_ref.shape[2] - 128
    chunk = 1024
    first = info_ref[0]
    base = first if k_ref.shape[0] > count else 0
    q_ref[:, 0] = own_ref[pl.ds(first, count)]
    q_ref[:, pl.ds(1 + core_ref[0], 1)] = near_ref[pl.ds(first, count)][:, None]
    q_ref[:, pl.ds(2 - core_ref[0], 1)] = passed_ref[pl.ds(first, count)][:, None]
    q_ref[:, 3] = far_ref[...]

    tops = []
    for i in range(count):
        limit = limits_ref[pl.ds(first + i, 1), :1]
        queries = q_ref[i].reshape(rows, -1)[:, :key_width]
        top = jnp.full((rows, 128), lowest_max, f32)
        for c in range(0, cached, chunk):
            keys = k_ref[base + i, :, c : c + chunk]
            part = jnp.dot(queries, keys, preferred_element_type=f32) * scale
            column = lax.broadcasted_iota(jnp.int32, (1, chunk), 1) + c
            part = jnp.where(column < limit, part, masked_score)
            scores[i][:, c : c + chunk] = part
            for at in range(0, chunk, 128):
                top = jnp.maximum(top, part[:, at : at + 128])
        tops.append(jnp.max(top, axis=1, keepdims=True))

    for i in range(count):
        total = jnp.zeros((rows, 128), f32)
        for c in range(0, cached, chunk):
            weights = jnp.exp2(scores[i][:, c : c + chunk] - tops[i])
            for at in range(0, chunk, 128):
                total = total + weights[:, at : at + 128]
            part = lax.dot_general(
                weights.astype(bf16),
                k_ref[base + i, :width, c : c + chunk],
                (((1,), (1,)), ((), ())),
                preferred_element_type=f32,
            )
            mixed = part if c == 0 else mixed + part
        total = jnp.sum(total, axis=1, keepdims=True)
        at = slice(i * share, (i + 1) * share)
        out_ref[:, at, :width] = mixed.astype(bf16).reshape(owners, share, width)
        out_ref[:, at, width:] = split_stats(tops[i], total, rows).astype(bf16).reshape(owners, share, 128)


def fresh_kernel(scale, steps, heads, info_ref, place_ref, own_ref, new_ref, out_ref):
    requests, share, _ = own_ref.shape
    key_width = new_ref.shape[1]
    width = out_ref.shape[1] - 128
    fresh = new_ref[...]
    shape = (share, fresh.shape[0])
    key = lax.broadcasted_iota(jnp.int32, shape, 1)
    step = (lax.broadcasted_iota(jnp.int32, shape, 0) // heads) % steps
    counted = place_ref[0] == 0
    for i in range(out_ref.shape[0] // share):
        request = info_ref[0] + i
        scores = (
            lax.dot_general(
                own_ref[request][:, :key_width], fresh, (((1,), (1,)), ((), ())), preferred_element_type=f32
            )
            * scale
        )
        visible = (key % requests == request) & (key // requests <= step) & counted
        scores = jnp.where(visible, scores, masked_score)
        top = jnp.maximum(jnp.max(scores, axis=1, keepdims=True), lowest_max)
        weights = jnp.exp2(scores - top)
        total = jnp.sum(weights, axis=1, keepdims=True)
        mixed = jnp.dot(weights.astype(bf16), fresh[:, :width], preferred_element_type=f32)
        at = slice(i * share, (i + 1) * share)
        out_ref[at, :width] = mixed.astype(bf16)
        out_ref[at, width:] = split_stats(top, total, share).astype(bf16)


def merge_parts(parts, width):
    tops = []
    sums = []
    for part in parts:
        stat = part[:, width:].astype(f32)
        tops.append(stat[:, 0:1] + stat[:, 1:2] + stat[:, 2:3])
        sums.append(stat[:, 3:4] + stat[:, 4:5])
    peak = functools.reduce(jnp.maximum, tops)
    weights = [jnp.exp2(t - peak) for t in tops]
    weight_sum = sum(w * s for w, s in zip(weights, sums))
    merged = sum(w * part[:, :width].astype(f32) for w, part in zip(weights, parts))
    return merged, peak, weight_sum


def pair_kernel(a_ref, b_ref, *sent_refs):
    rows = sent_refs[0].shape[0]
    width = a_ref.shape[2] - 128
    for owner, sent_ref in enumerate(sent_refs):
        merged, peak, weight_sum = merge_parts((a_ref[owner], b_ref[owner]), width)
        sent_ref[:, :width] = merged.astype(bf16)
        sent_ref[:, width:] = split_stats(peak, weight_sum, rows).astype(bf16)


def project_kernel(heads, *refs):
    *parts, up_ref, out_ref, mixed, projected = refs
    rows = parts[0].shape[0]
    merged, peak, weight_sum = merge_parts([part[...] for part in parts], up_ref.shape[1])
    mixed[...] = merged.reshape(mixed.shape)
    stats = split_stats(peak, weight_sum, rows).T[:16].astype(bf16)
    count = rows // heads
    for h in range(heads):
        part = mixed[:, h, :]
        high = part.astype(bf16)
        low = (part - high.astype(f32)).astype(bf16)
        both = jnp.dot(jnp.concatenate([high, low], axis=0), up_ref[h], preferred_element_type=f32)
        projected[:, h, :] = both[:count] + both[count:]
    values = projected[...].reshape(rows, projected.shape[2]).astype(bf16)
    out_ref[:rows, :] = values
    out_ref[rows:, :] = stats


def merge_rows(parts, rows):
    tops = []
    sums = []
    for part in parts:
        stat = part[rows:, :].astype(f32)
        tops.append(stat[0:1] + stat[1:2] + stat[2:3])
        sums.append(stat[3:4] + stat[4:5])
    tops = jnp.concatenate(tops, axis=0)
    peak = jnp.max(tops, axis=0, keepdims=True)
    weights = jnp.exp2(tops - peak)
    weight_sum = jnp.sum(weights * jnp.concatenate(sums, axis=0), axis=0, keepdims=True)
    return weights, peak, weight_sum


def weigh(parts, weights, rows):
    spread = jnp.concatenate([weights, jnp.zeros((128 - len(parts), weights.shape[1]), f32)], axis=0).T
    return sum(part[:rows, :].astype(f32) * spread[:rows, i : i + 1] for i, part in enumerate(parts))


def middle_kernel(*refs):
    *parts, out_ref = refs
    parts = [part[...] for part in parts]
    rows = out_ref.shape[0] - 16
    weights, peak, weight_sum = merge_rows(parts, rows)
    out_ref[:rows, :] = weigh(parts, weights, rows).astype(bf16)
    line = lax.broadcasted_iota(jnp.int32, (16, weights.shape[1]), 0)
    first = peak.astype(bf16).astype(f32)
    second = (peak - first).astype(bf16).astype(f32)
    sum_first = weight_sum.astype(bf16).astype(f32)
    stats = jnp.where(line == 0, first, 0.0)
    stats = jnp.where(line == 1, second, stats)
    stats = jnp.where(line == 2, peak - first - second, stats)
    stats = jnp.where(line == 3, sum_first, stats)
    out_ref[rows:, :] = jnp.where(line == 4, weight_sum - sum_first, stats).astype(bf16)


def finish_kernel(*refs):
    *parts, out_ref = refs
    parts = [part[...] for part in parts]
    steps, half = out_ref.shape[:2]
    rows = steps * half * out_ref.shape[2]
    weights, _, weight_sum = merge_rows(parts, rows)
    result = weigh(parts, weights / weight_sum, rows)
    result = result.astype(bf16).reshape(half, steps, *out_ref.shape[2:])
    for b in range(half):
        out_ref[:, b] = result[b]


def place_kernel(info_ref, own_ref, other_ref, out_ref):
    half = own_ref.shape[1]
    first = info_ref[0]
    out_ref[:, pl.ds(first, half)] = own_ref[...]
    out_ref[:, pl.ds(half - first, half)] = other_ref[...]


def on_device(
    query_heads, up_keys, up_values, latent_cache, new_latent, context_lengths, positions
):
    steps, requests, heads, query_width = query_heads.shape
    nope = up_keys.shape[1]
    width = up_keys.shape[2]
    key_width = latent_cache.shape[2]
    rope = key_width - width
    value_width = up_values.shape[2]
    cached = latent_cache.shape[1]
    owners = lax.axis_size("head")
    plane = lax.axis_size("z") * lax.axis_size("x")
    pairs = steps * requests
    half = requests // 2
    scale = float(query_width) ** (-0.5) * log2_e

    core = lax.axis_index("core")
    slot = lax.axis_index(("z", "x", "core", "head"))

    vmem = pl.BlockSpec(memory_space=pltpu.VMEM)
    smem = pl.BlockSpec(memory_space=pltpu.SMEM)
    small = pltpu.CompilerParams(vmem_limit_bytes=12 * 2**20)
    anywhere = pl.BlockSpec(memory_space=pltpu.HBM)
    wide = 640
    in_hbm = functools.partial(pltpu.with_memory_space_constraint, memory_space=pltpu.HBM)
    core32 = core.astype(jnp.int32)
    own_first = (core32 * half).reshape(1)
    other_first = (half - core32 * half).reshape(1)
    first_row = (slot.astype(jnp.int32) * cached).reshape(1)
    place = lax.axis_index(("z", "x")).astype(jnp.int32).reshape(1)
    chunk = half * steps * heads
    own_queries, sent_queries, new_keys, limits = pl.pallas_call(
        functools.partial(queries_kernel, steps),
        in_specs=[smem] * 2 + [anywhere] * 5,
        out_specs=[vmem] * 4,
        out_shape=(
            jax.ShapeDtypeStruct((requests, steps * heads, wide), bf16),
            jax.ShapeDtypeStruct((half, steps * heads, wide), bf16),
            jax.ShapeDtypeStruct((pairs, key_width), bf16),
            jax.ShapeDtypeStruct((8, 128), jnp.int32),
        ),
        scratch_shapes=[
            pltpu.SMEM((requests,), jnp.int32),
            pltpu.SMEM((requests,), jnp.int32),
            pltpu.VMEM((pairs, heads, query_width), bf16),
            pltpu.VMEM(up_keys.shape, bf16),
            pltpu.VMEM(new_latent.shape, bf16),
            pltpu.VMEM((pairs, heads, width), f32),
            pltpu.SemaphoreType.DMA((8,)),
        ],
        compiler_params=pltpu.CompilerParams(vmem_limit_bytes=24 * 2**20),
        name="queries",
    )(
        other_first,
        first_row,
        in_hbm(positions),
        in_hbm(context_lengths),
        in_hbm(query_heads.reshape(pairs, heads, query_width)),
        in_hbm(up_keys),
        in_hbm(new_latent),
    )

    def over_head(array, k):
        return lax.ppermute(array, "head", [(i, i ^ k) for i in range(owners)])

    swap = [(0, 1), (1, 0)]
    partners = (1, 3, 2)
    far = over_head(sent_queries, 2)
    beside = [(c * owners + i, c * owners + (i ^ (1 + 2 * c))) for c in range(2) for i in range(owners)]
    near = lax.ppermute(own_queries, ("core", "head"), beside)
    fresh = pl.pallas_call(
        functools.partial(fresh_kernel, scale, steps, heads),
        in_specs=[smem, smem, vmem, vmem],
        out_specs=vmem,
        out_shape=jax.ShapeDtypeStruct((chunk, width + 128), bf16),
        compiler_params=small,
        cost_estimate=pl.CostEstimate(flops=10**9, bytes_accessed=4 * 10**6, transcendentals=0),
        name="fresh",
    )(own_first, place, own_queries, new_keys)
    cache = jnp.swapaxes(latent_cache, 1, 2)
    staged_shape = pltpu.VMEM((half, key_width, cached), bf16)
    in_vmem = functools.partial(pltpu.with_memory_space_constraint, memory_space=pltpu.VMEM)
    staged = pl.pallas_call(
        stage_kernel,
        in_specs=[smem, anywhere],
        out_specs=vmem,
        out_shape=staged_shape,
        scratch_shapes=[pltpu.SemaphoreType.DMA((half,))],
        compiler_params=small,
        cost_estimate=pl.CostEstimate(flops=0, bytes_accessed=2 * half * key_width * cached, transcendentals=0),
        name="stage",
    )(other_first, in_hbm(cache))
    near, far, staged = lax.optimization_barrier((near, far, staged))
    near_passed = lax.ppermute(near, "core", swap)
    far_passed = lax.ppermute(far, "core", swap)
    near_passed, far_passed = lax.optimization_barrier((near_passed, far_passed))
    rows = owners * steps * heads

    def attend(first, far, keys):
        return pl.pallas_call(
            functools.partial(attention_kernel, scale),
            in_specs=[smem] * 2 + [vmem] * 6,
            out_specs=vmem,
            scratch_shapes=[pltpu.VMEM((half, owners, steps * heads, wide), bf16)]
            + [pltpu.VMEM((rows, cached), f32)] * half,
            out_shape=jax.ShapeDtypeStruct((owners, chunk, width + 128), bf16),
            compiler_params=pltpu.CompilerParams(vmem_limit_bytes=18 * 2**20),
            cost_estimate=pl.CostEstimate(
                flops=2 * half * rows * cached * (key_width + width),
                bytes_accessed=half * cached * key_width * 2,
                transcendentals=half * rows * cached,
            ),
            name="attention",
        )(first, core32.reshape(1), limits, own_queries, near, near_passed, far, keys)

    other_part = lax.ppermute(attend(other_first, far, in_vmem(staged)), "core", swap)
    own_part = attend(own_first, far_passed, cache)
    sent = pl.pallas_call(
        pair_kernel,
        in_specs=[vmem] * 2,
        out_specs=[vmem] * owners,
        out_shape=[pltpu.VMEM((chunk, width + 128), bf16)] * owners,
        compiler_params=small,
        name="pair_merge",
    )(other_part, own_part)
    arrived = [over_head(array, k) for array, k in zip(sent[1:], partners)]
    part = pl.pallas_call(
        functools.partial(project_kernel, heads),
        in_specs=[vmem] * 6,
        out_specs=vmem,
        out_shape=jax.ShapeDtypeStruct((chunk + 16, value_width), bf16),
        scratch_shapes=[
            pltpu.VMEM((chunk // heads, heads, width), f32),
            pltpu.VMEM((chunk // heads, heads, value_width), f32),
        ],
        compiler_params=small,
        name="project",
    )(sent[0], *arrived, fresh, up_values)

    def over_plane(array, k):
        return lax.ppermute(array, ("z", "x"), [(i, i ^ k) for i in range(plane)])

    part = pl.pallas_call(
        middle_kernel,
        in_specs=[vmem] * 4,
        out_specs=vmem,
        out_shape=jax.ShapeDtypeStruct(part.shape, bf16),
        compiler_params=small,
        name="middle_merge",
    )(part, *[over_plane(part, k) for k in (1, 3, 2)])
    own = pl.pallas_call(
        finish_kernel,
        in_specs=[vmem] * 4,
        out_specs=vmem,
        out_shape=jax.ShapeDtypeStruct((steps, half, heads, value_width), bf16),
        compiler_params=small,
        name="finish",
    )(part, *[over_plane(part, k) for k in (4, 12, 8)])
    theirs = lax.ppermute(own, "core", swap)
    return pl.pallas_call(
        place_kernel,
        in_specs=[smem, vmem, vmem],
        out_specs=vmem,
        out_shape=jax.ShapeDtypeStruct((steps, requests, heads, value_width), bf16),
        compiler_params=small,
        name="place",
    )(own_first, own, theirs)


def solution(mesh):
    fine = Mesh(mesh.devices.reshape(4, 4, 2, 4), ("z", "x", "core", "head"))
    in_specs = (
        P(None, None, "head", None),
        P("head", None, None),
        P("head", None, None),
        P(None, ("z", "x", "core", "head"), None),
        P(),
        P(),
        P(),
    )
    out_specs = P(None, None, "head", None)
    return jax.shard_map(
        on_device, mesh=fine, in_specs=in_specs, out_specs=out_specs, check_vma=False
    )
```

```python
import functools

import jax
import jax.numpy as jnp
from jax import lax
from jax.experimental import pallas as pl
from jax.experimental.pallas import tpu as pltpu
from jax.sharding import Mesh, PartitionSpec as P

rope_base = 50000.0
masked_score = -1e30
lowest_max = -1e29
log2_e = 1.4426950408889634
bf16 = jnp.bfloat16
f32 = jnp.float32


def swap_halves(values):
    half = values.shape[-1] // 2
    return jnp.concatenate([values[..., half:], values[..., :half]], axis=-1)


def rope_tables(positions_ref, steps, width):
    requests = positions_ref.shape[0]
    pairs = steps * requests
    half = width // 2
    row = lax.broadcasted_iota(jnp.int32, (pairs, width), 0)
    lane = lax.broadcasted_iota(jnp.int32, (pairs, width), 1)
    where_at = row // requests
    for b in range(requests):
        where_at += jnp.where(row % requests == b, positions_ref[b], 0)
    counter = lax.broadcasted_iota(jnp.int32, (1, width), 1) % half
    inverse = jnp.zeros((1, width), f32)
    for i in range(half):
        inverse = jnp.where(counter == i, f32(rope_base ** (-2.0 * i / width)), inverse)
    angles = where_at.astype(f32) * inverse
    return jnp.cos(angles), jnp.where(lane < half, -1.0, 1.0) * jnp.sin(angles)


def queries_kernel(
    steps,
    info_ref,
    own_first_ref,
    row_ref,
    place_ref,
    positions_hbm,
    lengths_hbm,
    q_hbm,
    up_hbm,
    new_hbm,
    own_ref,
    sent_ref,
    keys_ref,
    limits_ref,
    positions,
    lengths,
    q,
    up,
    new,
    lat,
    sems,
):
    pairs, heads, _ = q.shape
    requests = pairs // steps
    nope, width = up.shape[1], up.shape[2]
    key_width = new.shape[2]
    fetches = [
        pltpu.make_async_copy(positions_hbm, positions, sems.at[0]),
        pltpu.make_async_copy(q_hbm, q, sems.at[1]),
        pltpu.make_async_copy(new_hbm, new, sems.at[2]),
        pltpu.make_async_copy(lengths_hbm, lengths, sems.at[3]),
    ]
    groups = 4
    share = heads // groups
    for g in range(groups):
        at = pl.ds(g * share, share)
        fetches.append(pltpu.make_async_copy(up_hbm.at[at], up.at[at], sems.at[4 + g]))
    for fetch in fetches:
        fetch.start()
    own_ref[:, :, key_width:] = jnp.zeros(own_ref.shape[:2] + (own_ref.shape[2] - key_width,), bf16)
    fetches[0].wait()
    cos, sin = rope_tables(positions, steps, key_width - width)
    fetches[1].wait()
    rope = q[:, :, nope:].astype(f32)
    rope = (rope * cos[:, None, :] + swap_halves(rope) * sin[:, None, :]).astype(bf16)
    for s in range(steps):
        for b in range(requests):
            own_ref[b, s * heads : (s + 1) * heads, width:key_width] = rope[s * requests + b]
    fetches[3].wait()
    line = lax.broadcasted_iota(jnp.int32, limits_ref.shape, 0)
    limits = jnp.zeros(limits_ref.shape, jnp.int32)
    for b in range(requests):
        limits = jnp.where(line == b, lengths[b] - row_ref[0], limits)
    limits_ref[...] = jnp.where(line == requests, place_ref[0], limits)
    fetches[2].wait()
    rows = jnp.concatenate([new[t].astype(f32) for t in range(steps)], axis=0)
    tail = rows[:, width:]
    tail = tail * cos + swap_halves(tail) * sin
    keys_ref[...] = jnp.concatenate([rows[:, :width], tail], axis=-1).astype(bf16)
    q_f32 = q[:, :, :nope].astype(f32)
    for h in range(heads):
        if h % share == 0:
            fetches[4 + h // share].wait()
        lat[:, h, :] = jnp.dot(q_f32[:, h, :].astype(bf16), up[h], preferred_element_type=f32)
    for s in range(steps):
        for b in range(requests):
            own_ref[b, s * heads : (s + 1) * heads, :width] = lat[s * requests + b].astype(bf16)
    sent_ref[...] = own_ref[pl.ds(info_ref[0], sent_ref.shape[0])]


def split_stats(peak, weight_sum, rows):
    lane = lax.broadcasted_iota(jnp.int32, (rows, 128), 1)
    first = peak.astype(bf16).astype(f32)
    rest = peak - first
    second = rest.astype(bf16).astype(f32)
    third = rest - second
    sum_first = weight_sum.astype(bf16).astype(f32)
    sum_second = weight_sum - sum_first
    out = jnp.where(lane == 0, first, 0.0)
    out = jnp.where(lane == 1, second, out)
    out = jnp.where(lane == 2, third, out)
    out = jnp.where(lane == 3, sum_first, out)
    return jnp.where(lane == 4, sum_second, out)


def stage_kernel(info_ref, cache_hbm, out_ref, sems):
    copies = []
    for i in range(out_ref.shape[0]):
        copies.append(pltpu.make_async_copy(cache_hbm.at[info_ref[0] + i], out_ref.at[i], sems.at[i]))
    for copy in copies:
        copy.start()
    for copy in copies:
        copy.wait()


def attention_kernel(scale, info_ref, limits_ref, own_ref, q1_ref, q2_ref, q3_ref, k_ref, out_ref, q_ref, *scores):
    count, owners, share, _ = q_ref.shape
    rows = owners * share
    key_width, cached = k_ref.shape[1:]
    width = out_ref.shape[2] - 128
    chunk = 1024
    first = info_ref[0]
    base = first if k_ref.shape[0] > count else 0
    q_ref[:, 0] = own_ref[pl.ds(first, count)]
    q_ref[:, 1] = q1_ref[...]
    q_ref[:, 2] = q2_ref[...]
    q_ref[:, 3] = q3_ref[...]

    tops = []
    for i in range(count):
        limit = limits_ref[pl.ds(first + i, 1), :1]
        queries = q_ref[i].reshape(rows, -1)[:, :key_width]
        top = jnp.full((rows, 128), lowest_max, f32)
        for c in range(0, cached, chunk):
            keys = k_ref[base + i, :, c : c + chunk]
            part = jnp.dot(queries, keys, preferred_element_type=f32) * scale
            column = lax.broadcasted_iota(jnp.int32, (1, chunk), 1) + c
            part = jnp.where(column < limit, part, masked_score)
            scores[i][:, c : c + chunk] = part
            for at in range(0, chunk, 128):
                top = jnp.maximum(top, part[:, at : at + 128])
        tops.append(jnp.max(top, axis=1, keepdims=True))

    for i in range(count):
        total = jnp.zeros((rows, 128), f32)
        for c in range(0, cached, chunk):
            weights = jnp.exp2(scores[i][:, c : c + chunk] - tops[i])
            for at in range(0, chunk, 128):
                total = total + weights[:, at : at + 128]
            part = lax.dot_general(
                weights.astype(bf16),
                k_ref[base + i, :width, c : c + chunk],
                (((1,), (1,)), ((), ())),
                preferred_element_type=f32,
            )
            mixed = part if c == 0 else mixed + part
        total = jnp.sum(total, axis=1, keepdims=True)
        at = slice(i * share, (i + 1) * share)
        out_ref[:, at, :width] = mixed.astype(bf16).reshape(owners, share, width)
        out_ref[:, at, width:] = split_stats(tops[i], total, rows).astype(bf16).reshape(owners, share, 128)


def fresh_kernel(scale, steps, heads, info_ref, limits_ref, own_ref, new_ref, out_ref):
    requests, share, _ = own_ref.shape
    key_width = new_ref.shape[1]
    width = out_ref.shape[1] - 128
    fresh = new_ref[...]
    shape = (share, fresh.shape[0])
    key = lax.broadcasted_iota(jnp.int32, shape, 1)
    step = (lax.broadcasted_iota(jnp.int32, shape, 0) // heads) % steps
    counted = limits_ref[requests : requests + 1, :1] == 0
    for i in range(out_ref.shape[0] // share):
        request = info_ref[0] + i
        scores = (
            lax.dot_general(
                own_ref[request][:, :key_width], fresh, (((1,), (1,)), ((), ())), preferred_element_type=f32
            )
            * scale
        )
        visible = (key % requests == request) & (key // requests <= step) & counted
        scores = jnp.where(visible, scores, masked_score)
        top = jnp.maximum(jnp.max(scores, axis=1, keepdims=True), lowest_max)
        weights = jnp.exp2(scores - top)
        total = jnp.sum(weights, axis=1, keepdims=True)
        mixed = jnp.dot(weights.astype(bf16), fresh[:, :width], preferred_element_type=f32)
        at = slice(i * share, (i + 1) * share)
        out_ref[at, :width] = mixed.astype(bf16)
        out_ref[at, width:] = split_stats(top, total, share).astype(bf16)


def merge_parts(parts, width):
    tops = []
    sums = []
    for part in parts:
        stat = part[:, width:].astype(f32)
        tops.append(stat[:, 0:1] + stat[:, 1:2] + stat[:, 2:3])
        sums.append(stat[:, 3:4] + stat[:, 4:5])
    peak = functools.reduce(jnp.maximum, tops)
    weights = [jnp.exp2(t - peak) for t in tops]
    weight_sum = sum(w * s for w, s in zip(weights, sums))
    merged = sum(w * part[:, :width].astype(f32) for w, part in zip(weights, parts))
    return merged, peak, weight_sum


def pair_kernel(a_ref, b_ref, *sent_refs):
    rows = sent_refs[0].shape[0]
    width = a_ref.shape[2] - 128
    for owner, sent_ref in enumerate(sent_refs):
        merged, peak, weight_sum = merge_parts((a_ref[owner], b_ref[owner]), width)
        sent_ref[:, :width] = merged.astype(bf16)
        sent_ref[:, width:] = split_stats(peak, weight_sum, rows).astype(bf16)


def project_kernel(heads, *refs):
    *parts, up_ref, out_ref, mixed, projected = refs
    rows = parts[0].shape[0]
    merged, peak, weight_sum = merge_parts([part[...] for part in parts], up_ref.shape[1])
    mixed[...] = merged.reshape(mixed.shape)
    stats = split_stats(peak, weight_sum, rows).T[:16].astype(bf16)
    count = rows // heads
    for h in range(heads):
        part = mixed[:, h, :]
        high = part.astype(bf16)
        low = (part - high.astype(f32)).astype(bf16)
        both = jnp.dot(jnp.concatenate([high, low], axis=0), up_ref[h], preferred_element_type=f32)
        projected[:, h, :] = both[:count] + both[count:]
    values = projected[...].reshape(rows, projected.shape[2]).astype(bf16)
    out_ref[:rows, :] = values
    out_ref[rows:, :] = stats


def merge_rows(parts, rows):
    tops = []
    sums = []
    for part in parts:
        stat = part[rows:, :].astype(f32)
        tops.append(stat[0:1] + stat[1:2] + stat[2:3])
        sums.append(stat[3:4] + stat[4:5])
    tops = jnp.concatenate(tops, axis=0)
    peak = jnp.max(tops, axis=0, keepdims=True)
    weights = jnp.exp2(tops - peak)
    weight_sum = jnp.sum(weights * jnp.concatenate(sums, axis=0), axis=0, keepdims=True)
    return weights, peak, weight_sum


def weigh(parts, weights, rows):
    spread = jnp.concatenate([weights, jnp.zeros((128 - len(parts), weights.shape[1]), f32)], axis=0).T
    return sum(part[:rows, :].astype(f32) * spread[:rows, i : i + 1] for i, part in enumerate(parts))


def middle_kernel(*refs):
    *parts, out_ref = refs
    parts = [part[...] for part in parts]
    rows = out_ref.shape[0] - 16
    weights, peak, weight_sum = merge_rows(parts, rows)
    out_ref[:rows, :] = weigh(parts, weights, rows).astype(bf16)
    line = lax.broadcasted_iota(jnp.int32, (16, weights.shape[1]), 0)
    first = peak.astype(bf16).astype(f32)
    second = (peak - first).astype(bf16).astype(f32)
    sum_first = weight_sum.astype(bf16).astype(f32)
    stats = jnp.where(line == 0, first, 0.0)
    stats = jnp.where(line == 1, second, stats)
    stats = jnp.where(line == 2, peak - first - second, stats)
    stats = jnp.where(line == 3, sum_first, stats)
    out_ref[rows:, :] = jnp.where(line == 4, weight_sum - sum_first, stats).astype(bf16)


def finish_kernel(*refs):
    *parts, out_ref = refs
    parts = [part[...] for part in parts]
    steps, half = out_ref.shape[:2]
    rows = steps * half * out_ref.shape[2]
    weights, _, weight_sum = merge_rows(parts, rows)
    result = weigh(parts, weights / weight_sum, rows)
    result = result.astype(bf16).reshape(half, steps, *out_ref.shape[2:])
    for b in range(half):
        out_ref[:, b] = result[b]


def place_kernel(info_ref, own_ref, other_ref, out_ref):
    half = own_ref.shape[1]
    first = info_ref[0]
    out_ref[:, pl.ds(first, half)] = own_ref[...]
    out_ref[:, pl.ds(half - first, half)] = other_ref[...]


def on_device(
    query_heads, up_keys, up_values, latent_cache, new_latent, context_lengths, positions
):
    steps, requests, heads, query_width = query_heads.shape
    nope = up_keys.shape[1]
    width = up_keys.shape[2]
    key_width = latent_cache.shape[2]
    rope = key_width - width
    value_width = up_values.shape[2]
    cached = latent_cache.shape[1]
    owners = lax.axis_size("head")
    plane = lax.axis_size("z") * lax.axis_size("x")
    pairs = steps * requests
    half = requests // 2
    scale = float(query_width) ** (-0.5) * log2_e

    core = lax.axis_index("core")
    slot = lax.axis_index(("z", "x", "core", "head"))

    vmem = pl.BlockSpec(memory_space=pltpu.VMEM)
    smem = pl.BlockSpec(memory_space=pltpu.SMEM)
    small = pltpu.CompilerParams(vmem_limit_bytes=12 * 2**20)
    anywhere = pl.BlockSpec(memory_space=pltpu.HBM)
    wide = 640
    in_hbm = functools.partial(pltpu.with_memory_space_constraint, memory_space=pltpu.HBM)
    core32 = core.astype(jnp.int32)
    own_first = (core32 * half).reshape(1)
    other_first = (half - core32 * half).reshape(1)
    first_row = (slot.astype(jnp.int32) * cached).reshape(1)
    place = lax.axis_index(("z", "x")).astype(jnp.int32).reshape(1)
    chunk = half * steps * heads
    own_queries, sent_queries, new_keys, limits = pl.pallas_call(
        functools.partial(queries_kernel, steps),
        in_specs=[smem] * 4 + [anywhere] * 5,
        out_specs=[vmem] * 4,
        out_shape=(
            jax.ShapeDtypeStruct((requests, steps * heads, wide), bf16),
            jax.ShapeDtypeStruct((half, steps * heads, wide), bf16),
            jax.ShapeDtypeStruct((pairs, key_width), bf16),
            jax.ShapeDtypeStruct((8, 128), jnp.int32),
        ),
        scratch_shapes=[
            pltpu.SMEM((requests,), jnp.int32),
            pltpu.SMEM((requests,), jnp.int32),
            pltpu.VMEM((pairs, heads, query_width), bf16),
            pltpu.VMEM(up_keys.shape, bf16),
            pltpu.VMEM(new_latent.shape, bf16),
            pltpu.VMEM((pairs, heads, width), f32),
            pltpu.SemaphoreType.DMA((8,)),
        ],
        compiler_params=pltpu.CompilerParams(vmem_limit_bytes=24 * 2**20),
        name="queries",
    )(
        other_first,
        own_first,
        first_row,
        place,
        in_hbm(positions),
        in_hbm(context_lengths),
        in_hbm(query_heads.reshape(pairs, heads, query_width)),
        in_hbm(up_keys),
        in_hbm(new_latent),
    )

    def over_head(array, k):
        return lax.ppermute(array, "head", [(i, i ^ k) for i in range(owners)])

    swap = [(0, 1), (1, 0)]
    partners = (2, 3, 1)
    got = [over_head(sent_queries, k) for k in partners]
    fresh = pl.pallas_call(
        functools.partial(fresh_kernel, scale, steps, heads),
        in_specs=[smem, vmem, vmem, vmem],
        out_specs=vmem,
        out_shape=jax.ShapeDtypeStruct((chunk, width + 128), bf16),
        compiler_params=small,
        cost_estimate=pl.CostEstimate(flops=10**9, bytes_accessed=4 * 10**6, transcendentals=0),
        name="fresh",
    )(own_first, limits, own_queries, new_keys)
    cache = jnp.swapaxes(latent_cache, 1, 2)
    staged_shape = pltpu.VMEM((half, key_width, cached), bf16)
    in_vmem = functools.partial(pltpu.with_memory_space_constraint, memory_space=pltpu.VMEM)
    staged = pl.pallas_call(
        stage_kernel,
        in_specs=[smem, anywhere],
        out_specs=vmem,
        out_shape=staged_shape,
        scratch_shapes=[pltpu.SemaphoreType.DMA((half,))],
        compiler_params=small,
        cost_estimate=pl.CostEstimate(flops=0, bytes_accessed=2 * half * key_width * cached, transcendentals=0),
        name="stage",
    )(other_first, in_hbm(cache))
    got[0], staged = lax.optimization_barrier((got[0], staged))
    passed = [lax.ppermute(g, "core", swap) for g in got]
    got, passed = lax.optimization_barrier((got, passed))

    rows = owners * steps * heads

    def attend(first, got, keys):
        return pl.pallas_call(
            functools.partial(attention_kernel, scale),
            in_specs=[smem] + [vmem] * 6,
            out_specs=vmem,
            scratch_shapes=[pltpu.VMEM((half, owners, steps * heads, wide), bf16)]
            + [pltpu.VMEM((rows, cached), f32)] * half,
            out_shape=jax.ShapeDtypeStruct((owners, chunk, width + 128), bf16),
            compiler_params=pltpu.CompilerParams(vmem_limit_bytes=18 * 2**20),
            cost_estimate=pl.CostEstimate(
                flops=2 * half * rows * cached * (key_width + width),
                bytes_accessed=half * cached * key_width * 2,
                transcendentals=half * rows * cached,
            ),
            name="attention",
        )(first, limits, own_queries, *got, keys)

    other_part = lax.ppermute(attend(other_first, got, in_vmem(staged)), "core", swap)
    own_part = attend(own_first, passed, cache)
    sent = pl.pallas_call(
        pair_kernel,
        in_specs=[vmem] * 2,
        out_specs=[vmem] * owners,
        out_shape=[jax.ShapeDtypeStruct((chunk, width + 128), bf16)] * owners,
        compiler_params=small,
        name="pair_merge",
    )(other_part, own_part)
    arrived = [over_head(array, k) for array, k in zip(sent[1:], partners)]
    part = pl.pallas_call(
        functools.partial(project_kernel, heads),
        in_specs=[vmem] * 6,
        out_specs=vmem,
        out_shape=jax.ShapeDtypeStruct((chunk + 16, value_width), bf16),
        scratch_shapes=[
            pltpu.VMEM((chunk // heads, heads, width), f32),
            pltpu.VMEM((chunk // heads, heads, value_width), f32),
        ],
        compiler_params=small,
        name="project",
    )(sent[0], *arrived, fresh, up_values)

    def over_plane(array, k):
        return lax.ppermute(array, ("z", "x"), [(i, i ^ k) for i in range(plane)])

    part = pl.pallas_call(
        middle_kernel,
        in_specs=[vmem] * 4,
        out_specs=vmem,
        out_shape=jax.ShapeDtypeStruct(part.shape, bf16),
        compiler_params=small,
        name="middle_merge",
    )(part, *[over_plane(part, k) for k in (2, 3, 1)])
    own = pl.pallas_call(
        finish_kernel,
        in_specs=[vmem] * 4,
        out_specs=vmem,
        out_shape=jax.ShapeDtypeStruct((steps, half, heads, value_width), bf16),
        compiler_params=small,
        name="finish",
    )(part, *[over_plane(part, k) for k in (8, 12, 4)])
    theirs = lax.ppermute(own, "core", swap)
    return pl.pallas_call(
        place_kernel,
        in_specs=[smem, vmem, vmem],
        out_specs=vmem,
        out_shape=jax.ShapeDtypeStruct((steps, requests, heads, value_width), bf16),
        compiler_params=small,
        name="place",
    )(own_first, own, theirs)


def solution(mesh):
    fine = Mesh(mesh.devices.reshape(4, 4, 2, 4), ("z", "x", "core", "head"))
    in_specs = (
        P(None, None, "head", None),
        P("head", None, None),
        P("head", None, None),
        P(None, ("z", "x", "core", "head"), None),
        P(),
        P(),
        P(),
    )
    out_specs = P(None, None, "head", None)
    return jax.shard_map(
        on_device, mesh=fine, in_specs=in_specs, out_specs=out_specs, check_vma=False
    )
```

```python
import functools

import jax
import jax.numpy as jnp
from jax import lax
from jax.experimental import pallas as pl
from jax.experimental.pallas import tpu as pltpu
from jax.sharding import Mesh, PartitionSpec as P

rope_base = 50000.0
masked_score = -1e30
lowest_max = -1e29
log2_e = 1.4426950408889634
bf16 = jnp.bfloat16
f32 = jnp.float32


def swap_halves(values):
    half = values.shape[-1] // 2
    return jnp.concatenate([values[..., half:], values[..., :half]], axis=-1)


def rope_tables(positions_ref, steps, width):
    requests = positions_ref.shape[0]
    pairs = steps * requests
    half = width // 2
    row = lax.broadcasted_iota(jnp.int32, (pairs, width), 0)
    lane = lax.broadcasted_iota(jnp.int32, (pairs, width), 1)
    where_at = row // requests
    for b in range(requests):
        where_at += jnp.where(row % requests == b, positions_ref[b], 0)
    counter = lax.broadcasted_iota(jnp.int32, (1, width), 1) % half
    inverse = jnp.zeros((1, width), f32)
    for i in range(half):
        inverse = jnp.where(counter == i, f32(rope_base ** (-2.0 * i / width)), inverse)
    angles = where_at.astype(f32) * inverse
    return jnp.cos(angles), jnp.where(lane < half, -1.0, 1.0) * jnp.sin(angles)


def queries_kernel(
    steps,
    info_ref,
    own_first_ref,
    row_ref,
    place_ref,
    positions_hbm,
    lengths_hbm,
    q_hbm,
    up_hbm,
    new_hbm,
    own_ref,
    sent_ref,
    keys_ref,
    limits_ref,
    positions,
    lengths,
    q,
    up,
    new,
    lat,
    sems,
):
    pairs, heads, _ = q.shape
    requests = pairs // steps
    nope, width = up.shape[1], up.shape[2]
    key_width = new.shape[2]
    fetches = [
        pltpu.make_async_copy(positions_hbm, positions, sems.at[0]),
        pltpu.make_async_copy(q_hbm, q, sems.at[1]),
        pltpu.make_async_copy(new_hbm, new, sems.at[2]),
        pltpu.make_async_copy(lengths_hbm, lengths, sems.at[3]),
    ]
    groups = 4
    share = heads // groups
    for g in range(groups):
        at = pl.ds(g * share, share)
        fetches.append(pltpu.make_async_copy(up_hbm.at[at], up.at[at], sems.at[4 + g]))
    for fetch in fetches:
        fetch.start()
    own_ref[:, :, key_width:] = jnp.zeros(own_ref.shape[:2] + (own_ref.shape[2] - key_width,), bf16)
    fetches[0].wait()
    cos, sin = rope_tables(positions, steps, key_width - width)
    fetches[1].wait()
    rope = q[:, :, nope:].astype(f32)
    rope = (rope * cos[:, None, :] + swap_halves(rope) * sin[:, None, :]).astype(bf16)
    for s in range(steps):
        for b in range(requests):
            own_ref[b, s * heads : (s + 1) * heads, width:key_width] = rope[s * requests + b]
    fetches[3].wait()
    line = lax.broadcasted_iota(jnp.int32, limits_ref.shape, 0)
    limits = jnp.zeros(limits_ref.shape, jnp.int32)
    for b in range(requests):
        limits = jnp.where(line == b, lengths[b] - row_ref[0], limits)
    limits_ref[...] = jnp.where(line == requests, place_ref[0], limits)
    fetches[2].wait()
    rows = jnp.concatenate([new[t].astype(f32) for t in range(steps)], axis=0)
    tail = rows[:, width:]
    tail = tail * cos + swap_halves(tail) * sin
    keys_ref[...] = jnp.concatenate([rows[:, :width], tail], axis=-1).astype(bf16)
    q_f32 = q[:, :, :nope].astype(f32)
    for h in range(heads):
        if h % share == 0:
            fetches[4 + h // share].wait()
        lat[:, h, :] = jnp.dot(q_f32[:, h, :].astype(bf16), up[h], preferred_element_type=f32)
    for s in range(steps):
        for b in range(requests):
            own_ref[b, s * heads : (s + 1) * heads, :width] = lat[s * requests + b].astype(bf16)
    packed = [own_ref[info_ref[0] + i] for i in range(sent_ref.shape[1] // key_width)]
    latents = [row[:, :width] for row in packed]
    sent_ref[...] = jnp.concatenate(latents + [row[:, width:key_width] for row in packed], axis=-1)


def split_stats(peak, weight_sum, rows):
    lane = lax.broadcasted_iota(jnp.int32, (rows, 128), 1)
    first = peak.astype(bf16).astype(f32)
    rest = peak - first
    second = rest.astype(bf16).astype(f32)
    third = rest - second
    sum_first = weight_sum.astype(bf16).astype(f32)
    sum_second = weight_sum - sum_first
    out = jnp.where(lane == 0, first, 0.0)
    out = jnp.where(lane == 1, second, out)
    out = jnp.where(lane == 2, third, out)
    out = jnp.where(lane == 3, sum_first, out)
    return jnp.where(lane == 4, sum_second, out)


def stage_kernel(info_ref, cache_hbm, out_ref, sems):
    copies = []
    for i in range(out_ref.shape[0]):
        copies.append(pltpu.make_async_copy(cache_hbm.at[info_ref[0] + i], out_ref.at[i], sems.at[i]))
    for copy in copies:
        copy.start()
    for copy in copies:
        copy.wait()


def stat_rows(peak, weight_sum):
    line = lax.broadcasted_iota(jnp.int32, (16, peak.shape[1]), 0)
    first = peak.astype(bf16).astype(f32)
    second = (peak - first).astype(bf16).astype(f32)
    sum_first = weight_sum.astype(bf16).astype(f32)
    stats = jnp.where(line == 0, first, 0.0)
    stats = jnp.where(line == 1, second, stats)
    stats = jnp.where(line == 2, peak - first - second, stats)
    stats = jnp.where(line == 3, sum_first, stats)
    return jnp.where(line == 4, weight_sum - sum_first, stats).astype(bf16)


def attention_kernel(scale, info_ref, limits_ref, own_ref, q1_ref, q2_ref, q3_ref, k_ref, out_ref, q_ref, *scores):
    count, owners, share, _ = q_ref.shape
    rows = owners * share
    key_width, cached = k_ref.shape[1:]
    width = out_ref.shape[2] - 128
    chunk = 1024
    first = info_ref[0]
    base = first if k_ref.shape[0] > count else 0
    q_ref[:, 0] = own_ref[pl.ds(first, count)]
    rope = key_width - width
    for k, packed_ref in enumerate((q1_ref, q2_ref, q3_ref)):
        for i in range(count):
            q_ref[i, 1 + k, :, :width] = packed_ref[:, i * width : (i + 1) * width]
            at = count * width + i * rope
            q_ref[i, 1 + k, :, width:key_width] = packed_ref[:, at : at + rope]

    tops = []
    for i in range(count):
        limit = limits_ref[pl.ds(first + i, 1), :1]
        queries = q_ref[i].reshape(rows, -1)[:, :key_width]
        top = jnp.full((rows, 128), lowest_max, f32)
        for c in range(0, cached, chunk):
            keys = k_ref[base + i, :, c : c + chunk]
            part = jnp.dot(queries, keys, preferred_element_type=f32) * scale
            column = lax.broadcasted_iota(jnp.int32, (1, chunk), 1) + c
            part = jnp.where(column < limit, part, masked_score)
            scores[i][:, c : c + chunk] = part
            for at in range(0, chunk, 128):
                top = jnp.maximum(top, part[:, at : at + 128])
        tops.append(jnp.max(top, axis=1, keepdims=True))

    for i in range(count):
        total = jnp.zeros((rows, 128), f32)
        for c in range(0, cached, chunk):
            weights = jnp.exp2(scores[i][:, c : c + chunk] - tops[i])
            for at in range(0, chunk, 128):
                total = total + weights[:, at : at + 128]
            part = lax.dot_general(
                weights.astype(bf16),
                k_ref[base + i, :width, c : c + chunk],
                (((1,), (1,)), ((), ())),
                preferred_element_type=f32,
            )
            mixed = part if c == 0 else mixed + part
        total = jnp.sum(total, axis=1, keepdims=True)
        at = slice(i * share, (i + 1) * share)
        out_ref[:, at, :width] = mixed.astype(bf16).reshape(owners, share, width)
        out_ref[:, at, width:] = split_stats(tops[i], total, rows).astype(bf16).reshape(owners, share, 128)


def fresh_kernel(scale, steps, heads, info_ref, limits_ref, own_ref, new_ref, out_ref):
    requests, share, _ = own_ref.shape
    key_width = new_ref.shape[1]
    width = out_ref.shape[1]
    requests_rows = out_ref.shape[0] - 16
    stats = []
    fresh = new_ref[...]
    shape = (share, fresh.shape[0])
    key = lax.broadcasted_iota(jnp.int32, shape, 1)
    step = (lax.broadcasted_iota(jnp.int32, shape, 0) // heads) % steps
    counted = limits_ref[requests : requests + 1, :1] == 0
    for i in range(requests_rows // share):
        request = info_ref[0] + i
        scores = (
            lax.dot_general(
                own_ref[request][:, :key_width], fresh, (((1,), (1,)), ((), ())), preferred_element_type=f32
            )
            * scale
        )
        visible = (key % requests == request) & (key // requests <= step) & counted
        scores = jnp.where(visible, scores, masked_score)
        top = jnp.maximum(jnp.max(scores, axis=1, keepdims=True), lowest_max)
        weights = jnp.exp2(scores - top)
        total = jnp.sum(weights, axis=1, keepdims=True)
        mixed = jnp.dot(weights.astype(bf16), fresh[:, :width], preferred_element_type=f32)
        out_ref[i * share : (i + 1) * share, :] = mixed.astype(bf16)
        stats.append(split_stats(top, total, share))
    out_ref[requests_rows:, :] = jnp.zeros((16, width), bf16)
    out_ref[requests_rows:, :requests_rows] = jnp.concatenate(stats, axis=0).T[:16].astype(bf16)


def merge_parts(parts, width):
    tops = []
    sums = []
    for part in parts:
        stat = part[:, width:].astype(f32)
        tops.append(stat[:, 0:1] + stat[:, 1:2] + stat[:, 2:3])
        sums.append(stat[:, 3:4] + stat[:, 4:5])
    peak = functools.reduce(jnp.maximum, tops)
    weights = [jnp.exp2(t - peak) for t in tops]
    weight_sum = sum(w * s for w, s in zip(weights, sums))
    merged = sum(w * part[:, :width].astype(f32) for w, part in zip(weights, parts))
    return merged, peak, weight_sum


def pair_kernel(a_ref, b_ref, *sent_refs):
    width = sent_refs[0].shape[1]
    rows = sent_refs[0].shape[0] - 16
    for owner, sent_ref in enumerate(sent_refs):
        merged, peak, weight_sum = merge_parts((a_ref[owner], b_ref[owner]), width)
        sent_ref[:rows, :] = merged.astype(bf16)
        sent_ref[rows:, :] = jnp.zeros((16, width), bf16)
        sent_ref[rows:, :rows] = split_stats(peak, weight_sum, rows).T[:16].astype(bf16)


def project_kernel(heads, *refs):
    *parts, up_ref, out_ref = refs
    parts = [part[...] for part in parts]
    rows = out_ref.shape[0] - 16
    weights, peak, weight_sum = merge_rows(parts, rows)
    mixed = weigh(parts, weights, rows)
    high = mixed.astype(bf16)
    both = jnp.concatenate([high, (mixed - high.astype(f32)).astype(bf16)], axis=0)
    value_width = out_ref.shape[1]
    head = lax.broadcasted_iota(jnp.int32, (rows, value_width), 0) % heads
    values = jnp.zeros((rows, value_width), f32)
    for h in range(0, heads, 2):
        two = jnp.concatenate([up_ref[h], up_ref[h + 1]], axis=1)
        part = jnp.dot(both, two, preferred_element_type=f32)
        part = part[:rows] + part[rows:]
        values = jnp.where(head == h, part[:, :value_width], values)
        values = jnp.where(head == h + 1, part[:, value_width:], values)
    out_ref[:rows, :] = values.astype(bf16)
    out_ref[rows:, :] = stat_rows(peak, weight_sum)


def merge_rows(parts, rows):
    tops = []
    sums = []
    for part in parts:
        stat = part[rows:, :rows].astype(f32)
        tops.append(stat[0:1] + stat[1:2] + stat[2:3])
        sums.append(stat[3:4] + stat[4:5])
    tops = jnp.concatenate(tops, axis=0)
    peak = jnp.max(tops, axis=0, keepdims=True)
    weights = jnp.exp2(tops - peak)
    weight_sum = jnp.sum(weights * jnp.concatenate(sums, axis=0), axis=0, keepdims=True)
    return weights, peak, weight_sum


def weigh(parts, weights, rows):
    spread = jnp.concatenate([weights, jnp.zeros((128 - len(parts), weights.shape[1]), f32)], axis=0).T
    return sum(part[:rows, :].astype(f32) * spread[:rows, i : i + 1] for i, part in enumerate(parts))


def middle_kernel(*refs):
    *parts, out_ref = refs
    parts = [part[...] for part in parts]
    rows = out_ref.shape[0] - 16
    weights, peak, weight_sum = merge_rows(parts, rows)
    out_ref[:rows, :] = weigh(parts, weights, rows).astype(bf16)
    out_ref[rows:, :] = stat_rows(peak, weight_sum)


def finish_kernel(*refs):
    *parts, out_ref = refs
    parts = [part[...] for part in parts]
    steps, half = out_ref.shape[:2]
    rows = steps * half * out_ref.shape[2]
    weights, _, weight_sum = merge_rows(parts, rows)
    result = weigh(parts, weights / weight_sum, rows)
    result = result.astype(bf16).reshape(half, steps, *out_ref.shape[2:])
    for b in range(half):
        out_ref[:, b] = result[b]


def place_kernel(info_ref, own_ref, other_ref, out_ref):
    half = own_ref.shape[1]
    first = info_ref[0]
    out_ref[:, pl.ds(first, half)] = own_ref[...]
    out_ref[:, pl.ds(half - first, half)] = other_ref[...]


def on_device(
    query_heads, up_keys, up_values, latent_cache, new_latent, context_lengths, positions
):
    steps, requests, heads, query_width = query_heads.shape
    nope = up_keys.shape[1]
    width = up_keys.shape[2]
    key_width = latent_cache.shape[2]
    rope = key_width - width
    value_width = up_values.shape[2]
    cached = latent_cache.shape[1]
    owners = lax.axis_size("head")
    plane = lax.axis_size("z") * lax.axis_size("x")
    pairs = steps * requests
    half = requests // 2
    scale = float(query_width) ** (-0.5) * log2_e

    core = lax.axis_index("core")
    slot = lax.axis_index(("z", "x", "core", "head"))

    vmem = pl.BlockSpec(memory_space=pltpu.VMEM)
    smem = pl.BlockSpec(memory_space=pltpu.SMEM)
    small = pltpu.CompilerParams(vmem_limit_bytes=12 * 2**20)
    anywhere = pl.BlockSpec(memory_space=pltpu.HBM)
    wide = 640
    in_hbm = functools.partial(pltpu.with_memory_space_constraint, memory_space=pltpu.HBM)
    core32 = core.astype(jnp.int32)
    own_first = (core32 * half).reshape(1)
    other_first = (half - core32 * half).reshape(1)
    first_row = (slot.astype(jnp.int32) * cached).reshape(1)
    place = lax.axis_index(("z", "x")).astype(jnp.int32).reshape(1)
    chunk = half * steps * heads
    own_queries, sent_queries, new_keys, limits = pl.pallas_call(
        functools.partial(queries_kernel, steps),
        in_specs=[smem] * 4 + [anywhere] * 5,
        out_specs=[vmem] * 4,
        out_shape=(
            jax.ShapeDtypeStruct((requests, steps * heads, wide), bf16),
            jax.ShapeDtypeStruct((steps * heads, half * key_width), bf16),
            jax.ShapeDtypeStruct((pairs, key_width), bf16),
            jax.ShapeDtypeStruct((8, 128), jnp.int32),
        ),
        scratch_shapes=[
            pltpu.SMEM((requests,), jnp.int32),
            pltpu.SMEM((requests,), jnp.int32),
            pltpu.VMEM((pairs, heads, query_width), bf16),
            pltpu.VMEM(up_keys.shape, bf16),
            pltpu.VMEM(new_latent.shape, bf16),
            pltpu.VMEM((pairs, heads, width), f32),
            pltpu.SemaphoreType.DMA((8,)),
        ],
        compiler_params=pltpu.CompilerParams(vmem_limit_bytes=24 * 2**20),
        name="queries",
    )(
        other_first,
        own_first,
        first_row,
        place,
        in_hbm(positions),
        in_hbm(context_lengths),
        in_hbm(query_heads.reshape(pairs, heads, query_width)),
        in_hbm(up_keys),
        in_hbm(new_latent),
    )

    def over_head(array, k):
        return lax.ppermute(array, "head", [(i, i ^ k) for i in range(owners)])

    swap = [(0, 1), (1, 0)]
    partners = (2, 3, 1)
    got = [over_head(sent_queries, k) for k in partners]
    fresh = pl.pallas_call(
        functools.partial(fresh_kernel, scale, steps, heads),
        in_specs=[smem, vmem, vmem, vmem],
        out_specs=vmem,
        out_shape=jax.ShapeDtypeStruct((chunk + 16, width), bf16),
        compiler_params=small,
        cost_estimate=pl.CostEstimate(flops=10**9, bytes_accessed=4 * 10**6, transcendentals=0),
        name="fresh",
    )(own_first, limits, own_queries, new_keys)
    cache = jnp.swapaxes(latent_cache, 1, 2)
    staged_shape = pltpu.VMEM((half, key_width, cached), bf16)
    in_vmem = functools.partial(pltpu.with_memory_space_constraint, memory_space=pltpu.VMEM)
    staged = pl.pallas_call(
        stage_kernel,
        in_specs=[smem, anywhere],
        out_specs=vmem,
        out_shape=staged_shape,
        scratch_shapes=[pltpu.SemaphoreType.DMA((half,))],
        compiler_params=small,
        cost_estimate=pl.CostEstimate(flops=0, bytes_accessed=2 * half * key_width * cached, transcendentals=0),
        name="stage",
    )(other_first, in_hbm(cache))
    got[0], staged = lax.optimization_barrier((got[0], staged))
    passed = [lax.ppermute(g, "core", swap) for g in got]
    got, passed = lax.optimization_barrier((got, passed))

    rows = owners * steps * heads

    def attend(first, got, keys):
        return pl.pallas_call(
            functools.partial(attention_kernel, scale),
            in_specs=[smem] + [vmem] * 6,
            out_specs=vmem,
            scratch_shapes=[pltpu.VMEM((half, owners, steps * heads, wide), bf16)]
            + [pltpu.VMEM((rows, cached), f32)] * half,
            out_shape=jax.ShapeDtypeStruct((owners, chunk, width + 128), bf16),
            compiler_params=pltpu.CompilerParams(vmem_limit_bytes=18 * 2**20),
            cost_estimate=pl.CostEstimate(
                flops=2 * half * rows * cached * (key_width + width),
                bytes_accessed=half * cached * key_width * 2,
                transcendentals=half * rows * cached,
            ),
            name="attention",
        )(first, limits, own_queries, *got, keys)

    other_part = lax.ppermute(attend(other_first, got, in_vmem(staged)), "core", swap)
    own_part = attend(own_first, passed, cache)
    sent = pl.pallas_call(
        pair_kernel,
        in_specs=[vmem] * 2,
        out_specs=[vmem] * owners,
        out_shape=[jax.ShapeDtypeStruct((chunk + 16, width), bf16)] * owners,
        compiler_params=small,
        name="pair_merge",
    )(other_part, own_part)
    arrived = [over_head(array, k) for array, k in zip(sent[1:], partners)]
    part = pl.pallas_call(
        functools.partial(project_kernel, heads),
        in_specs=[vmem] * 6,
        out_specs=vmem,
        out_shape=jax.ShapeDtypeStruct((chunk + 16, value_width), bf16),
        compiler_params=small,
        name="project",
    )(sent[0], *arrived, fresh, up_values)

    def over_plane(array, k):
        return lax.ppermute(array, ("z", "x"), [(i, i ^ k) for i in range(plane)])

    part = pl.pallas_call(
        middle_kernel,
        in_specs=[vmem] * 4,
        out_specs=vmem,
        out_shape=jax.ShapeDtypeStruct(part.shape, bf16),
        compiler_params=small,
        name="middle_merge",
    )(part, *[over_plane(part, k) for k in (2, 3, 1)])
    own = pl.pallas_call(
        finish_kernel,
        in_specs=[vmem] * 4,
        out_specs=vmem,
        out_shape=jax.ShapeDtypeStruct((steps, half, heads, value_width), bf16),
        compiler_params=small,
        name="finish",
    )(part, *[over_plane(part, k) for k in (8, 12, 4)])
    theirs = lax.ppermute(own, "core", swap)
    return pl.pallas_call(
        place_kernel,
        in_specs=[smem, vmem, vmem],
        out_specs=vmem,
        out_shape=jax.ShapeDtypeStruct((steps, requests, heads, value_width), bf16),
        compiler_params=small,
        name="place",
    )(own_first, own, theirs)


def solution(mesh):
    fine = Mesh(mesh.devices.reshape(4, 4, 2, 4), ("z", "x", "core", "head"))
    in_specs = (
        P(None, None, "head", None),
        P("head", None, None),
        P("head", None, None),
        P(None, ("z", "x", "core", "head"), None),
        P(),
        P(),
        P(),
    )
    out_specs = P(None, None, "head", None)
    return jax.shard_map(
        on_device, mesh=fine, in_specs=in_specs, out_specs=out_specs, check_vma=False
    )
```

```python
import functools

import jax
import jax.numpy as jnp
from jax import lax
from jax.experimental import pallas as pl
from jax.experimental.pallas import tpu as pltpu
from jax.sharding import Mesh, PartitionSpec as P

rope_base = 50000.0
masked_score = -1e30
lowest_max = -1e29
log2_e = 1.4426950408889634
bf16 = jnp.bfloat16
f32 = jnp.float32


def swap_halves(values):
    half = values.shape[-1] // 2
    return jnp.concatenate([values[..., half:], values[..., :half]], axis=-1)


def rope_tables(positions_ref, steps, width):
    requests = positions_ref.shape[0]
    pairs = steps * requests
    half = width // 2
    row = lax.broadcasted_iota(jnp.int32, (pairs, width), 0)
    lane = lax.broadcasted_iota(jnp.int32, (pairs, width), 1)
    where_at = row // requests
    for b in range(requests):
        where_at += jnp.where(row % requests == b, positions_ref[b], 0)
    counter = lax.broadcasted_iota(jnp.int32, (1, width), 1) % half
    inverse = jnp.zeros((1, width), f32)
    for i in range(half):
        inverse = jnp.where(counter == i, f32(rope_base ** (-2.0 * i / width)), inverse)
    angles = where_at.astype(f32) * inverse
    return jnp.cos(angles), jnp.where(lane < half, -1.0, 1.0) * jnp.sin(angles)


def queries_kernel(
    steps,
    info_ref,
    own_first_ref,
    row_ref,
    place_ref,
    positions_hbm,
    lengths_hbm,
    q_hbm,
    up_hbm,
    new_hbm,
    own_ref,
    sent_ref,
    keys_ref,
    limits_ref,
    positions,
    lengths,
    q,
    up,
    new,
    lat,
    sems,
):
    pairs, heads, _ = q.shape
    requests = pairs // steps
    nope, width = up.shape[1], up.shape[2]
    key_width = new.shape[2]
    fetches = [
        pltpu.make_async_copy(positions_hbm, positions, sems.at[0]),
        pltpu.make_async_copy(q_hbm, q, sems.at[1]),
        pltpu.make_async_copy(new_hbm, new, sems.at[2]),
        pltpu.make_async_copy(lengths_hbm, lengths, sems.at[3]),
    ]
    groups = 4
    share = heads // groups
    for g in range(groups):
        at = pl.ds(g * share, share)
        fetches.append(pltpu.make_async_copy(up_hbm.at[at], up.at[at], sems.at[4 + g]))
    for fetch in fetches:
        fetch.start()
    own_ref[:, :, key_width:] = jnp.zeros(own_ref.shape[:2] + (own_ref.shape[2] - key_width,), bf16)
    fetches[0].wait()
    cos, sin = rope_tables(positions, steps, key_width - width)
    fetches[1].wait()
    rope = q[:, :, nope:].astype(f32)
    rope = (rope * cos[:, None, :] + swap_halves(rope) * sin[:, None, :]).astype(bf16)
    for s in range(steps):
        for b in range(requests):
            own_ref[b, s * heads : (s + 1) * heads, width:key_width] = rope[s * requests + b]
    fetches[3].wait()
    line = lax.broadcasted_iota(jnp.int32, limits_ref.shape, 0)
    limits = jnp.zeros(limits_ref.shape, jnp.int32)
    for b in range(requests):
        limits = jnp.where(line == b, lengths[b] - row_ref[0], limits)
    limits_ref[...] = jnp.where(line == requests, place_ref[0], limits)
    fetches[2].wait()
    rows = jnp.concatenate([new[t].astype(f32) for t in range(steps)], axis=0)
    tail = rows[:, width:]
    tail = tail * cos + swap_halves(tail) * sin
    keys_ref[...] = jnp.concatenate([rows[:, :width], tail], axis=-1).astype(bf16)
    q_f32 = q[:, :, :nope].astype(f32)
    for h in range(heads):
        if h % share == 0:
            fetches[4 + h // share].wait()
        lat[:, h, :] = jnp.dot(q_f32[:, h, :].astype(bf16), up[h], preferred_element_type=f32)
    for s in range(steps):
        for b in range(requests):
            own_ref[b, s * heads : (s + 1) * heads, :width] = lat[s * requests + b].astype(bf16)
    packed = [own_ref[info_ref[0] + i] for i in range(sent_ref.shape[1] // key_width)]
    latents = [row[:, :width] for row in packed]
    sent_ref[...] = jnp.concatenate(latents + [row[:, width:key_width] for row in packed], axis=-1)


def split_stats(peak, weight_sum, rows):
    lane = lax.broadcasted_iota(jnp.int32, (rows, 128), 1)
    first = peak.astype(bf16).astype(f32)
    rest = peak - first
    second = rest.astype(bf16).astype(f32)
    third = rest - second
    sum_first = weight_sum.astype(bf16).astype(f32)
    sum_second = weight_sum - sum_first
    out = jnp.where(lane == 0, first, 0.0)
    out = jnp.where(lane == 1, second, out)
    out = jnp.where(lane == 2, third, out)
    out = jnp.where(lane == 3, sum_first, out)
    return jnp.where(lane == 4, sum_second, out)


def stage_kernel(info_ref, cache_hbm, out_ref, sems):
    copies = []
    for i in range(out_ref.shape[0]):
        copies.append(pltpu.make_async_copy(cache_hbm.at[info_ref[0] + i], out_ref.at[i], sems.at[i]))
    for copy in copies:
        copy.start()
    for copy in copies:
        copy.wait()


def stat_rows(peak, weight_sum):
    line = lax.broadcasted_iota(jnp.int32, (16, peak.shape[1]), 0)
    first = peak.astype(bf16).astype(f32)
    second = (peak - first).astype(bf16).astype(f32)
    sum_first = weight_sum.astype(bf16).astype(f32)
    stats = jnp.where(line == 0, first, 0.0)
    stats = jnp.where(line == 1, second, stats)
    stats = jnp.where(line == 2, peak - first - second, stats)
    stats = jnp.where(line == 3, sum_first, stats)
    return jnp.where(line == 4, weight_sum - sum_first, stats).astype(bf16)


def attention_kernel(scale, info_ref, limits_ref, own_ref, q1_ref, q2_ref, q3_ref, k_ref, out_ref, q_ref, *scores):
    count, owners, share, _ = q_ref.shape
    rows = owners * share
    key_width, cached = k_ref.shape[1:]
    width = out_ref.shape[2] - 128
    chunk = 1024
    first = info_ref[0]
    base = first if k_ref.shape[0] > count else 0
    q_ref[:, 0] = own_ref[pl.ds(first, count)]
    rope = key_width - width
    for k, packed_ref in enumerate((q1_ref, q2_ref, q3_ref)):
        for i in range(count):
            q_ref[i, 1 + k, :, :width] = packed_ref[:, i * width : (i + 1) * width]
            at = count * width + i * rope
            q_ref[i, 1 + k, :, width:key_width] = packed_ref[:, at : at + rope]

    tops = []
    for i in range(count):
        limit = limits_ref[pl.ds(first + i, 1), :1]
        queries = q_ref[i].reshape(rows, -1)[:, :key_width]
        top = jnp.full((rows, 128), lowest_max, f32)
        for c in range(0, cached, chunk):
            keys = k_ref[base + i, :, c : c + chunk]
            part = jnp.dot(queries, keys, preferred_element_type=f32) * scale
            column = lax.broadcasted_iota(jnp.int32, (1, chunk), 1) + c
            part = jnp.where(column < limit, part, masked_score)
            scores[i][:, c : c + chunk] = part
            for at in range(0, chunk, 128):
                top = jnp.maximum(top, part[:, at : at + 128])
        tops.append(jnp.max(top, axis=1, keepdims=True))

    for i in range(count):
        total = jnp.zeros((rows, 128), f32)
        for c in range(0, cached, chunk):
            weights = jnp.exp2(scores[i][:, c : c + chunk] - tops[i])
            for at in range(0, chunk, 128):
                total = total + weights[:, at : at + 128]
            part = lax.dot_general(
                weights.astype(bf16),
                k_ref[base + i, :width, c : c + chunk],
                (((1,), (1,)), ((), ())),
                preferred_element_type=f32,
            )
            mixed = part if c == 0 else mixed + part
        total = jnp.sum(total, axis=1, keepdims=True)
        at = slice(i * share, (i + 1) * share)
        out_ref[:, at, :width] = mixed.astype(bf16).reshape(owners, share, width)
        out_ref[:, at, width:] = split_stats(tops[i], total, rows).astype(bf16).reshape(owners, share, 128)


def fresh_kernel(scale, steps, heads, info_ref, limits_ref, own_ref, new_ref, out_ref):
    requests, share, _ = own_ref.shape
    key_width = new_ref.shape[1]
    width = out_ref.shape[1]
    requests_rows = out_ref.shape[0] - 16
    stats = []
    fresh = new_ref[...]
    shape = (share, fresh.shape[0])
    key = lax.broadcasted_iota(jnp.int32, shape, 1)
    step = (lax.broadcasted_iota(jnp.int32, shape, 0) // heads) % steps
    counted = limits_ref[requests : requests + 1, :1] == 0
    for i in range(requests_rows // share):
        request = info_ref[0] + i
        scores = (
            lax.dot_general(
                own_ref[request][:, :key_width], fresh, (((1,), (1,)), ((), ())), preferred_element_type=f32
            )
            * scale
        )
        visible = (key % requests == request) & (key // requests <= step) & counted
        scores = jnp.where(visible, scores, masked_score)
        top = jnp.maximum(jnp.max(scores, axis=1, keepdims=True), lowest_max)
        weights = jnp.exp2(scores - top)
        total = jnp.sum(weights, axis=1, keepdims=True)
        mixed = jnp.dot(weights.astype(bf16), fresh[:, :width], preferred_element_type=f32)
        out_ref[i * share : (i + 1) * share, :] = mixed.astype(bf16)
        stats.append(split_stats(top, total, share))
    out_ref[requests_rows:, :] = jnp.zeros((16, width), bf16)
    out_ref[requests_rows:, :requests_rows] = jnp.concatenate(stats, axis=0).T[:16].astype(bf16)


def merge_parts(parts, width):
    tops = []
    sums = []
    for part in parts:
        stat = part[:, width:].astype(f32)
        tops.append(stat[:, 0:1] + stat[:, 1:2] + stat[:, 2:3])
        sums.append(stat[:, 3:4] + stat[:, 4:5])
    peak = functools.reduce(jnp.maximum, tops)
    weights = [jnp.exp2(t - peak) for t in tops]
    weight_sum = sum(w * s for w, s in zip(weights, sums))
    merged = sum(w * part[:, :width].astype(f32) for w, part in zip(weights, parts))
    return merged, peak, weight_sum


def pair_kernel(a_ref, b_ref, *sent_refs):
    width = sent_refs[0].shape[1]
    rows = sent_refs[0].shape[0] - 16
    for owner, sent_ref in enumerate(sent_refs):
        merged, peak, weight_sum = merge_parts((a_ref[owner], b_ref[owner]), width)
        sent_ref[:rows, :] = merged.astype(bf16)
        sent_ref[rows:, :] = jnp.zeros((16, width), bf16)
        sent_ref[rows:, :rows] = split_stats(peak, weight_sum, rows).T[:16].astype(bf16)


def project_kernel(heads, *refs):
    *parts, up_ref, out_ref = refs
    parts = [part[...] for part in parts]
    rows = out_ref.shape[0] - 16
    weights, peak, weight_sum = merge_rows(parts, rows)
    mixed = weigh(parts, weights, rows)
    high = mixed.astype(bf16)
    both = jnp.concatenate([high, (mixed - high.astype(f32)).astype(bf16)], axis=0)
    value_width = out_ref.shape[1]
    head = lax.broadcasted_iota(jnp.int32, (rows, value_width), 0) % heads
    values = jnp.zeros((rows, value_width), f32)
    for h in range(0, heads, 2):
        two = jnp.concatenate([up_ref[h], up_ref[h + 1]], axis=1)
        part = jnp.dot(both, two, preferred_element_type=f32)
        part = part[:rows] + part[rows:]
        values = jnp.where(head == h, part[:, :value_width], values)
        values = jnp.where(head == h + 1, part[:, value_width:], values)
    out_ref[:rows, :] = values.astype(bf16)
    out_ref[rows:, :] = stat_rows(peak, weight_sum)


def merge_rows(parts, rows):
    tops = []
    sums = []
    for part in parts:
        stat = part[rows:, :rows].astype(f32)
        tops.append(stat[0:1] + stat[1:2] + stat[2:3])
        sums.append(stat[3:4] + stat[4:5])
    tops = jnp.concatenate(tops, axis=0)
    peak = jnp.max(tops, axis=0, keepdims=True)
    weights = jnp.exp2(tops - peak)
    weight_sum = jnp.sum(weights * jnp.concatenate(sums, axis=0), axis=0, keepdims=True)
    return weights, peak, weight_sum


def weigh(parts, weights, rows):
    spread = jnp.concatenate([weights, jnp.zeros((128 - len(parts), weights.shape[1]), f32)], axis=0).T
    return sum(part[:rows, :].astype(f32) * spread[:rows, i : i + 1] for i, part in enumerate(parts))


def middle_kernel(*refs):
    *parts, out_ref = refs
    parts = [part[...] for part in parts]
    rows = out_ref.shape[0] - 16
    weights, peak, weight_sum = merge_rows(parts, rows)
    out_ref[:rows, :] = weigh(parts, weights, rows).astype(bf16)
    out_ref[rows:, :] = stat_rows(peak, weight_sum)


def finish_kernel(*refs):
    *parts, out_ref = refs
    parts = [part[...] for part in parts]
    steps, half = out_ref.shape[:2]
    rows = steps * half * out_ref.shape[2]
    weights, _, weight_sum = merge_rows(parts, rows)
    result = weigh(parts, weights / weight_sum, rows)
    result = result.astype(bf16).reshape(half, steps, *out_ref.shape[2:])
    for b in range(half):
        out_ref[:, b] = result[b]


def place_kernel(info_ref, own_ref, other_ref, out_ref):
    half = own_ref.shape[1]
    first = info_ref[0]
    out_ref[:, pl.ds(first, half)] = own_ref[...]
    out_ref[:, pl.ds(half - first, half)] = other_ref[...]


def on_device(
    query_heads, up_keys, up_values, latent_cache, new_latent, context_lengths, positions
):
    steps, requests, heads, query_width = query_heads.shape
    nope = up_keys.shape[1]
    width = up_keys.shape[2]
    key_width = latent_cache.shape[2]
    rope = key_width - width
    value_width = up_values.shape[2]
    cached = latent_cache.shape[1]
    owners = lax.axis_size("head")
    plane = lax.axis_size("z") * lax.axis_size("x")
    pairs = steps * requests
    half = requests // 2
    scale = float(query_width) ** (-0.5) * log2_e

    core = lax.axis_index("core")
    slot = lax.axis_index(("z", "x", "core", "head"))

    vmem = pl.BlockSpec(memory_space=pltpu.VMEM)
    smem = pl.BlockSpec(memory_space=pltpu.SMEM)
    small = pltpu.CompilerParams(vmem_limit_bytes=12 * 2**20)
    anywhere = pl.BlockSpec(memory_space=pltpu.HBM)
    wide = 640
    in_hbm = functools.partial(pltpu.with_memory_space_constraint, memory_space=pltpu.HBM)
    core32 = core.astype(jnp.int32)
    own_first = (core32 * half).reshape(1)
    other_first = (half - core32 * half).reshape(1)
    first_row = (slot.astype(jnp.int32) * cached).reshape(1)
    place = lax.axis_index(("z", "x")).astype(jnp.int32).reshape(1)
    chunk = half * steps * heads
    own_queries, sent_queries, new_keys, limits = pl.pallas_call(
        functools.partial(queries_kernel, steps),
        in_specs=[smem] * 4 + [anywhere] * 5,
        out_specs=[vmem] * 4,
        out_shape=(
            jax.ShapeDtypeStruct((requests, steps * heads, wide), bf16),
            jax.ShapeDtypeStruct((steps * heads, half * key_width), bf16),
            jax.ShapeDtypeStruct((pairs, key_width), bf16),
            jax.ShapeDtypeStruct((8, 128), jnp.int32),
        ),
        scratch_shapes=[
            pltpu.SMEM((requests,), jnp.int32),
            pltpu.SMEM((requests,), jnp.int32),
            pltpu.VMEM((pairs, heads, query_width), bf16),
            pltpu.VMEM(up_keys.shape, bf16),
            pltpu.VMEM(new_latent.shape, bf16),
            pltpu.VMEM((pairs, heads, width), f32),
            pltpu.SemaphoreType.DMA((8,)),
        ],
        compiler_params=pltpu.CompilerParams(vmem_limit_bytes=24 * 2**20),
        name="queries",
    )(
        other_first,
        own_first,
        first_row,
        place,
        in_hbm(positions),
        in_hbm(context_lengths),
        in_hbm(query_heads.reshape(pairs, heads, query_width)),
        in_hbm(up_keys),
        in_hbm(new_latent),
    )

    def over_head(array, k):
        return lax.ppermute(array, "head", [(i, i ^ k) for i in range(owners)])

    swap = [(0, 1), (1, 0)]
    partners = (2, 3, 1)
    got = [over_head(sent_queries, k) for k in partners]
    fresh = pl.pallas_call(
        functools.partial(fresh_kernel, scale, steps, heads),
        in_specs=[smem, vmem, vmem, vmem],
        out_specs=vmem,
        out_shape=jax.ShapeDtypeStruct((chunk + 16, width), bf16),
        compiler_params=small,
        cost_estimate=pl.CostEstimate(flops=10**9, bytes_accessed=4 * 10**6, transcendentals=0),
        name="fresh",
    )(own_first, limits, own_queries, new_keys)
    cache = jnp.swapaxes(latent_cache, 1, 2)
    staged_shape = pltpu.VMEM((half, key_width, cached), bf16)
    in_vmem = functools.partial(pltpu.with_memory_space_constraint, memory_space=pltpu.VMEM)
    staged = pl.pallas_call(
        stage_kernel,
        in_specs=[smem, anywhere],
        out_specs=vmem,
        out_shape=staged_shape,
        scratch_shapes=[pltpu.SemaphoreType.DMA((half,))],
        compiler_params=small,
        cost_estimate=pl.CostEstimate(flops=0, bytes_accessed=2 * half * key_width * cached, transcendentals=0),
        name="stage",
    )(other_first, in_hbm(cache))
    got[0], staged = lax.optimization_barrier((got[0], staged))
    passed = [lax.ppermute(g, "core", swap) for g in got]

    rows = owners * steps * heads

    def attend(first, got, keys):
        return pl.pallas_call(
            functools.partial(attention_kernel, scale),
            in_specs=[smem] + [vmem] * 6,
            out_specs=vmem,
            scratch_shapes=[pltpu.VMEM((half, owners, steps * heads, wide), bf16)]
            + [pltpu.VMEM((rows, cached), f32)] * half,
            out_shape=jax.ShapeDtypeStruct((owners, chunk, width + 128), bf16),
            compiler_params=pltpu.CompilerParams(vmem_limit_bytes=18 * 2**20),
            cost_estimate=pl.CostEstimate(
                flops=20 * half * rows * cached * (key_width + width),
                bytes_accessed=half * cached * key_width * 2,
                transcendentals=half * rows * cached,
            ),
            name="attention",
        )(first, limits, own_queries, *got, keys)

    other_part = lax.ppermute(attend(other_first, got, in_vmem(staged)), "core", swap)
    own_part = attend(own_first, passed, cache)
    sent = pl.pallas_call(
        pair_kernel,
        in_specs=[vmem] * 2,
        out_specs=[vmem] * owners,
        out_shape=[jax.ShapeDtypeStruct((chunk + 16, width), bf16)] * owners,
        compiler_params=small,
        name="pair_merge",
    )(other_part, own_part)
    arrived = [over_head(array, k) for array, k in zip(sent[1:], partners)]
    part = pl.pallas_call(
        functools.partial(project_kernel, heads),
        in_specs=[vmem] * 6,
        out_specs=vmem,
        out_shape=jax.ShapeDtypeStruct((chunk + 16, value_width), bf16),
        compiler_params=small,
        name="project",
    )(sent[0], *arrived, fresh, up_values)

    def over_plane(array, k):
        return lax.ppermute(array, ("z", "x"), [(i, i ^ k) for i in range(plane)])

    part = pl.pallas_call(
        middle_kernel,
        in_specs=[vmem] * 4,
        out_specs=vmem,
        out_shape=jax.ShapeDtypeStruct(part.shape, bf16),
        compiler_params=small,
        name="middle_merge",
    )(part, *[over_plane(part, k) for k in (2, 3, 1)])
    own = pl.pallas_call(
        finish_kernel,
        in_specs=[vmem] * 4,
        out_specs=vmem,
        out_shape=jax.ShapeDtypeStruct((steps, half, heads, value_width), bf16),
        compiler_params=small,
        name="finish",
    )(part, *[over_plane(part, k) for k in (8, 12, 4)])
    theirs = lax.ppermute(own, "core", swap)
    return pl.pallas_call(
        place_kernel,
        in_specs=[smem, vmem, vmem],
        out_specs=vmem,
        out_shape=jax.ShapeDtypeStruct((steps, requests, heads, value_width), bf16),
        compiler_params=small,
        name="place",
    )(own_first, own, theirs)


def solution(mesh):
    fine = Mesh(mesh.devices.reshape(4, 4, 2, 4), ("z", "x", "core", "head"))
    in_specs = (
        P(None, None, "head", None),
        P("head", None, None),
        P("head", None, None),
        P(None, ("z", "x", "core", "head"), None),
        P(),
        P(),
        P(),
    )
    out_specs = P(None, None, "head", None)
    return jax.shard_map(
        on_device, mesh=fine, in_specs=in_specs, out_specs=out_specs, check_vma=False
    )
```

```python
import functools

import jax
import jax.numpy as jnp
from jax import lax
from jax.experimental import pallas as pl
from jax.experimental.pallas import tpu as pltpu
from jax.sharding import Mesh, PartitionSpec as P

rope_base = 50000.0
masked_score = -1e30
lowest_max = -1e29
log2_e = 1.4426950408889634
bf16 = jnp.bfloat16
f32 = jnp.float32


def swap_halves(values):
    half = values.shape[-1] // 2
    return jnp.concatenate([values[..., half:], values[..., :half]], axis=-1)


def rope_tables(positions_ref, steps, width):
    requests = positions_ref.shape[0]
    pairs = steps * requests
    half = width // 2
    row = lax.broadcasted_iota(jnp.int32, (pairs, width), 0)
    lane = lax.broadcasted_iota(jnp.int32, (pairs, width), 1)
    where_at = row // requests
    for b in range(requests):
        where_at += jnp.where(row % requests == b, positions_ref[b], 0)
    counter = lax.broadcasted_iota(jnp.int32, (1, width), 1) % half
    inverse = jnp.zeros((1, width), f32)
    for i in range(half):
        inverse = jnp.where(counter == i, f32(rope_base ** (-2.0 * i / width)), inverse)
    angles = where_at.astype(f32) * inverse
    return jnp.cos(angles), jnp.where(lane < half, -1.0, 1.0) * jnp.sin(angles)


def queries_kernel(
    steps,
    info_ref,
    own_first_ref,
    row_ref,
    place_ref,
    positions_hbm,
    lengths_hbm,
    q_hbm,
    up_hbm,
    new_hbm,
    own_ref,
    sent_ref,
    keys_ref,
    limits_ref,
    positions,
    lengths,
    q,
    up,
    new,
    lat,
    sems,
):
    pairs, heads, _ = q.shape
    requests = pairs // steps
    nope, width = up.shape[1], up.shape[2]
    key_width = new.shape[2]
    fetches = [
        pltpu.make_async_copy(positions_hbm, positions, sems.at[0]),
        pltpu.make_async_copy(q_hbm, q, sems.at[1]),
        pltpu.make_async_copy(new_hbm, new, sems.at[2]),
        pltpu.make_async_copy(lengths_hbm, lengths, sems.at[3]),
    ]
    groups = 4
    share = heads // groups
    for g in range(groups):
        at = pl.ds(g * share, share)
        fetches.append(pltpu.make_async_copy(up_hbm.at[at], up.at[at], sems.at[4 + g]))
    for fetch in fetches:
        fetch.start()
    own_ref[:, :, key_width:] = jnp.zeros(own_ref.shape[:2] + (own_ref.shape[2] - key_width,), bf16)
    fetches[0].wait()
    cos, sin = rope_tables(positions, steps, key_width - width)
    fetches[1].wait()
    rope = q[:, :, nope:].astype(f32)
    rope = (rope * cos[:, None, :] + swap_halves(rope) * sin[:, None, :]).astype(bf16)
    for s in range(steps):
        for b in range(requests):
            own_ref[b, s * heads : (s + 1) * heads, width:key_width] = rope[s * requests + b]
    fetches[3].wait()
    line = lax.broadcasted_iota(jnp.int32, limits_ref.shape, 0)
    limits = jnp.zeros(limits_ref.shape, jnp.int32)
    for b in range(requests):
        limits = jnp.where(line == b, lengths[b] - row_ref[0], limits)
    limits_ref[...] = jnp.where(line == requests, place_ref[0], limits)
    fetches[2].wait()
    rows = jnp.concatenate([new[t].astype(f32) for t in range(steps)], axis=0)
    tail = rows[:, width:]
    tail = tail * cos + swap_halves(tail) * sin
    keys_ref[...] = jnp.concatenate([rows[:, :width], tail], axis=-1).astype(bf16)
    q_f32 = q[:, :, :nope].astype(f32)
    for h in range(heads):
        if h % share == 0:
            fetches[4 + h // share].wait()
        lat[:, h, :] = jnp.dot(q_f32[:, h, :].astype(bf16), up[h], preferred_element_type=f32)
    for s in range(steps):
        for b in range(requests):
            own_ref[b, s * heads : (s + 1) * heads, :width] = lat[s * requests + b].astype(bf16)
    packed = [own_ref[info_ref[0] + i] for i in range(sent_ref.shape[1] // key_width)]
    latents = [row[:, :width] for row in packed]
    sent_ref[...] = jnp.concatenate(latents + [row[:, width:key_width] for row in packed], axis=-1)


def split_stats(peak, weight_sum, rows):
    lane = lax.broadcasted_iota(jnp.int32, (rows, 128), 1)
    first = peak.astype(bf16).astype(f32)
    rest = peak - first
    second = rest.astype(bf16).astype(f32)
    third = rest - second
    sum_first = weight_sum.astype(bf16).astype(f32)
    sum_second = weight_sum - sum_first
    out = jnp.where(lane == 0, first, 0.0)
    out = jnp.where(lane == 1, second, out)
    out = jnp.where(lane == 2, third, out)
    out = jnp.where(lane == 3, sum_first, out)
    return jnp.where(lane == 4, sum_second, out)


def stage_kernel(info_ref, cache_hbm, out_ref, sems):
    copies = []
    for i in range(out_ref.shape[0]):
        copies.append(pltpu.make_async_copy(cache_hbm.at[info_ref[0] + i], out_ref.at[i], sems.at[i]))
    for copy in copies:
        copy.start()
    for copy in copies:
        copy.wait()


def stat_rows(peak, weight_sum):
    line = lax.broadcasted_iota(jnp.int32, (16, peak.shape[1]), 0)
    first = peak.astype(bf16).astype(f32)
    second = (peak - first).astype(bf16).astype(f32)
    sum_first = weight_sum.astype(bf16).astype(f32)
    stats = jnp.where(line == 0, first, 0.0)
    stats = jnp.where(line == 1, second, stats)
    stats = jnp.where(line == 2, peak - first - second, stats)
    stats = jnp.where(line == 3, sum_first, stats)
    return jnp.where(line == 4, weight_sum - sum_first, stats).astype(bf16)


def attention_kernel(scale, info_ref, limits_ref, own_ref, q1_ref, q2_ref, q3_ref, k_ref, out_ref, q_ref, *scores):
    count, owners, share, _ = q_ref.shape
    rows = owners * share
    key_width, cached = k_ref.shape[1:]
    width = out_ref.shape[2] - 128
    chunk = 1024
    first = info_ref[0]
    base = first if k_ref.shape[0] > count else 0
    q_ref[:, 0] = own_ref[pl.ds(first, count)]
    rope = key_width - width
    for k, packed_ref in enumerate((q1_ref, q2_ref, q3_ref)):
        for i in range(count):
            q_ref[i, 1 + k, :, :width] = packed_ref[:, i * width : (i + 1) * width]
            at = count * width + i * rope
            q_ref[i, 1 + k, :, width:key_width] = packed_ref[:, at : at + rope]

    tops = []
    for i in range(count):
        limit = limits_ref[pl.ds(first + i, 1), :1]
        queries = q_ref[i].reshape(rows, -1)[:, :key_width]
        top = jnp.full((rows, 128), lowest_max, f32)
        for c in range(0, cached, chunk):
            keys = k_ref[base + i, :, c : c + chunk]
            part = jnp.dot(queries, keys, preferred_element_type=f32) * scale
            column = lax.broadcasted_iota(jnp.int32, (1, chunk), 1) + c
            part = jnp.where(column < limit, part, masked_score)
            scores[i][:, c : c + chunk] = part
            for at in range(0, chunk, 128):
                top = jnp.maximum(top, part[:, at : at + 128])
        tops.append(jnp.max(top, axis=1, keepdims=True))

    for i in range(count):
        total = jnp.zeros((rows, 128), f32)
        for c in range(0, cached, chunk):
            weights = jnp.exp2(scores[i][:, c : c + chunk] - tops[i])
            for at in range(0, chunk, 128):
                total = total + weights[:, at : at + 128]
            part = lax.dot_general(
                weights.astype(bf16),
                k_ref[base + i, :width, c : c + chunk],
                (((1,), (1,)), ((), ())),
                preferred_element_type=f32,
            )
            mixed = part if c == 0 else mixed + part
        total = jnp.sum(total, axis=1, keepdims=True)
        at = slice(i * share, (i + 1) * share)
        out_ref[:, at, :width] = mixed.astype(bf16).reshape(owners, share, width)
        out_ref[:, at, width:] = split_stats(tops[i], total, rows).astype(bf16).reshape(owners, share, 128)


def fresh_kernel(scale, steps, heads, info_ref, limits_ref, own_ref, new_ref, out_ref):
    requests, share, _ = own_ref.shape
    key_width = new_ref.shape[1]
    width = out_ref.shape[1]
    requests_rows = out_ref.shape[0] - 16
    stats = []
    fresh = new_ref[...]
    shape = (share, fresh.shape[0])
    key = lax.broadcasted_iota(jnp.int32, shape, 1)
    step = (lax.broadcasted_iota(jnp.int32, shape, 0) // heads) % steps
    counted = limits_ref[requests : requests + 1, :1] == 0
    for i in range(requests_rows // share):
        request = info_ref[0] + i
        scores = (
            lax.dot_general(
                own_ref[request][:, :key_width], fresh, (((1,), (1,)), ((), ())), preferred_element_type=f32
            )
            * scale
        )
        visible = (key % requests == request) & (key // requests <= step) & counted
        scores = jnp.where(visible, scores, masked_score)
        top = jnp.maximum(jnp.max(scores, axis=1, keepdims=True), lowest_max)
        weights = jnp.exp2(scores - top)
        total = jnp.sum(weights, axis=1, keepdims=True)
        mixed = jnp.dot(weights.astype(bf16), fresh[:, :width], preferred_element_type=f32)
        out_ref[i * share : (i + 1) * share, :] = mixed.astype(bf16)
        stats.append(split_stats(top, total, share))
    out_ref[requests_rows:, :] = jnp.zeros((16, width), bf16)
    out_ref[requests_rows:, :requests_rows] = jnp.concatenate(stats, axis=0).T[:16].astype(bf16)


def merge_parts(parts, width):
    tops = []
    sums = []
    for part in parts:
        stat = part[:, width:].astype(f32)
        tops.append(stat[:, 0:1] + stat[:, 1:2] + stat[:, 2:3])
        sums.append(stat[:, 3:4] + stat[:, 4:5])
    peak = functools.reduce(jnp.maximum, tops)
    weights = [jnp.exp2(t - peak) for t in tops]
    weight_sum = sum(w * s for w, s in zip(weights, sums))
    merged = sum(w * part[:, :width].astype(f32) for w, part in zip(weights, parts))
    return merged, peak, weight_sum


def pair_kernel(first, a_ref, b_ref, *sent_refs):
    width = sent_refs[0].shape[1]
    rows = sent_refs[0].shape[0] - 16
    for owner, sent_ref in enumerate(sent_refs, first):
        merged, peak, weight_sum = merge_parts((a_ref[owner], b_ref[owner]), width)
        sent_ref[:rows, :] = merged.astype(bf16)
        sent_ref[rows:, :] = jnp.zeros((16, width), bf16)
        sent_ref[rows:, :rows] = split_stats(peak, weight_sum, rows).T[:16].astype(bf16)


def project_kernel(heads, *refs):
    *parts, up_ref, out_ref = refs
    parts = [part[...] for part in parts]
    rows = out_ref.shape[0] - 16
    weights, peak, weight_sum = merge_rows(parts, rows)
    mixed = weigh(parts, weights, rows)
    high = mixed.astype(bf16)
    both = jnp.concatenate([high, (mixed - high.astype(f32)).astype(bf16)], axis=0)
    value_width = out_ref.shape[1]
    head = lax.broadcasted_iota(jnp.int32, (rows, value_width), 0) % heads
    values = jnp.zeros((rows, value_width), f32)
    for h in range(0, heads, 2):
        two = jnp.concatenate([up_ref[h], up_ref[h + 1]], axis=1)
        part = jnp.dot(both, two, preferred_element_type=f32)
        part = part[:rows] + part[rows:]
        values = jnp.where(head == h, part[:, :value_width], values)
        values = jnp.where(head == h + 1, part[:, value_width:], values)
    out_ref[:rows, :] = values.astype(bf16)
    out_ref[rows:, :] = stat_rows(peak, weight_sum)


def merge_rows(parts, rows):
    tops = []
    sums = []
    for part in parts:
        stat = part[rows:, :rows].astype(f32)
        tops.append(stat[0:1] + stat[1:2] + stat[2:3])
        sums.append(stat[3:4] + stat[4:5])
    tops = jnp.concatenate(tops, axis=0)
    peak = jnp.max(tops, axis=0, keepdims=True)
    weights = jnp.exp2(tops - peak)
    weight_sum = jnp.sum(weights * jnp.concatenate(sums, axis=0), axis=0, keepdims=True)
    return weights, peak, weight_sum


def weigh(parts, weights, rows):
    spread = jnp.concatenate([weights, jnp.zeros((128 - len(parts), weights.shape[1]), f32)], axis=0).T
    return sum(part[:rows, :].astype(f32) * spread[:rows, i : i + 1] for i, part in enumerate(parts))


def middle_kernel(*refs):
    *parts, out_ref = refs
    parts = [part[...] for part in parts]
    rows = out_ref.shape[0] - 16
    weights, peak, weight_sum = merge_rows(parts, rows)
    out_ref[:rows, :] = weigh(parts, weights, rows).astype(bf16)
    out_ref[rows:, :] = stat_rows(peak, weight_sum)


def finish_kernel(*refs):
    *parts, out_ref = refs
    parts = [part[...] for part in parts]
    steps, half = out_ref.shape[:2]
    rows = steps * half * out_ref.shape[2]
    weights, _, weight_sum = merge_rows(parts, rows)
    result = weigh(parts, weights / weight_sum, rows)
    result = result.astype(bf16).reshape(half, steps, *out_ref.shape[2:])
    for b in range(half):
        out_ref[:, b] = result[b]


def place_kernel(info_ref, own_ref, other_ref, out_ref):
    half = own_ref.shape[1]
    first = info_ref[0]
    out_ref[:, pl.ds(first, half)] = own_ref[...]
    out_ref[:, pl.ds(half - first, half)] = other_ref[...]


def on_device(
    query_heads, up_keys, up_values, latent_cache, new_latent, context_lengths, positions
):
    steps, requests, heads, query_width = query_heads.shape
    nope = up_keys.shape[1]
    width = up_keys.shape[2]
    key_width = latent_cache.shape[2]
    rope = key_width - width
    value_width = up_values.shape[2]
    cached = latent_cache.shape[1]
    owners = lax.axis_size("head")
    plane = lax.axis_size("z") * lax.axis_size("x")
    pairs = steps * requests
    half = requests // 2
    scale = float(query_width) ** (-0.5) * log2_e

    core = lax.axis_index("core")
    slot = lax.axis_index(("z", "x", "core", "head"))

    vmem = pl.BlockSpec(memory_space=pltpu.VMEM)
    smem = pl.BlockSpec(memory_space=pltpu.SMEM)
    small = pltpu.CompilerParams(vmem_limit_bytes=12 * 2**20)
    anywhere = pl.BlockSpec(memory_space=pltpu.HBM)
    wide = 640
    in_hbm = functools.partial(pltpu.with_memory_space_constraint, memory_space=pltpu.HBM)
    core32 = core.astype(jnp.int32)
    own_first = (core32 * half).reshape(1)
    other_first = (half - core32 * half).reshape(1)
    first_row = (slot.astype(jnp.int32) * cached).reshape(1)
    place = lax.axis_index(("z", "x")).astype(jnp.int32).reshape(1)
    chunk = half * steps * heads
    own_queries, sent_queries, new_keys, limits = pl.pallas_call(
        functools.partial(queries_kernel, steps),
        in_specs=[smem] * 4 + [anywhere] * 5,
        out_specs=[vmem] * 4,
        out_shape=(
            jax.ShapeDtypeStruct((requests, steps * heads, wide), bf16),
            jax.ShapeDtypeStruct((steps * heads, half * key_width), bf16),
            jax.ShapeDtypeStruct((pairs, key_width), bf16),
            jax.ShapeDtypeStruct((8, 128), jnp.int32),
        ),
        scratch_shapes=[
            pltpu.SMEM((requests,), jnp.int32),
            pltpu.SMEM((requests,), jnp.int32),
            pltpu.VMEM((pairs, heads, query_width), bf16),
            pltpu.VMEM(up_keys.shape, bf16),
            pltpu.VMEM(new_latent.shape, bf16),
            pltpu.VMEM((pairs, heads, width), f32),
            pltpu.SemaphoreType.DMA((8,)),
        ],
        compiler_params=pltpu.CompilerParams(vmem_limit_bytes=24 * 2**20),
        name="queries",
    )(
        other_first,
        own_first,
        first_row,
        place,
        in_hbm(positions),
        in_hbm(context_lengths),
        in_hbm(query_heads.reshape(pairs, heads, query_width)),
        in_hbm(up_keys),
        in_hbm(new_latent),
    )

    def over_head(array, k):
        return lax.ppermute(array, "head", [(i, i ^ k) for i in range(owners)])

    swap = [(0, 1), (1, 0)]
    partners = (2, 3, 1)
    got = [over_head(sent_queries, k) for k in partners]
    fresh = pl.pallas_call(
        functools.partial(fresh_kernel, scale, steps, heads),
        in_specs=[smem, vmem, vmem, vmem],
        out_specs=vmem,
        out_shape=jax.ShapeDtypeStruct((chunk + 16, width), bf16),
        compiler_params=small,
        cost_estimate=pl.CostEstimate(flops=10**9, bytes_accessed=4 * 10**6, transcendentals=0),
        name="fresh",
    )(own_first, limits, own_queries, new_keys)
    cache = jnp.swapaxes(latent_cache, 1, 2)
    staged_shape = pltpu.VMEM((half, key_width, cached), bf16)
    in_vmem = functools.partial(pltpu.with_memory_space_constraint, memory_space=pltpu.VMEM)
    staged = pl.pallas_call(
        stage_kernel,
        in_specs=[smem, anywhere],
        out_specs=vmem,
        out_shape=staged_shape,
        scratch_shapes=[pltpu.SemaphoreType.DMA((half,))],
        compiler_params=small,
        cost_estimate=pl.CostEstimate(flops=0, bytes_accessed=2 * half * key_width * cached, transcendentals=0),
        name="stage",
    )(other_first, in_hbm(cache))
    got[0], staged = lax.optimization_barrier((got[0], staged))
    passed = [lax.ppermute(g, "core", swap) for g in got]

    rows = owners * steps * heads

    def attend(first, got, keys):
        return pl.pallas_call(
            functools.partial(attention_kernel, scale),
            in_specs=[smem] + [vmem] * 6,
            out_specs=vmem,
            scratch_shapes=[pltpu.VMEM((half, owners, steps * heads, wide), bf16)]
            + [pltpu.VMEM((rows, cached), f32)] * half,
            out_shape=jax.ShapeDtypeStruct((owners, chunk, width + 128), bf16),
            compiler_params=pltpu.CompilerParams(vmem_limit_bytes=18 * 2**20),
            cost_estimate=pl.CostEstimate(
                flops=20 * half * rows * cached * (key_width + width),
                bytes_accessed=half * cached * key_width * 2,
                transcendentals=half * rows * cached,
            ),
            name="attention",
        )(first, limits, own_queries, *got, keys)

    other_part = lax.ppermute(attend(other_first, got, in_vmem(staged)), "core", swap)
    own_part = attend(own_first, passed, cache)
    def pair(first, count):
        return pl.pallas_call(
            functools.partial(pair_kernel, first),
            in_specs=[vmem] * 2,
            out_specs=[vmem] * count,
            out_shape=[pltpu.VMEM((chunk + 16, width), bf16)] * count,
            compiler_params=small,
            name="pair_merge",
        )(other_part, own_part)

    sent = dict(zip(partners, pair(1, owners - 1)))
    arrived = [over_head(sent[k], k) for k in (1, 3, 2)]
    (kept,) = pair(0, 1)
    part = pl.pallas_call(
        functools.partial(project_kernel, heads),
        in_specs=[vmem] * 6,
        out_specs=vmem,
        out_shape=jax.ShapeDtypeStruct((chunk + 16, value_width), bf16),
        compiler_params=small,
        name="project",
    )(kept, *arrived, fresh, up_values)

    def over_plane(array, k):
        return lax.ppermute(array, ("z", "x"), [(i, i ^ k) for i in range(plane)])

    part = pl.pallas_call(
        middle_kernel,
        in_specs=[vmem] * 4,
        out_specs=vmem,
        out_shape=jax.ShapeDtypeStruct(part.shape, bf16),
        compiler_params=small,
        name="middle_merge",
    )(part, *[over_plane(part, k) for k in (2, 3, 1)])
    own = pl.pallas_call(
        finish_kernel,
        in_specs=[vmem] * 4,
        out_specs=vmem,
        out_shape=jax.ShapeDtypeStruct((steps, half, heads, value_width), bf16),
        compiler_params=small,
        name="finish",
    )(part, *[over_plane(part, k) for k in (8, 12, 4)])
    theirs = lax.ppermute(own, "core", swap)
    return pl.pallas_call(
        place_kernel,
        in_specs=[smem, vmem, vmem],
        out_specs=vmem,
        out_shape=jax.ShapeDtypeStruct((steps, requests, heads, value_width), bf16),
        compiler_params=small,
        name="place",
    )(own_first, own, theirs)


def solution(mesh):
    fine = Mesh(mesh.devices.reshape(4, 4, 2, 4), ("z", "x", "core", "head"))
    in_specs = (
        P(None, None, "head", None),
        P("head", None, None),
        P("head", None, None),
        P(None, ("z", "x", "core", "head"), None),
        P(),
        P(),
        P(),
    )
    out_specs = P(None, None, "head", None)
    return jax.shard_map(
        on_device, mesh=fine, in_specs=in_specs, out_specs=out_specs, check_vma=False
    )
```

```python
import functools

import jax
import jax.numpy as jnp
from jax import lax
from jax.experimental import pallas as pl
from jax.experimental.pallas import tpu as pltpu
from jax.sharding import Mesh, PartitionSpec as P

rope_base = 50000.0
masked_score = -1e30
lowest_max = -1e29
log2_e = 1.4426950408889634
bf16 = jnp.bfloat16
f32 = jnp.float32


def swap_halves(values):
    half = values.shape[-1] // 2
    return jnp.concatenate([values[..., half:], values[..., :half]], axis=-1)


def rope_tables(positions_ref, steps, width):
    requests = positions_ref.shape[0]
    pairs = steps * requests
    half = width // 2
    row = lax.broadcasted_iota(jnp.int32, (pairs, width), 0)
    lane = lax.broadcasted_iota(jnp.int32, (pairs, width), 1)
    where_at = row // requests
    for b in range(requests):
        where_at += jnp.where(row % requests == b, positions_ref[b], 0)
    counter = lax.broadcasted_iota(jnp.int32, (1, width), 1) % half
    inverse = jnp.zeros((1, width), f32)
    for i in range(half):
        inverse = jnp.where(counter == i, f32(rope_base ** (-2.0 * i / width)), inverse)
    angles = where_at.astype(f32) * inverse
    return jnp.cos(angles), jnp.where(lane < half, -1.0, 1.0) * jnp.sin(angles)


def queries_kernel(
    steps,
    info_ref,
    own_first_ref,
    row_ref,
    place_ref,
    positions_hbm,
    lengths_hbm,
    q_hbm,
    up_hbm,
    new_hbm,
    own_ref,
    sent_ref,
    keys_ref,
    limits_ref,
    positions,
    lengths,
    q,
    up,
    new,
    lat,
    sems,
):
    pairs, heads, _ = q.shape
    requests = pairs // steps
    nope, width = up.shape[1], up.shape[2]
    key_width = new.shape[2]
    fetches = [
        pltpu.make_async_copy(positions_hbm, positions, sems.at[0]),
        pltpu.make_async_copy(q_hbm, q, sems.at[1]),
        pltpu.make_async_copy(new_hbm, new, sems.at[2]),
        pltpu.make_async_copy(lengths_hbm, lengths, sems.at[3]),
    ]
    groups = 4
    share = heads // groups
    for g in range(groups):
        at = pl.ds(g * share, share)
        fetches.append(pltpu.make_async_copy(up_hbm.at[at], up.at[at], sems.at[4 + g]))
    for fetch in fetches:
        fetch.start()
    own_ref[:, :, key_width:] = jnp.zeros(own_ref.shape[:2] + (own_ref.shape[2] - key_width,), bf16)
    fetches[0].wait()
    cos, sin = rope_tables(positions, steps, key_width - width)
    fetches[1].wait()
    rope = q[:, :, nope:].astype(f32)
    rope = (rope * cos[:, None, :] + swap_halves(rope) * sin[:, None, :]).astype(bf16)
    for s in range(steps):
        for b in range(requests):
            own_ref[b, s * heads : (s + 1) * heads, width:key_width] = rope[s * requests + b]
    fetches[3].wait()
    line = lax.broadcasted_iota(jnp.int32, limits_ref.shape, 0)
    limits = jnp.zeros(limits_ref.shape, jnp.int32)
    for b in range(requests):
        limits = jnp.where(line == b, lengths[b] - row_ref[0], limits)
    limits_ref[...] = jnp.where(line == requests, place_ref[0], limits)
    fetches[2].wait()
    rows = jnp.concatenate([new[t].astype(f32) for t in range(steps)], axis=0)
    tail = rows[:, width:]
    tail = tail * cos + swap_halves(tail) * sin
    keys_ref[...] = jnp.concatenate([rows[:, :width], tail], axis=-1).astype(bf16)
    q_f32 = q[:, :, :nope].astype(f32)
    for h in range(heads):
        if h % share == 0:
            fetches[4 + h // share].wait()
        lat[:, h, :] = jnp.dot(q_f32[:, h, :].astype(bf16), up[h], preferred_element_type=f32)
    for s in range(steps):
        for b in range(requests):
            own_ref[b, s * heads : (s + 1) * heads, :width] = lat[s * requests + b].astype(bf16)
    packed = [own_ref[info_ref[0] + i] for i in range(sent_ref.shape[1] // key_width)]
    latents = [row[:, :width] for row in packed]
    sent_ref[...] = jnp.concatenate(latents + [row[:, width:key_width] for row in packed], axis=-1)


def split_stats(peak, weight_sum, rows):
    lane = lax.broadcasted_iota(jnp.int32, (rows, 128), 1)
    first = peak.astype(bf16).astype(f32)
    rest = peak - first
    second = rest.astype(bf16).astype(f32)
    third = rest - second
    sum_first = weight_sum.astype(bf16).astype(f32)
    sum_second = weight_sum - sum_first
    out = jnp.where(lane == 0, first, 0.0)
    out = jnp.where(lane == 1, second, out)
    out = jnp.where(lane == 2, third, out)
    out = jnp.where(lane == 3, sum_first, out)
    return jnp.where(lane == 4, sum_second, out)


def stage_kernel(info_ref, cache_hbm, out_ref, sems):
    copies = []
    for i in range(out_ref.shape[0]):
        copies.append(pltpu.make_async_copy(cache_hbm.at[info_ref[0] + i], out_ref.at[i], sems.at[i]))
    for copy in copies:
        copy.start()
    for copy in copies:
        copy.wait()


def stat_rows(peak, weight_sum):
    line = lax.broadcasted_iota(jnp.int32, (16, peak.shape[1]), 0)
    first = peak.astype(bf16).astype(f32)
    second = (peak - first).astype(bf16).astype(f32)
    sum_first = weight_sum.astype(bf16).astype(f32)
    stats = jnp.where(line == 0, first, 0.0)
    stats = jnp.where(line == 1, second, stats)
    stats = jnp.where(line == 2, peak - first - second, stats)
    stats = jnp.where(line == 3, sum_first, stats)
    return jnp.where(line == 4, weight_sum - sum_first, stats).astype(bf16)


def attention_kernel(scale, info_ref, limits_ref, own_ref, q1_ref, q2_ref, q3_ref, k_ref, out_ref, q_ref, *scores):
    count, owners, share, _ = q_ref.shape
    rows = owners * share
    key_width, cached = k_ref.shape[1:]
    width = out_ref.shape[2] - 128
    chunk = 1024
    first = info_ref[0]
    base = first if k_ref.shape[0] > count else 0
    q_ref[:, 0] = own_ref[pl.ds(first, count)]
    rope = key_width - width
    for k, packed_ref in enumerate((q1_ref, q2_ref, q3_ref)):
        for i in range(count):
            q_ref[i, 1 + k, :, :width] = packed_ref[:, i * width : (i + 1) * width]
            at = count * width + i * rope
            q_ref[i, 1 + k, :, width:key_width] = packed_ref[:, at : at + rope]

    tops = []
    for i in range(count):
        limit = limits_ref[pl.ds(first + i, 1), :1]
        queries = q_ref[i].reshape(rows, -1)[:, :key_width]
        top = jnp.full((rows, 128), lowest_max, f32)
        for c in range(0, cached, chunk):
            keys = k_ref[base + i, :, c : c + chunk]
            part = jnp.dot(queries, keys, preferred_element_type=f32) * scale
            column = lax.broadcasted_iota(jnp.int32, (1, chunk), 1) + c
            part = jnp.where(column < limit, part, masked_score)
            scores[i][:, c : c + chunk] = part
            for at in range(0, chunk, 128):
                top = jnp.maximum(top, part[:, at : at + 128])
        tops.append(jnp.max(top, axis=1, keepdims=True))

    for i in range(count):
        total = jnp.zeros((rows, 128), f32)
        for c in range(0, cached, chunk):
            weights = jnp.exp2(scores[i][:, c : c + chunk] - tops[i])
            for at in range(0, chunk, 128):
                total = total + weights[:, at : at + 128]
            part = lax.dot_general(
                weights.astype(bf16),
                k_ref[base + i, :width, c : c + chunk],
                (((1,), (1,)), ((), ())),
                preferred_element_type=f32,
            )
            mixed = part if c == 0 else mixed + part
        total = jnp.sum(total, axis=1, keepdims=True)
        at = slice(i * share, (i + 1) * share)
        out_ref[:, at, :width] = mixed.astype(bf16).reshape(owners, share, width)
        out_ref[:, at, width:] = split_stats(tops[i], total, rows).astype(bf16).reshape(owners, share, 128)


def fresh_kernel(scale, steps, heads, info_ref, limits_ref, own_ref, new_ref, out_ref):
    requests, share, _ = own_ref.shape
    key_width = new_ref.shape[1]
    width = out_ref.shape[1]
    requests_rows = out_ref.shape[0] - 16
    stats = []
    fresh = new_ref[...]
    shape = (share, fresh.shape[0])
    key = lax.broadcasted_iota(jnp.int32, shape, 1)
    step = (lax.broadcasted_iota(jnp.int32, shape, 0) // heads) % steps
    counted = limits_ref[requests : requests + 1, :1] == 0
    for i in range(requests_rows // share):
        request = info_ref[0] + i
        scores = (
            lax.dot_general(
                own_ref[request][:, :key_width], fresh, (((1,), (1,)), ((), ())), preferred_element_type=f32
            )
            * scale
        )
        visible = (key % requests == request) & (key // requests <= step) & counted
        scores = jnp.where(visible, scores, masked_score)
        top = jnp.maximum(jnp.max(scores, axis=1, keepdims=True), lowest_max)
        weights = jnp.exp2(scores - top)
        total = jnp.sum(weights, axis=1, keepdims=True)
        mixed = jnp.dot(weights.astype(bf16), fresh[:, :width], preferred_element_type=f32)
        out_ref[i * share : (i + 1) * share, :] = mixed.astype(bf16)
        stats.append(split_stats(top, total, share))
    out_ref[requests_rows:, :] = jnp.zeros((16, width), bf16)
    out_ref[requests_rows:, :requests_rows] = jnp.concatenate(stats, axis=0).T[:16].astype(bf16)


def merge_parts(parts, width):
    tops = []
    sums = []
    for part in parts:
        stat = part[:, width:].astype(f32)
        tops.append(stat[:, 0:1] + stat[:, 1:2] + stat[:, 2:3])
        sums.append(stat[:, 3:4] + stat[:, 4:5])
    peak = functools.reduce(jnp.maximum, tops)
    weights = [jnp.exp2(t - peak) for t in tops]
    weight_sum = sum(w * s for w, s in zip(weights, sums))
    merged = sum(w * part[:, :width].astype(f32) for w, part in zip(weights, parts))
    return merged, peak, weight_sum


def pair_kernel(first, a_ref, b_ref, *sent_refs):
    width = sent_refs[0].shape[1]
    rows = sent_refs[0].shape[0] - 16
    for owner, sent_ref in enumerate(sent_refs, first):
        merged, peak, weight_sum = merge_parts((a_ref[owner], b_ref[owner]), width)
        sent_ref[:rows, :] = merged.astype(bf16)
        sent_ref[rows:, :] = jnp.zeros((16, width), bf16)
        sent_ref[rows:, :rows] = split_stats(peak, weight_sum, rows).T[:16].astype(bf16)


def project_kernel(heads, *refs):
    *parts, up_ref, out_ref = refs
    parts = [part[...] for part in parts]
    rows = out_ref.shape[0] - 16
    weights, peak, weight_sum = merge_rows(parts, rows)
    mixed = weigh(parts, weights, rows)
    high = mixed.astype(bf16)
    both = jnp.concatenate([high, (mixed - high.astype(f32)).astype(bf16)], axis=0)
    value_width = out_ref.shape[1]
    head = lax.broadcasted_iota(jnp.int32, (rows, value_width), 0) % heads
    values = jnp.zeros((rows, value_width), f32)
    for h in range(0, heads, 2):
        two = jnp.concatenate([up_ref[h], up_ref[h + 1]], axis=1)
        part = jnp.dot(both, two, preferred_element_type=f32)
        part = part[:rows] + part[rows:]
        values = jnp.where(head == h, part[:, :value_width], values)
        values = jnp.where(head == h + 1, part[:, value_width:], values)
    out_ref[:rows, :] = values.astype(bf16)
    out_ref[rows:, :] = stat_rows(peak, weight_sum)


def merge_rows(parts, rows):
    tops = []
    sums = []
    for part in parts:
        stat = part[rows:, :rows].astype(f32)
        tops.append(stat[0:1] + stat[1:2] + stat[2:3])
        sums.append(stat[3:4] + stat[4:5])
    tops = jnp.concatenate(tops, axis=0)
    peak = jnp.max(tops, axis=0, keepdims=True)
    weights = jnp.exp2(tops - peak)
    weight_sum = jnp.sum(weights * jnp.concatenate(sums, axis=0), axis=0, keepdims=True)
    return weights, peak, weight_sum


def weigh(parts, weights, rows):
    spread = jnp.concatenate([weights, jnp.zeros((128 - len(parts), weights.shape[1]), f32)], axis=0).T
    return sum(part[:rows, :].astype(f32) * spread[:rows, i : i + 1] for i, part in enumerate(parts))


def middle_kernel(*refs):
    *parts, out_ref = refs
    parts = [part[...] for part in parts]
    rows = out_ref.shape[0] - 16
    weights, peak, weight_sum = merge_rows(parts, rows)
    out_ref[:rows, :] = weigh(parts, weights, rows).astype(bf16)
    out_ref[rows:, :] = stat_rows(peak, weight_sum)


def finish_kernel(*refs):
    *parts, out_ref = refs
    parts = [part[...] for part in parts]
    steps, half = out_ref.shape[:2]
    rows = steps * half * out_ref.shape[2]
    weights, _, weight_sum = merge_rows(parts, rows)
    result = weigh(parts, weights / weight_sum, rows)
    result = result.astype(bf16).reshape(half, steps, *out_ref.shape[2:])
    for b in range(half):
        out_ref[:, b] = result[b]


def place_kernel(info_ref, own_ref, other_ref, out_ref):
    half = own_ref.shape[1]
    first = info_ref[0]
    out_ref[:, pl.ds(first, half)] = own_ref[...]
    out_ref[:, pl.ds(half - first, half)] = other_ref[...]


def on_device(
    query_heads, up_keys, up_values, latent_cache, new_latent, context_lengths, positions
):
    steps, requests, heads, query_width = query_heads.shape
    nope = up_keys.shape[1]
    width = up_keys.shape[2]
    key_width = latent_cache.shape[2]
    rope = key_width - width
    value_width = up_values.shape[2]
    cached = latent_cache.shape[1]
    owners = lax.axis_size("head")
    plane = lax.axis_size("z") * lax.axis_size("x")
    pairs = steps * requests
    half = requests // 2
    scale = float(query_width) ** (-0.5) * log2_e

    core = lax.axis_index("core")
    slot = lax.axis_index(("z", "x", "core", "head"))

    vmem = pl.BlockSpec(memory_space=pltpu.VMEM)
    smem = pl.BlockSpec(memory_space=pltpu.SMEM)
    small = pltpu.CompilerParams(vmem_limit_bytes=12 * 2**20)
    anywhere = pl.BlockSpec(memory_space=pltpu.HBM)
    wide = 640
    in_hbm = functools.partial(pltpu.with_memory_space_constraint, memory_space=pltpu.HBM)
    core32 = core.astype(jnp.int32)
    own_first = (core32 * half).reshape(1)
    other_first = (half - core32 * half).reshape(1)
    first_row = (slot.astype(jnp.int32) * cached).reshape(1)
    place = lax.axis_index(("z", "x")).astype(jnp.int32).reshape(1)
    chunk = half * steps * heads
    own_queries, sent_queries, new_keys, limits = pl.pallas_call(
        functools.partial(queries_kernel, steps),
        in_specs=[smem] * 4 + [anywhere] * 5,
        out_specs=[vmem] * 4,
        out_shape=(
            jax.ShapeDtypeStruct((requests, steps * heads, wide), bf16),
            jax.ShapeDtypeStruct((steps * heads, half * key_width), bf16),
            jax.ShapeDtypeStruct((pairs, key_width), bf16),
            jax.ShapeDtypeStruct((8, 128), jnp.int32),
        ),
        scratch_shapes=[
            pltpu.SMEM((requests,), jnp.int32),
            pltpu.SMEM((requests,), jnp.int32),
            pltpu.VMEM((pairs, heads, query_width), bf16),
            pltpu.VMEM(up_keys.shape, bf16),
            pltpu.VMEM(new_latent.shape, bf16),
            pltpu.VMEM((pairs, heads, width), f32),
            pltpu.SemaphoreType.DMA((8,)),
        ],
        compiler_params=pltpu.CompilerParams(vmem_limit_bytes=24 * 2**20),
        name="queries",
    )(
        other_first,
        own_first,
        first_row,
        place,
        in_hbm(positions),
        in_hbm(context_lengths),
        in_hbm(query_heads.reshape(pairs, heads, query_width)),
        in_hbm(up_keys),
        in_hbm(new_latent),
    )

    def over_head(array, k):
        return lax.ppermute(array, "head", [(i, i ^ k) for i in range(owners)])

    swap = [(0, 1), (1, 0)]
    partners = (2, 3, 1)
    got = [over_head(sent_queries, k) for k in partners]
    fresh = pl.pallas_call(
        functools.partial(fresh_kernel, scale, steps, heads),
        in_specs=[smem, vmem, vmem, vmem],
        out_specs=vmem,
        out_shape=jax.ShapeDtypeStruct((chunk + 16, width), bf16),
        compiler_params=small,
        cost_estimate=pl.CostEstimate(flops=10**9, bytes_accessed=4 * 10**6, transcendentals=0),
        name="fresh",
    )(own_first, limits, own_queries, new_keys)
    cache = jnp.swapaxes(latent_cache, 1, 2)
    staged_shape = pltpu.VMEM((half, key_width, cached), bf16)
    in_vmem = functools.partial(pltpu.with_memory_space_constraint, memory_space=pltpu.VMEM)
    staged = pl.pallas_call(
        stage_kernel,
        in_specs=[smem, anywhere],
        out_specs=vmem,
        out_shape=staged_shape,
        scratch_shapes=[pltpu.SemaphoreType.DMA((half,))],
        compiler_params=small,
        cost_estimate=pl.CostEstimate(flops=0, bytes_accessed=2 * half * key_width * cached, transcendentals=0),
        name="stage",
    )(other_first, in_hbm(cache))
    got[0], staged = lax.optimization_barrier((got[0], staged))
    passed = [lax.ppermute(g, "core", swap) for g in got]

    rows = owners * steps * heads

    def attend(first, got, keys):
        return pl.pallas_call(
            functools.partial(attention_kernel, scale),
            in_specs=[smem] + [vmem] * 6,
            out_specs=vmem,
            scratch_shapes=[pltpu.VMEM((half, owners, steps * heads, wide), bf16)]
            + [pltpu.VMEM((rows, cached), f32)] * half,
            out_shape=jax.ShapeDtypeStruct((owners, chunk, width + 128), bf16),
            compiler_params=pltpu.CompilerParams(vmem_limit_bytes=18 * 2**20),
            cost_estimate=pl.CostEstimate(
                flops=20 * half * rows * cached * (key_width + width),
                bytes_accessed=half * cached * key_width * 2,
                transcendentals=half * rows * cached,
            ),
            name="attention",
        )(first, limits, own_queries, *got, keys)

    other_part = lax.ppermute(attend(other_first, got, in_vmem(staged)), "core", swap)
    own_part = attend(own_first, passed, cache)
    def pair(first, count):
        return pl.pallas_call(
            functools.partial(pair_kernel, first),
            in_specs=[vmem] * 2,
            out_specs=[vmem] * count,
            out_shape=[pltpu.VMEM((chunk + 16, width), bf16)] * count,
            compiler_params=small,
            name="pair_merge",
        )(other_part, own_part)

    sent = dict(zip(partners, pair(1, owners - 1)))
    arrived = [over_head(sent[k], k) for k in (1, 3, 2)]
    (kept,) = pair(0, 1)
    part = pl.pallas_call(
        functools.partial(project_kernel, heads),
        in_specs=[vmem] * 6,
        out_specs=vmem,
        out_shape=jax.ShapeDtypeStruct((chunk + 16, value_width), bf16),
        compiler_params=small,
        name="project",
    )(kept, *arrived, fresh, up_values)

    def over_plane(array, k):
        return lax.ppermute(array, ("z", "x"), [(i, i ^ k) for i in range(plane)])

    part = pl.pallas_call(
        middle_kernel,
        in_specs=[vmem] * 4,
        out_specs=vmem,
        out_shape=jax.ShapeDtypeStruct(part.shape, bf16),
        compiler_params=small,
        name="middle_merge",
    )(part, *[over_plane(part, k) for k in (8, 12, 4)])
    own = pl.pallas_call(
        finish_kernel,
        in_specs=[vmem] * 4,
        out_specs=vmem,
        out_shape=jax.ShapeDtypeStruct((steps, half, heads, value_width), bf16),
        compiler_params=small,
        name="finish",
    )(part, *[over_plane(part, k) for k in (2, 3, 1)])
    theirs = lax.ppermute(own, "core", swap)
    return pl.pallas_call(
        place_kernel,
        in_specs=[smem, vmem, vmem],
        out_specs=vmem,
        out_shape=jax.ShapeDtypeStruct((steps, requests, heads, value_width), bf16),
        compiler_params=small,
        name="place",
    )(own_first, own, theirs)


def solution(mesh):
    fine = Mesh(mesh.devices.reshape(4, 4, 2, 4), ("z", "x", "core", "head"))
    in_specs = (
        P(None, None, "head", None),
        P("head", None, None),
        P("head", None, None),
        P(None, ("z", "x", "core", "head"), None),
        P(),
        P(),
        P(),
    )
    out_specs = P(None, None, "head", None)
    return jax.shard_map(
        on_device, mesh=fine, in_specs=in_specs, out_specs=out_specs, check_vma=False
    )
```

```python
import functools

import jax
import jax.numpy as jnp
from jax import lax
from jax.experimental import pallas as pl
from jax.experimental.pallas import tpu as pltpu
from jax.sharding import Mesh, PartitionSpec as P

rope_base = 50000.0
masked_score = -1e30
lowest_max = -1e29
log2_e = 1.4426950408889634
bf16 = jnp.bfloat16
f32 = jnp.float32


def swap_halves(values):
    half = values.shape[-1] // 2
    return jnp.concatenate([values[..., half:], values[..., :half]], axis=-1)


def rope_tables(positions_ref, steps, width):
    requests = positions_ref.shape[0]
    pairs = steps * requests
    half = width // 2
    row = lax.broadcasted_iota(jnp.int32, (pairs, width), 0)
    lane = lax.broadcasted_iota(jnp.int32, (pairs, width), 1)
    where_at = row // requests
    for b in range(requests):
        where_at += jnp.where(row % requests == b, positions_ref[b], 0)
    counter = lax.broadcasted_iota(jnp.int32, (1, width), 1) % half
    inverse = jnp.zeros((1, width), f32)
    for i in range(half):
        inverse = jnp.where(counter == i, f32(rope_base ** (-2.0 * i / width)), inverse)
    angles = where_at.astype(f32) * inverse
    return jnp.cos(angles), jnp.where(lane < half, -1.0, 1.0) * jnp.sin(angles)


def queries_kernel(
    steps,
    info_ref,
    own_first_ref,
    row_ref,
    place_ref,
    positions_hbm,
    lengths_hbm,
    q_hbm,
    up_hbm,
    new_hbm,
    own_ref,
    sent_ref,
    keys_ref,
    limits_ref,
    positions,
    lengths,
    q,
    up,
    new,
    lat,
    sems,
):
    pairs, heads, _ = q.shape
    requests = pairs // steps
    nope, width = up.shape[1], up.shape[2]
    key_width = new.shape[2]
    fetches = [
        pltpu.make_async_copy(positions_hbm, positions, sems.at[0]),
        pltpu.make_async_copy(q_hbm, q, sems.at[1]),
        pltpu.make_async_copy(new_hbm, new, sems.at[2]),
        pltpu.make_async_copy(lengths_hbm, lengths, sems.at[3]),
    ]
    groups = 4
    share = heads // groups
    for g in range(groups):
        at = pl.ds(g * share, share)
        fetches.append(pltpu.make_async_copy(up_hbm.at[at], up.at[at], sems.at[4 + g]))
    for fetch in fetches:
        fetch.start()
    own_ref[:, :, key_width:] = jnp.zeros(own_ref.shape[:2] + (own_ref.shape[2] - key_width,), bf16)
    fetches[0].wait()
    cos, sin = rope_tables(positions, steps, key_width - width)
    fetches[1].wait()
    rope = q[:, :, nope:].astype(f32)
    rope = (rope * cos[:, None, :] + swap_halves(rope) * sin[:, None, :]).astype(bf16)
    for s in range(steps):
        for b in range(requests):
            own_ref[b, s * heads : (s + 1) * heads, width:key_width] = rope[s * requests + b]
    fetches[3].wait()
    line = lax.broadcasted_iota(jnp.int32, limits_ref.shape, 0)
    limits = jnp.zeros(limits_ref.shape, jnp.int32)
    for b in range(requests):
        limits = jnp.where(line == b, lengths[b] - row_ref[0], limits)
    limits_ref[...] = jnp.where(line == requests, place_ref[0], limits)
    fetches[2].wait()
    rows = jnp.concatenate([new[t].astype(f32) for t in range(steps)], axis=0)
    tail = rows[:, width:]
    tail = tail * cos + swap_halves(tail) * sin
    keys_ref[...] = jnp.concatenate([rows[:, :width], tail], axis=-1).astype(bf16)
    q_f32 = q[:, :, :nope].astype(f32)
    for h in range(heads):
        if h % share == 0:
            fetches[4 + h // share].wait()
        lat[:, h, :] = jnp.dot(q_f32[:, h, :].astype(bf16), up[h], preferred_element_type=f32)
    for s in range(steps):
        for b in range(requests):
            own_ref[b, s * heads : (s + 1) * heads, :width] = lat[s * requests + b].astype(bf16)
    packed = [own_ref[info_ref[0] + i] for i in range(sent_ref.shape[1] // key_width)]
    latents = [row[:, :width] for row in packed]
    sent_ref[...] = jnp.concatenate(latents + [row[:, width:key_width] for row in packed], axis=-1)


def split_stats(peak, weight_sum, rows):
    lane = lax.broadcasted_iota(jnp.int32, (rows, 128), 1)
    first = peak.astype(bf16).astype(f32)
    rest = peak - first
    second = rest.astype(bf16).astype(f32)
    third = rest - second
    sum_first = weight_sum.astype(bf16).astype(f32)
    sum_second = weight_sum - sum_first
    out = jnp.where(lane == 0, first, 0.0)
    out = jnp.where(lane == 1, second, out)
    out = jnp.where(lane == 2, third, out)
    out = jnp.where(lane == 3, sum_first, out)
    return jnp.where(lane == 4, sum_second, out)


def stage_kernel(info_ref, cache_hbm, out_ref, sems):
    copies = []
    for i in range(out_ref.shape[0]):
        copies.append(pltpu.make_async_copy(cache_hbm.at[info_ref[0] + i], out_ref.at[i], sems.at[i]))
    for copy in copies:
        copy.start()
    for copy in copies:
        copy.wait()


def stat_rows(peak, weight_sum):
    line = lax.broadcasted_iota(jnp.int32, (16, peak.shape[1]), 0)
    first = peak.astype(bf16).astype(f32)
    second = (peak - first).astype(bf16).astype(f32)
    sum_first = weight_sum.astype(bf16).astype(f32)
    stats = jnp.where(line == 0, first, 0.0)
    stats = jnp.where(line == 1, second, stats)
    stats = jnp.where(line == 2, peak - first - second, stats)
    stats = jnp.where(line == 3, sum_first, stats)
    return jnp.where(line == 4, weight_sum - sum_first, stats).astype(bf16)


def attention_kernel(scale, info_ref, limits_ref, own_ref, q1_ref, q2_ref, q3_ref, k_ref, out_ref, q_ref, *scores):
    count, owners, share, _ = q_ref.shape
    rows = owners * share
    key_width, cached = k_ref.shape[1:]
    width = out_ref.shape[2] - 128
    chunk = 1024
    first = info_ref[0]
    base = first if k_ref.shape[0] > count else 0
    q_ref[:, 0] = own_ref[pl.ds(first, count)]
    rope = key_width - width
    for k, packed_ref in enumerate((q1_ref, q2_ref, q3_ref)):
        for i in range(count):
            q_ref[i, 1 + k, :, :width] = packed_ref[:, i * width : (i + 1) * width]
            at = count * width + i * rope
            q_ref[i, 1 + k, :, width:key_width] = packed_ref[:, at : at + rope]

    tops = []
    for i in range(count):
        limit = limits_ref[pl.ds(first + i, 1), :1]
        queries = q_ref[i].reshape(rows, -1)[:, :key_width]
        top = jnp.full((rows, 128), lowest_max, f32)
        for c in range(0, cached, chunk):
            keys = k_ref[base + i, :, c : c + chunk]
            part = jnp.dot(queries, keys, preferred_element_type=f32) * scale
            column = lax.broadcasted_iota(jnp.int32, (1, chunk), 1) + c
            part = jnp.where(column < limit, part, masked_score)
            scores[i][:, c : c + chunk] = part
            for at in range(0, chunk, 128):
                top = jnp.maximum(top, part[:, at : at + 128])
        tops.append(jnp.max(top, axis=1, keepdims=True))

    for i in range(count):
        total = jnp.zeros((rows, 128), f32)
        for c in range(0, cached, chunk):
            weights = jnp.exp2(scores[i][:, c : c + chunk] - tops[i])
            for at in range(0, chunk, 128):
                total = total + weights[:, at : at + 128]
            part = lax.dot_general(
                weights.astype(bf16),
                k_ref[base + i, :width, c : c + chunk],
                (((1,), (1,)), ((), ())),
                preferred_element_type=f32,
            )
            mixed = part if c == 0 else mixed + part
        total = jnp.sum(total, axis=1, keepdims=True)
        at = slice(i * share, (i + 1) * share)
        out_ref[:, at, :width] = mixed.astype(bf16).reshape(owners, share, width)
        out_ref[:, at, width:] = split_stats(tops[i], total, rows).astype(bf16).reshape(owners, share, 128)


def fresh_kernel(scale, steps, heads, info_ref, limits_ref, own_ref, new_ref, out_ref):
    requests, share, _ = own_ref.shape
    key_width = new_ref.shape[1]
    width = out_ref.shape[1]
    requests_rows = out_ref.shape[0] - 16
    stats = []
    fresh = new_ref[...]
    shape = (share, fresh.shape[0])
    key = lax.broadcasted_iota(jnp.int32, shape, 1)
    step = (lax.broadcasted_iota(jnp.int32, shape, 0) // heads) % steps
    counted = limits_ref[requests : requests + 1, :1] == 0
    for i in range(requests_rows // share):
        request = info_ref[0] + i
        scores = (
            lax.dot_general(
                own_ref[request][:, :key_width], fresh, (((1,), (1,)), ((), ())), preferred_element_type=f32
            )
            * scale
        )
        visible = (key % requests == request) & (key // requests <= step) & counted
        scores = jnp.where(visible, scores, masked_score)
        top = jnp.maximum(jnp.max(scores, axis=1, keepdims=True), lowest_max)
        weights = jnp.exp2(scores - top)
        total = jnp.sum(weights, axis=1, keepdims=True)
        mixed = jnp.dot(weights.astype(bf16), fresh[:, :width], preferred_element_type=f32)
        out_ref[i * share : (i + 1) * share, :] = mixed.astype(bf16)
        stats.append(split_stats(top, total, share))
    out_ref[requests_rows:, :] = jnp.zeros((16, width), bf16)
    out_ref[requests_rows:, :requests_rows] = jnp.concatenate(stats, axis=0).T[:16].astype(bf16)


def merge_parts(parts, width):
    tops = []
    sums = []
    for part in parts:
        stat = part[:, width:].astype(f32)
        tops.append(stat[:, 0:1] + stat[:, 1:2] + stat[:, 2:3])
        sums.append(stat[:, 3:4] + stat[:, 4:5])
    peak = functools.reduce(jnp.maximum, tops)
    weights = [jnp.exp2(t - peak) for t in tops]
    weight_sum = sum(w * s for w, s in zip(weights, sums))
    merged = sum(w * part[:, :width].astype(f32) for w, part in zip(weights, parts))
    return merged, peak, weight_sum


def pair_kernel(first, a_ref, b_ref, *sent_refs):
    width = sent_refs[0].shape[1]
    rows = sent_refs[0].shape[0] - 16
    for owner, sent_ref in enumerate(sent_refs, first):
        merged, peak, weight_sum = merge_parts((a_ref[owner], b_ref[owner]), width)
        sent_ref[:rows, :] = merged.astype(bf16)
        sent_ref[rows:, :] = jnp.zeros((16, width), bf16)
        sent_ref[rows:, :rows] = split_stats(peak, weight_sum, rows).T[:16].astype(bf16)


def project_kernel(heads, *refs):
    *parts, up_ref, out_ref = refs
    parts = [part[...] for part in parts]
    rows = out_ref.shape[0] - 16
    weights, peak, weight_sum = merge_rows(parts, rows)
    mixed = weigh(parts, weights, rows)
    high = mixed.astype(bf16)
    both = jnp.concatenate([high, (mixed - high.astype(f32)).astype(bf16)], axis=0)
    value_width = out_ref.shape[1]
    head = lax.broadcasted_iota(jnp.int32, (rows, value_width), 0) % heads
    values = jnp.zeros((rows, value_width), f32)
    for h in range(0, heads, 2):
        two = jnp.concatenate([up_ref[h], up_ref[h + 1]], axis=1)
        part = jnp.dot(both, two, preferred_element_type=f32)
        part = part[:rows] + part[rows:]
        values = jnp.where(head == h, part[:, :value_width], values)
        values = jnp.where(head == h + 1, part[:, value_width:], values)
    out_ref[:rows, :] = values.astype(bf16)
    out_ref[rows:, :] = stat_rows(peak, weight_sum)


def merge_rows(parts, rows):
    tops = []
    sums = []
    for part in parts:
        stat = part[rows:, :rows].astype(f32)
        tops.append(stat[0:1] + stat[1:2] + stat[2:3])
        sums.append(stat[3:4] + stat[4:5])
    tops = jnp.concatenate(tops, axis=0)
    peak = jnp.max(tops, axis=0, keepdims=True)
    weights = jnp.exp2(tops - peak)
    weight_sum = jnp.sum(weights * jnp.concatenate(sums, axis=0), axis=0, keepdims=True)
    return weights, peak, weight_sum


def weigh(parts, weights, rows):
    spread = jnp.concatenate([weights, jnp.zeros((128 - len(parts), weights.shape[1]), f32)], axis=0).T
    return sum(part[:rows, :].astype(f32) * spread[:rows, i : i + 1] for i, part in enumerate(parts))


def middle_kernel(*refs):
    *parts, out_ref = refs
    parts = [part[...] for part in parts]
    rows = out_ref.shape[0] - 16
    weights, peak, weight_sum = merge_rows(parts, rows)
    out_ref[:rows, :] = weigh(parts, weights, rows).astype(bf16)
    out_ref[rows:, :] = stat_rows(peak, weight_sum)


def finish_kernel(*refs):
    *parts, out_ref = refs
    parts = [part[...] for part in parts]
    steps, half = out_ref.shape[:2]
    rows = steps * half * out_ref.shape[2]
    weights, _, weight_sum = merge_rows(parts, rows)
    result = weigh(parts, weights / weight_sum, rows)
    result = result.astype(bf16).reshape(half, steps, *out_ref.shape[2:])
    for b in range(half):
        out_ref[:, b] = result[b]


def place_kernel(info_ref, own_ref, other_ref, out_ref):
    half = own_ref.shape[1]
    first = info_ref[0]
    out_ref[:, pl.ds(first, half)] = own_ref[...]
    out_ref[:, pl.ds(half - first, half)] = other_ref[...]


def on_device(
    query_heads, up_keys, up_values, latent_cache, new_latent, context_lengths, positions
):
    steps, requests, heads, query_width = query_heads.shape
    nope = up_keys.shape[1]
    width = up_keys.shape[2]
    key_width = latent_cache.shape[2]
    rope = key_width - width
    value_width = up_values.shape[2]
    cached = latent_cache.shape[1]
    owners = lax.axis_size("head")
    plane = lax.axis_size("z") * lax.axis_size("x")
    pairs = steps * requests
    half = requests // 2
    scale = float(query_width) ** (-0.5) * log2_e

    core = lax.axis_index("core")
    slot = lax.axis_index(("z", "x", "core", "head"))

    vmem = pl.BlockSpec(memory_space=pltpu.VMEM)
    smem = pl.BlockSpec(memory_space=pltpu.SMEM)
    small = pltpu.CompilerParams(vmem_limit_bytes=12 * 2**20)
    anywhere = pl.BlockSpec(memory_space=pltpu.HBM)
    wide = 640
    in_hbm = functools.partial(pltpu.with_memory_space_constraint, memory_space=pltpu.HBM)
    core32 = core.astype(jnp.int32)
    own_first = (core32 * half).reshape(1)
    other_first = (half - core32 * half).reshape(1)
    first_row = (slot.astype(jnp.int32) * cached).reshape(1)
    place = lax.axis_index(("z", "x")).astype(jnp.int32).reshape(1)
    chunk = half * steps * heads
    own_queries, sent_queries, new_keys, limits = pl.pallas_call(
        functools.partial(queries_kernel, steps),
        in_specs=[smem] * 4 + [anywhere] * 5,
        out_specs=[vmem] * 4,
        out_shape=(
            jax.ShapeDtypeStruct((requests, steps * heads, wide), bf16),
            jax.ShapeDtypeStruct((steps * heads, half * key_width), bf16),
            jax.ShapeDtypeStruct((pairs, key_width), bf16),
            jax.ShapeDtypeStruct((8, 128), jnp.int32),
        ),
        scratch_shapes=[
            pltpu.SMEM((requests,), jnp.int32),
            pltpu.SMEM((requests,), jnp.int32),
            pltpu.VMEM((pairs, heads, query_width), bf16),
            pltpu.VMEM(up_keys.shape, bf16),
            pltpu.VMEM(new_latent.shape, bf16),
            pltpu.VMEM((pairs, heads, width), f32),
            pltpu.SemaphoreType.DMA((8,)),
        ],
        compiler_params=pltpu.CompilerParams(vmem_limit_bytes=24 * 2**20),
        name="queries",
    )(
        other_first,
        own_first,
        first_row,
        place,
        in_hbm(positions),
        in_hbm(context_lengths),
        in_hbm(query_heads.reshape(pairs, heads, query_width)),
        in_hbm(up_keys),
        in_hbm(new_latent),
    )

    def over_head(array, k):
        return lax.ppermute(array, "head", [(i, i ^ k) for i in range(owners)])

    swap = [(0, 1), (1, 0)]
    partners = (2, 3, 1)
    got = [over_head(sent_queries, k) for k in partners]
    fresh = pl.pallas_call(
        functools.partial(fresh_kernel, scale, steps, heads),
        in_specs=[smem, vmem, vmem, vmem],
        out_specs=vmem,
        out_shape=jax.ShapeDtypeStruct((chunk + 16, width), bf16),
        compiler_params=small,
        cost_estimate=pl.CostEstimate(flops=10**9, bytes_accessed=4 * 10**6, transcendentals=0),
        name="fresh",
    )(own_first, limits, own_queries, new_keys)
    cache = jnp.swapaxes(latent_cache, 1, 2)
    staged_shape = pltpu.VMEM((half, key_width, cached), bf16)
    in_vmem = functools.partial(pltpu.with_memory_space_constraint, memory_space=pltpu.VMEM)
    staged = pl.pallas_call(
        stage_kernel,
        in_specs=[smem, anywhere],
        out_specs=vmem,
        out_shape=staged_shape,
        scratch_shapes=[pltpu.SemaphoreType.DMA((half,))],
        compiler_params=small,
        cost_estimate=pl.CostEstimate(flops=0, bytes_accessed=2 * half * key_width * cached, transcendentals=0),
        name="stage",
    )(other_first, in_hbm(cache))
    got[0], staged = lax.optimization_barrier((got[0], staged))
    passed = [lax.ppermute(g, "core", swap) for g in got]

    rows = owners * steps * heads

    def attend(first, got, keys):
        return pl.pallas_call(
            functools.partial(attention_kernel, scale),
            in_specs=[smem] + [vmem] * 6,
            out_specs=vmem,
            scratch_shapes=[pltpu.VMEM((half, owners, steps * heads, wide), bf16)]
            + [pltpu.VMEM((rows, cached), f32)] * half,
            out_shape=jax.ShapeDtypeStruct((owners, chunk, width + 128), bf16),
            compiler_params=pltpu.CompilerParams(vmem_limit_bytes=18 * 2**20),
            cost_estimate=pl.CostEstimate(
                flops=20 * half * rows * cached * (key_width + width),
                bytes_accessed=half * cached * key_width * 2,
                transcendentals=half * rows * cached,
            ),
            name="attention",
        )(first, limits, own_queries, *got, keys)

    other_part = lax.ppermute(attend(other_first, got, in_vmem(staged)), "core", swap)
    own_part = attend(own_first, passed, cache)
    def pair(first, count):
        return pl.pallas_call(
            functools.partial(pair_kernel, first),
            in_specs=[vmem] * 2,
            out_specs=[vmem] * count,
            out_shape=[pltpu.VMEM((chunk + 16, width), bf16)] * count,
            compiler_params=small,
            name="pair_merge",
        )(other_part, own_part)

    sent = dict(zip(partners, pair(1, owners - 1)))
    arrived = [over_head(sent[k], k) for k in (1, 3, 2)]
    (kept,) = pair(0, 1)
    part = pl.pallas_call(
        functools.partial(project_kernel, heads),
        in_specs=[vmem] * 6,
        out_specs=vmem,
        out_shape=jax.ShapeDtypeStruct((chunk + 16, value_width), bf16),
        compiler_params=small,
        name="project",
    )(kept, *arrived, fresh, up_values)

    def crossing(array, axis):
        size = lax.axis_size(axis)
        sides = [(i, c) for i in range(size) for c in range(2)]
        got = [
            lax.ppermute(array, (axis, "core"), [(2 * i + c, 2 * (i ^ k) + 1 - c) for i, c in sides])
            for k in (2, 3, 1)
        ]
        return got + [lax.ppermute(array, "core", swap)]

    part = pl.pallas_call(
        middle_kernel,
        in_specs=[vmem] * 4,
        out_specs=vmem,
        out_shape=jax.ShapeDtypeStruct(part.shape, bf16),
        compiler_params=small,
        name="middle_merge",
    )(*crossing(part, "z"))
    own = pl.pallas_call(
        finish_kernel,
        in_specs=[vmem] * 4,
        out_specs=vmem,
        out_shape=jax.ShapeDtypeStruct((steps, half, heads, value_width), bf16),
        compiler_params=small,
        name="finish",
    )(*crossing(part, "x"))
    theirs = lax.ppermute(own, "core", swap)
    return pl.pallas_call(
        place_kernel,
        in_specs=[smem, vmem, vmem],
        out_specs=vmem,
        out_shape=jax.ShapeDtypeStruct((steps, requests, heads, value_width), bf16),
        compiler_params=small,
        name="place",
    )(own_first, own, theirs)


def solution(mesh):
    fine = Mesh(mesh.devices.reshape(4, 4, 2, 4), ("z", "x", "core", "head"))
    in_specs = (
        P(None, None, "head", None),
        P("head", None, None),
        P("head", None, None),
        P(None, ("z", "x", "core", "head"), None),
        P(),
        P(),
        P(),
    )
    out_specs = P(None, None, "head", None)
    return jax.shard_map(
        on_device, mesh=fine, in_specs=in_specs, out_specs=out_specs, check_vma=False
    )
```

```python
import functools

import jax
import jax.numpy as jnp
from jax import lax
from jax.experimental import pallas as pl
from jax.experimental.pallas import tpu as pltpu
from jax.sharding import Mesh, PartitionSpec as P

rope_base = 50000.0
masked_score = -1e30
lowest_max = -1e29
log2_e = 1.4426950408889634
bf16 = jnp.bfloat16
f32 = jnp.float32


def swap_halves(values):
    half = values.shape[-1] // 2
    return jnp.concatenate([values[..., half:], values[..., :half]], axis=-1)


def rope_tables(positions_ref, steps, width):
    requests = positions_ref.shape[0]
    pairs = steps * requests
    half = width // 2
    row = lax.broadcasted_iota(jnp.int32, (pairs, width), 0)
    lane = lax.broadcasted_iota(jnp.int32, (pairs, width), 1)
    where_at = row // requests
    for b in range(requests):
        where_at += jnp.where(row % requests == b, positions_ref[b], 0)
    counter = lax.broadcasted_iota(jnp.int32, (1, width), 1) % half
    inverse = jnp.zeros((1, width), f32)
    for i in range(half):
        inverse = jnp.where(counter == i, f32(rope_base ** (-2.0 * i / width)), inverse)
    angles = where_at.astype(f32) * inverse
    return jnp.cos(angles), jnp.where(lane < half, -1.0, 1.0) * jnp.sin(angles)


def queries_kernel(
    steps,
    info_ref,
    own_first_ref,
    row_ref,
    place_ref,
    positions_hbm,
    lengths_hbm,
    q_hbm,
    up_hbm,
    new_hbm,
    own_ref,
    sent_ref,
    keys_ref,
    limits_ref,
    positions,
    lengths,
    q,
    up,
    new,
    lat,
    sems,
):
    pairs, heads, _ = q.shape
    requests = pairs // steps
    nope, width = up.shape[1], up.shape[2]
    key_width = new.shape[2]
    fetches = [
        pltpu.make_async_copy(positions_hbm, positions, sems.at[0]),
        pltpu.make_async_copy(q_hbm, q, sems.at[1]),
        pltpu.make_async_copy(new_hbm, new, sems.at[2]),
        pltpu.make_async_copy(lengths_hbm, lengths, sems.at[3]),
    ]
    groups = 4
    share = heads // groups
    for g in range(groups):
        at = pl.ds(g * share, share)
        fetches.append(pltpu.make_async_copy(up_hbm.at[at], up.at[at], sems.at[4 + g]))
    for fetch in fetches:
        fetch.start()
    own_ref[:, :, key_width:] = jnp.zeros(own_ref.shape[:2] + (own_ref.shape[2] - key_width,), bf16)
    fetches[0].wait()
    cos, sin = rope_tables(positions, steps, key_width - width)
    fetches[1].wait()
    rope = q[:, :, nope:].astype(f32)
    rope = (rope * cos[:, None, :] + swap_halves(rope) * sin[:, None, :]).astype(bf16)
    for s in range(steps):
        for b in range(requests):
            own_ref[b, s * heads : (s + 1) * heads, width:key_width] = rope[s * requests + b]
    fetches[3].wait()
    line = lax.broadcasted_iota(jnp.int32, limits_ref.shape, 0)
    limits = jnp.zeros(limits_ref.shape, jnp.int32)
    for b in range(requests):
        limits = jnp.where(line == b, lengths[b] - row_ref[0], limits)
    limits_ref[...] = jnp.where(line == requests, place_ref[0], limits)
    fetches[2].wait()
    rows = jnp.concatenate([new[t].astype(f32) for t in range(steps)], axis=0)
    tail = rows[:, width:]
    tail = tail * cos + swap_halves(tail) * sin
    keys_ref[...] = jnp.concatenate([rows[:, :width], tail], axis=-1).astype(bf16)
    q_f32 = q[:, :, :nope].astype(f32)
    for h in range(heads):
        if h % share == 0:
            fetches[4 + h // share].wait()
        lat[:, h, :] = jnp.dot(q_f32[:, h, :].astype(bf16), up[h], preferred_element_type=f32)
    for s in range(steps):
        for b in range(requests):
            own_ref[b, s * heads : (s + 1) * heads, :width] = lat[s * requests + b].astype(bf16)
    packed = [own_ref[info_ref[0] + i] for i in range(sent_ref.shape[1] // key_width)]
    latents = [row[:, :width] for row in packed]
    sent_ref[...] = jnp.concatenate(latents + [row[:, width:key_width] for row in packed], axis=-1)


def split_stats(peak, weight_sum, rows):
    lane = lax.broadcasted_iota(jnp.int32, (rows, 128), 1)
    first = peak.astype(bf16).astype(f32)
    rest = peak - first
    second = rest.astype(bf16).astype(f32)
    third = rest - second
    sum_first = weight_sum.astype(bf16).astype(f32)
    sum_second = weight_sum - sum_first
    out = jnp.where(lane == 0, first, 0.0)
    out = jnp.where(lane == 1, second, out)
    out = jnp.where(lane == 2, third, out)
    out = jnp.where(lane == 3, sum_first, out)
    return jnp.where(lane == 4, sum_second, out)


def stage_kernel(info_ref, cache_hbm, out_ref, sems):
    copies = []
    for i in range(out_ref.shape[0]):
        copies.append(pltpu.make_async_copy(cache_hbm.at[info_ref[0] + i], out_ref.at[i], sems.at[i]))
    for copy in copies:
        copy.start()
    for copy in copies:
        copy.wait()


def stat_rows(peak, weight_sum):
    line = lax.broadcasted_iota(jnp.int32, (16, peak.shape[1]), 0)
    first = peak.astype(bf16).astype(f32)
    second = (peak - first).astype(bf16).astype(f32)
    sum_first = weight_sum.astype(bf16).astype(f32)
    stats = jnp.where(line == 0, first, 0.0)
    stats = jnp.where(line == 1, second, stats)
    stats = jnp.where(line == 2, peak - first - second, stats)
    stats = jnp.where(line == 3, sum_first, stats)
    return jnp.where(line == 4, weight_sum - sum_first, stats).astype(bf16)


def attention_kernel(scale, info_ref, limits_ref, own_ref, q1_ref, q2_ref, q3_ref, k_ref, out_ref, q_ref, *scores):
    count, owners, share, _ = q_ref.shape
    rows = owners * share
    key_width, cached = k_ref.shape[1:]
    width = out_ref.shape[2] - 128
    chunk = 1024
    first = info_ref[0]
    base = first if k_ref.shape[0] > count else 0
    q_ref[:, 0] = own_ref[pl.ds(first, count)]
    rope = key_width - width
    for k, packed_ref in enumerate((q1_ref, q2_ref, q3_ref)):
        for i in range(count):
            q_ref[i, 1 + k, :, :width] = packed_ref[:, i * width : (i + 1) * width]
            at = count * width + i * rope
            q_ref[i, 1 + k, :, width:key_width] = packed_ref[:, at : at + rope]

    tops = []
    for i in range(count):
        limit = limits_ref[pl.ds(first + i, 1), :1]
        queries = q_ref[i].reshape(rows, -1)[:, :key_width]
        top = jnp.full((rows, 128), lowest_max, f32)
        for c in range(0, cached, chunk):
            keys = k_ref[base + i, :, c : c + chunk]
            part = jnp.dot(queries, keys, preferred_element_type=f32) * scale
            column = lax.broadcasted_iota(jnp.int32, (1, chunk), 1) + c
            part = jnp.where(column < limit, part, masked_score)
            scores[i][:, c : c + chunk] = part
            for at in range(0, chunk, 128):
                top = jnp.maximum(top, part[:, at : at + 128])
        tops.append(jnp.max(top, axis=1, keepdims=True))

    for i in range(count):
        total = jnp.zeros((rows, 128), f32)
        for c in range(0, cached, chunk):
            weights = jnp.exp2(scores[i][:, c : c + chunk] - tops[i])
            for at in range(0, chunk, 128):
                total = total + weights[:, at : at + 128]
            part = lax.dot_general(
                weights.astype(bf16),
                k_ref[base + i, :width, c : c + chunk],
                (((1,), (1,)), ((), ())),
                preferred_element_type=f32,
            )
            mixed = part if c == 0 else mixed + part
        total = jnp.sum(total, axis=1, keepdims=True)
        at = slice(i * share, (i + 1) * share)
        out_ref[:, at, :width] = mixed.astype(bf16).reshape(owners, share, width)
        out_ref[:, at, width:] = split_stats(tops[i], total, rows).astype(bf16).reshape(owners, share, 128)


def fresh_kernel(scale, steps, heads, info_ref, limits_ref, own_ref, new_ref, out_ref):
    requests, share, _ = own_ref.shape
    key_width = new_ref.shape[1]
    width = out_ref.shape[1]
    requests_rows = out_ref.shape[0] - 16
    stats = []
    fresh = new_ref[...]
    shape = (share, fresh.shape[0])
    key = lax.broadcasted_iota(jnp.int32, shape, 1)
    step = (lax.broadcasted_iota(jnp.int32, shape, 0) // heads) % steps
    counted = limits_ref[requests : requests + 1, :1] == 0
    for i in range(requests_rows // share):
        request = info_ref[0] + i
        scores = (
            lax.dot_general(
                own_ref[request][:, :key_width], fresh, (((1,), (1,)), ((), ())), preferred_element_type=f32
            )
            * scale
        )
        visible = (key % requests == request) & (key // requests <= step) & counted
        scores = jnp.where(visible, scores, masked_score)
        top = jnp.maximum(jnp.max(scores, axis=1, keepdims=True), lowest_max)
        weights = jnp.exp2(scores - top)
        total = jnp.sum(weights, axis=1, keepdims=True)
        mixed = jnp.dot(weights.astype(bf16), fresh[:, :width], preferred_element_type=f32)
        out_ref[i * share : (i + 1) * share, :] = mixed.astype(bf16)
        stats.append(split_stats(top, total, share))
    out_ref[requests_rows:, :] = jnp.zeros((16, width), bf16)
    out_ref[requests_rows:, :requests_rows] = jnp.concatenate(stats, axis=0).T[:16].astype(bf16)


def merge_parts(parts, width):
    tops = []
    sums = []
    for part in parts:
        stat = part[:, width:].astype(f32)
        tops.append(stat[:, 0:1] + stat[:, 1:2] + stat[:, 2:3])
        sums.append(stat[:, 3:4] + stat[:, 4:5])
    peak = functools.reduce(jnp.maximum, tops)
    weights = [jnp.exp2(t - peak) for t in tops]
    weight_sum = sum(w * s for w, s in zip(weights, sums))
    merged = sum(w * part[:, :width].astype(f32) for w, part in zip(weights, parts))
    return merged, peak, weight_sum


def pair_kernel(first, a_ref, b_ref, *sent_refs):
    width = sent_refs[0].shape[1]
    rows = sent_refs[0].shape[0] - 16
    for owner, sent_ref in enumerate(sent_refs, first):
        merged, peak, weight_sum = merge_parts((a_ref[owner], b_ref[owner]), width)
        sent_ref[:rows, :] = merged.astype(bf16)
        sent_ref[rows:, :] = jnp.zeros((16, width), bf16)
        sent_ref[rows:, :rows] = split_stats(peak, weight_sum, rows).T[:16].astype(bf16)


def project_kernel(heads, *refs):
    *parts, up_ref, out_ref = refs
    parts = [part[...] for part in parts]
    rows = out_ref.shape[0] - 16
    weights, peak, weight_sum = merge_rows(parts, rows)
    mixed = weigh(parts, weights, rows)
    high = mixed.astype(bf16)
    both = jnp.concatenate([high, (mixed - high.astype(f32)).astype(bf16)], axis=0)
    value_width = out_ref.shape[1]
    head = lax.broadcasted_iota(jnp.int32, (rows, value_width), 0) % heads
    values = jnp.zeros((rows, value_width), f32)
    for h in range(0, heads, 2):
        two = jnp.concatenate([up_ref[h], up_ref[h + 1]], axis=1)
        part = jnp.dot(both, two, preferred_element_type=f32)
        part = part[:rows] + part[rows:]
        values = jnp.where(head == h, part[:, :value_width], values)
        values = jnp.where(head == h + 1, part[:, value_width:], values)
    out_ref[:rows, :] = values.astype(bf16)
    out_ref[rows:, :] = stat_rows(peak, weight_sum)


def merge_rows(parts, rows):
    tops = []
    sums = []
    for part in parts:
        stat = part[rows:, :rows].astype(f32)
        tops.append(stat[0:1] + stat[1:2] + stat[2:3])
        sums.append(stat[3:4] + stat[4:5])
    tops = jnp.concatenate(tops, axis=0)
    peak = jnp.max(tops, axis=0, keepdims=True)
    weights = jnp.exp2(tops - peak)
    weight_sum = jnp.sum(weights * jnp.concatenate(sums, axis=0), axis=0, keepdims=True)
    return weights, peak, weight_sum


def weigh(parts, weights, rows):
    spread = jnp.concatenate([weights, jnp.zeros((128 - len(parts), weights.shape[1]), f32)], axis=0).T
    return sum(part[:rows, :].astype(f32) * spread[:rows, i : i + 1] for i, part in enumerate(parts))


def middle_kernel(*refs):
    *parts, out_ref = refs
    parts = [part[...] for part in parts]
    rows = out_ref.shape[0] - 16
    weights, peak, weight_sum = merge_rows(parts, rows)
    out_ref[:rows, :] = weigh(parts, weights, rows).astype(bf16)
    out_ref[rows:, :] = stat_rows(peak, weight_sum)


def finish_kernel(*refs):
    *parts, out_ref = refs
    parts = [part[...] for part in parts]
    steps, half = out_ref.shape[:2]
    rows = steps * half * out_ref.shape[2]
    weights, _, weight_sum = merge_rows(parts, rows)
    result = weigh(parts, weights / weight_sum, rows)
    result = result.astype(bf16).reshape(half, steps, *out_ref.shape[2:])
    for b in range(half):
        out_ref[:, b] = result[b]


def place_kernel(info_ref, own_ref, other_ref, out_ref):
    half = own_ref.shape[1]
    first = info_ref[0]
    out_ref[:, pl.ds(first, half)] = own_ref[...]
    out_ref[:, pl.ds(half - first, half)] = other_ref[...]


def on_device(
    query_heads, up_keys, up_values, latent_cache, new_latent, context_lengths, positions
):
    steps, requests, heads, query_width = query_heads.shape
    nope = up_keys.shape[1]
    width = up_keys.shape[2]
    key_width = latent_cache.shape[2]
    rope = key_width - width
    value_width = up_values.shape[2]
    cached = latent_cache.shape[1]
    owners = lax.axis_size("head")
    plane = lax.axis_size("z") * lax.axis_size("x")
    pairs = steps * requests
    half = requests // 2
    scale = float(query_width) ** (-0.5) * log2_e

    core = lax.axis_index("core")
    slot = lax.axis_index(("z", "x", "core", "head"))

    vmem = pl.BlockSpec(memory_space=pltpu.VMEM)
    smem = pl.BlockSpec(memory_space=pltpu.SMEM)
    small = pltpu.CompilerParams(vmem_limit_bytes=12 * 2**20)
    anywhere = pl.BlockSpec(memory_space=pltpu.HBM)
    wide = 640
    in_hbm = functools.partial(pltpu.with_memory_space_constraint, memory_space=pltpu.HBM)
    core32 = core.astype(jnp.int32)
    own_first = (core32 * half).reshape(1)
    other_first = (half - core32 * half).reshape(1)
    first_row = (slot.astype(jnp.int32) * cached).reshape(1)
    place = lax.axis_index(("z", "x")).astype(jnp.int32).reshape(1)
    chunk = half * steps * heads
    own_queries, sent_queries, new_keys, limits = pl.pallas_call(
        functools.partial(queries_kernel, steps),
        in_specs=[smem] * 4 + [anywhere] * 5,
        out_specs=[vmem] * 4,
        out_shape=(
            jax.ShapeDtypeStruct((requests, steps * heads, wide), bf16),
            jax.ShapeDtypeStruct((steps * heads, half * key_width), bf16),
            jax.ShapeDtypeStruct((pairs, key_width), bf16),
            jax.ShapeDtypeStruct((8, 128), jnp.int32),
        ),
        scratch_shapes=[
            pltpu.SMEM((requests,), jnp.int32),
            pltpu.SMEM((requests,), jnp.int32),
            pltpu.VMEM((pairs, heads, query_width), bf16),
            pltpu.VMEM(up_keys.shape, bf16),
            pltpu.VMEM(new_latent.shape, bf16),
            pltpu.VMEM((pairs, heads, width), f32),
            pltpu.SemaphoreType.DMA((8,)),
        ],
        compiler_params=pltpu.CompilerParams(vmem_limit_bytes=24 * 2**20),
        name="queries",
    )(
        other_first,
        own_first,
        first_row,
        place,
        in_hbm(positions),
        in_hbm(context_lengths),
        in_hbm(query_heads.reshape(pairs, heads, query_width)),
        in_hbm(up_keys),
        in_hbm(new_latent),
    )

    def over_head(array, k):
        return lax.ppermute(array, "head", [(i, i ^ k) for i in range(owners)])

    swap = [(0, 1), (1, 0)]
    partners = (2, 3, 1)
    got = [over_head(sent_queries, k) for k in partners]
    fresh = pl.pallas_call(
        functools.partial(fresh_kernel, scale, steps, heads),
        in_specs=[smem, vmem, vmem, vmem],
        out_specs=vmem,
        out_shape=jax.ShapeDtypeStruct((chunk + 16, width), bf16),
        compiler_params=small,
        cost_estimate=pl.CostEstimate(flops=10**9, bytes_accessed=4 * 10**6, transcendentals=0),
        name="fresh",
    )(own_first, limits, own_queries, new_keys)
    cache = jnp.swapaxes(latent_cache, 1, 2)
    staged_shape = pltpu.VMEM((half, key_width, cached), bf16)
    in_vmem = functools.partial(pltpu.with_memory_space_constraint, memory_space=pltpu.VMEM)
    staged = pl.pallas_call(
        stage_kernel,
        in_specs=[smem, anywhere],
        out_specs=vmem,
        out_shape=staged_shape,
        scratch_shapes=[pltpu.SemaphoreType.DMA((half,))],
        compiler_params=small,
        cost_estimate=pl.CostEstimate(flops=0, bytes_accessed=2 * half * key_width * cached, transcendentals=0),
        name="stage",
    )(other_first, in_hbm(cache))
    got[0], staged = lax.optimization_barrier((got[0], staged))
    passed = [lax.ppermute(g, "core", swap) for g in got]

    rows = owners * steps * heads

    def attend(first, got, keys):
        return pl.pallas_call(
            functools.partial(attention_kernel, scale),
            in_specs=[smem] + [vmem] * 6,
            out_specs=vmem,
            scratch_shapes=[pltpu.VMEM((half, owners, steps * heads, wide), bf16)]
            + [pltpu.VMEM((rows, cached), f32)] * half,
            out_shape=jax.ShapeDtypeStruct((owners, chunk, width + 128), bf16),
            compiler_params=pltpu.CompilerParams(vmem_limit_bytes=18 * 2**20),
            cost_estimate=pl.CostEstimate(
                flops=20 * half * rows * cached * (key_width + width),
                bytes_accessed=half * cached * key_width * 2,
                transcendentals=half * rows * cached,
            ),
            name="attention",
        )(first, limits, own_queries, *got, keys)

    other_part = lax.ppermute(attend(other_first, got, in_vmem(staged)), "core", swap)
    own_part = attend(own_first, passed, cache)
    def pair(first, count):
        return pl.pallas_call(
            functools.partial(pair_kernel, first),
            in_specs=[vmem] * 2,
            out_specs=[vmem] * count,
            out_shape=[pltpu.VMEM((chunk + 16, width), bf16)] * count,
            compiler_params=small,
            name="pair_merge",
        )(other_part, own_part)

    sent = dict(zip(partners, pair(1, owners - 1)))
    arrived = [over_head(sent[k], k) for k in (2, 3, 1)]
    (kept,) = pair(0, 1)
    part = pl.pallas_call(
        functools.partial(project_kernel, heads),
        in_specs=[vmem] * 6,
        out_specs=vmem,
        out_shape=jax.ShapeDtypeStruct((chunk + 16, value_width), bf16),
        compiler_params=small,
        name="project",
    )(kept, *arrived, fresh, up_values)

    def crossing(array, axis):
        size = lax.axis_size(axis)
        sides = [(i, c) for i in range(size) for c in range(2)]
        got = [
            lax.ppermute(array, (axis, "core"), [(2 * i + c, 2 * (i ^ k) + 1 - c) for i, c in sides])
            for k in (2, 3, 1)
        ]
        return got + [lax.ppermute(array, "core", swap)]

    part = pl.pallas_call(
        middle_kernel,
        in_specs=[vmem] * 4,
        out_specs=vmem,
        out_shape=jax.ShapeDtypeStruct(part.shape, bf16),
        compiler_params=small,
        name="middle_merge",
    )(*crossing(part, "z"))
    own = pl.pallas_call(
        finish_kernel,
        in_specs=[vmem] * 4,
        out_specs=vmem,
        out_shape=jax.ShapeDtypeStruct((steps, half, heads, value_width), bf16),
        compiler_params=small,
        name="finish",
    )(*crossing(part, "x"))
    theirs = lax.ppermute(own, "core", swap)
    return pl.pallas_call(
        place_kernel,
        in_specs=[smem, vmem, vmem],
        out_specs=vmem,
        out_shape=jax.ShapeDtypeStruct((steps, requests, heads, value_width), bf16),
        compiler_params=small,
        name="place",
    )(own_first, own, theirs)


def solution(mesh):
    fine = Mesh(mesh.devices.reshape(4, 4, 2, 4), ("z", "x", "core", "head"))
    in_specs = (
        P(None, None, "head", None),
        P("head", None, None),
        P("head", None, None),
        P(None, ("z", "x", "core", "head"), None),
        P(),
        P(),
        P(),
    )
    out_specs = P(None, None, "head", None)
    return jax.shard_map(
        on_device, mesh=fine, in_specs=in_specs, out_specs=out_specs, check_vma=False
    )
```

```python
import functools

import jax
import jax.numpy as jnp
from jax import lax
from jax.experimental import pallas as pl
from jax.experimental.pallas import tpu as pltpu
from jax.sharding import Mesh, PartitionSpec as P

rope_base = 50000.0
masked_score = -1e30
lowest_max = -1e29
log2_e = 1.4426950408889634
bf16 = jnp.bfloat16
f32 = jnp.float32


def swap_halves(values):
    half = values.shape[-1] // 2
    return jnp.concatenate([values[..., half:], values[..., :half]], axis=-1)


def rope_tables(positions_ref, steps, width):
    requests = positions_ref.shape[0]
    pairs = steps * requests
    half = width // 2
    row = lax.broadcasted_iota(jnp.int32, (pairs, width), 0)
    lane = lax.broadcasted_iota(jnp.int32, (pairs, width), 1)
    where_at = row // requests
    for b in range(requests):
        where_at += jnp.where(row % requests == b, positions_ref[b], 0)
    counter = lax.broadcasted_iota(jnp.int32, (1, width), 1) % half
    inverse = jnp.zeros((1, width), f32)
    for i in range(half):
        inverse = jnp.where(counter == i, f32(rope_base ** (-2.0 * i / width)), inverse)
    angles = where_at.astype(f32) * inverse
    return jnp.cos(angles), jnp.where(lane < half, -1.0, 1.0) * jnp.sin(angles)


def queries_kernel(
    steps,
    info_ref,
    own_first_ref,
    row_ref,
    place_ref,
    positions_hbm,
    lengths_hbm,
    q_hbm,
    up_hbm,
    new_hbm,
    own_ref,
    sent_ref,
    keys_ref,
    limits_ref,
    positions,
    lengths,
    q,
    up,
    new,
    lat,
    sems,
):
    pairs, heads, _ = q.shape
    requests = pairs // steps
    nope, width = up.shape[1], up.shape[2]
    key_width = new.shape[2]
    fetches = [
        pltpu.make_async_copy(positions_hbm, positions, sems.at[0]),
        pltpu.make_async_copy(q_hbm, q, sems.at[1]),
        pltpu.make_async_copy(new_hbm, new, sems.at[2]),
        pltpu.make_async_copy(lengths_hbm, lengths, sems.at[3]),
    ]
    groups = 4
    share = heads // groups
    for g in range(groups):
        at = pl.ds(g * share, share)
        fetches.append(pltpu.make_async_copy(up_hbm.at[at], up.at[at], sems.at[4 + g]))
    for fetch in fetches:
        fetch.start()
    own_ref[:, :, key_width:] = jnp.zeros(own_ref.shape[:2] + (own_ref.shape[2] - key_width,), bf16)
    fetches[0].wait()
    cos, sin = rope_tables(positions, steps, key_width - width)
    fetches[1].wait()
    rope = q[:, :, nope:].astype(f32)
    rope = (rope * cos[:, None, :] + swap_halves(rope) * sin[:, None, :]).astype(bf16)
    for s in range(steps):
        for b in range(requests):
            own_ref[b, s * heads : (s + 1) * heads, width:key_width] = rope[s * requests + b]
    fetches[3].wait()
    line = lax.broadcasted_iota(jnp.int32, limits_ref.shape, 0)
    limits = jnp.zeros(limits_ref.shape, jnp.int32)
    for b in range(requests):
        limits = jnp.where(line == b, lengths[b] - row_ref[0], limits)
    limits_ref[...] = jnp.where(line == requests, place_ref[0], limits)
    fetches[2].wait()
    rows = jnp.concatenate([new[t].astype(f32) for t in range(steps)], axis=0)
    tail = rows[:, width:]
    tail = tail * cos + swap_halves(tail) * sin
    keys_ref[...] = jnp.concatenate([rows[:, :width], tail], axis=-1).astype(bf16)
    q_f32 = q[:, :, :nope].astype(f32)
    for h in range(heads):
        if h % share == 0:
            fetches[4 + h // share].wait()
        lat[:, h, :] = jnp.dot(q_f32[:, h, :].astype(bf16), up[h], preferred_element_type=f32)
    for s in range(steps):
        for b in range(requests):
            own_ref[b, s * heads : (s + 1) * heads, :width] = lat[s * requests + b].astype(bf16)
    packed = [own_ref[info_ref[0] + i] for i in range(sent_ref.shape[1] // key_width)]
    latents = [row[:, :width] for row in packed]
    sent_ref[...] = jnp.concatenate(latents + [row[:, width:key_width] for row in packed], axis=-1)


def split_stats(peak, weight_sum, rows):
    lane = lax.broadcasted_iota(jnp.int32, (rows, 128), 1)
    first = peak.astype(bf16).astype(f32)
    rest = peak - first
    second = rest.astype(bf16).astype(f32)
    third = rest - second
    sum_first = weight_sum.astype(bf16).astype(f32)
    sum_second = weight_sum - sum_first
    out = jnp.where(lane == 0, first, 0.0)
    out = jnp.where(lane == 1, second, out)
    out = jnp.where(lane == 2, third, out)
    out = jnp.where(lane == 3, sum_first, out)
    return jnp.where(lane == 4, sum_second, out)


def stage_kernel(info_ref, cache_hbm, out_ref, sems):
    copies = []
    for i in range(out_ref.shape[0]):
        copies.append(pltpu.make_async_copy(cache_hbm.at[info_ref[0] + i], out_ref.at[i], sems.at[i]))
    for copy in copies:
        copy.start()
    for copy in copies:
        copy.wait()


def stat_rows(peak, weight_sum):
    line = lax.broadcasted_iota(jnp.int32, (16, peak.shape[1]), 0)
    first = peak.astype(bf16).astype(f32)
    second = (peak - first).astype(bf16).astype(f32)
    sum_first = weight_sum.astype(bf16).astype(f32)
    stats = jnp.where(line == 0, first, 0.0)
    stats = jnp.where(line == 1, second, stats)
    stats = jnp.where(line == 2, peak - first - second, stats)
    stats = jnp.where(line == 3, sum_first, stats)
    return jnp.where(line == 4, weight_sum - sum_first, stats).astype(bf16)


def attention_kernel(scale, info_ref, limits_ref, own_ref, q1_ref, q2_ref, q3_ref, k_ref, out_ref, q_ref, *scores):
    count, owners, share, _ = q_ref.shape
    rows = owners * share
    key_width, cached = k_ref.shape[1:]
    width = out_ref.shape[2] - 128
    chunk = 1024
    first = info_ref[0]
    base = first if k_ref.shape[0] > count else 0
    q_ref[:, 0] = own_ref[pl.ds(first, count)]
    rope = key_width - width
    for k, packed_ref in enumerate((q1_ref, q2_ref, q3_ref)):
        for i in range(count):
            q_ref[i, 1 + k, :, :width] = packed_ref[:, i * width : (i + 1) * width]
            at = count * width + i * rope
            q_ref[i, 1 + k, :, width:key_width] = packed_ref[:, at : at + rope]

    tops = []
    for i in range(count):
        limit = limits_ref[pl.ds(first + i, 1), :1]
        queries = q_ref[i].reshape(rows, -1)[:, :key_width]
        top = jnp.full((rows, 128), lowest_max, f32)
        for c in range(0, cached, chunk):
            keys = k_ref[base + i, :, c : c + chunk]
            part = jnp.dot(queries, keys, preferred_element_type=f32) * scale
            column = lax.broadcasted_iota(jnp.int32, (1, chunk), 1) + c
            part = jnp.where(column < limit, part, masked_score)
            scores[i][:, c : c + chunk] = part
            for at in range(0, chunk, 128):
                top = jnp.maximum(top, part[:, at : at + 128])
        tops.append(jnp.max(top, axis=1, keepdims=True))

    for i in range(count):
        total = jnp.zeros((rows, 128), f32)
        for c in range(0, cached, chunk):
            weights = jnp.exp2(scores[i][:, c : c + chunk] - tops[i])
            for at in range(0, chunk, 128):
                total = total + weights[:, at : at + 128]
            part = lax.dot_general(
                weights.astype(bf16),
                k_ref[base + i, :width, c : c + chunk],
                (((1,), (1,)), ((), ())),
                preferred_element_type=f32,
            )
            mixed = part if c == 0 else mixed + part
        total = jnp.sum(total, axis=1, keepdims=True)
        at = slice(i * share, (i + 1) * share)
        out_ref[:, at, :width] = mixed.astype(bf16).reshape(owners, share, width)
        out_ref[:, at, width:] = split_stats(tops[i], total, rows).astype(bf16).reshape(owners, share, 128)


def fresh_kernel(scale, steps, heads, info_ref, limits_ref, own_ref, new_ref, out_ref):
    requests, share, _ = own_ref.shape
    key_width = new_ref.shape[1]
    width = out_ref.shape[1]
    requests_rows = out_ref.shape[0] - 16
    stats = []
    fresh = new_ref[...]
    shape = (share, fresh.shape[0])
    key = lax.broadcasted_iota(jnp.int32, shape, 1)
    step = (lax.broadcasted_iota(jnp.int32, shape, 0) // heads) % steps
    counted = limits_ref[requests : requests + 1, :1] == 0
    for i in range(requests_rows // share):
        request = info_ref[0] + i
        scores = (
            lax.dot_general(
                own_ref[request][:, :key_width], fresh, (((1,), (1,)), ((), ())), preferred_element_type=f32
            )
            * scale
        )
        visible = (key % requests == request) & (key // requests <= step) & counted
        scores = jnp.where(visible, scores, masked_score)
        top = jnp.maximum(jnp.max(scores, axis=1, keepdims=True), lowest_max)
        weights = jnp.exp2(scores - top)
        total = jnp.sum(weights, axis=1, keepdims=True)
        mixed = jnp.dot(weights.astype(bf16), fresh[:, :width], preferred_element_type=f32)
        out_ref[i * share : (i + 1) * share, :] = mixed.astype(bf16)
        stats.append(split_stats(top, total, share))
    out_ref[requests_rows:, :] = jnp.zeros((16, width), bf16)
    out_ref[requests_rows:, :requests_rows] = jnp.concatenate(stats, axis=0).T[:16].astype(bf16)


def merge_parts(parts, width):
    tops = []
    sums = []
    for part in parts:
        stat = part[:, width:].astype(f32)
        tops.append(stat[:, 0:1] + stat[:, 1:2] + stat[:, 2:3])
        sums.append(stat[:, 3:4] + stat[:, 4:5])
    peak = functools.reduce(jnp.maximum, tops)
    weights = [jnp.exp2(t - peak) for t in tops]
    weight_sum = sum(w * s for w, s in zip(weights, sums))
    merged = sum(w * part[:, :width].astype(f32) for w, part in zip(weights, parts))
    return merged, peak, weight_sum


def pair_kernel(first, a_ref, b_ref, *sent_refs):
    width = sent_refs[0].shape[1]
    rows = sent_refs[0].shape[0] - 16
    for owner, sent_ref in enumerate(sent_refs, first):
        merged, peak, weight_sum = merge_parts((a_ref[owner], b_ref[owner]), width)
        sent_ref[:rows, :] = merged.astype(bf16)
        sent_ref[rows:, :] = jnp.zeros((16, width), bf16)
        sent_ref[rows:, :rows] = split_stats(peak, weight_sum, rows).T[:16].astype(bf16)


def project_kernel(heads, *refs):
    *parts, up_ref, out_ref = refs
    parts = [part[...] for part in parts]
    rows = out_ref.shape[0] - 16
    weights, peak, weight_sum = merge_rows(parts, rows)
    mixed = weigh(parts, weights, rows)
    high = mixed.astype(bf16)
    both = jnp.concatenate([high, (mixed - high.astype(f32)).astype(bf16)], axis=0)
    value_width = out_ref.shape[1]
    head = lax.broadcasted_iota(jnp.int32, (rows, value_width), 0) % heads
    values = jnp.zeros((rows, value_width), f32)
    for h in range(0, heads, 2):
        two = jnp.concatenate([up_ref[h], up_ref[h + 1]], axis=1)
        part = jnp.dot(both, two, preferred_element_type=f32)
        part = part[:rows] + part[rows:]
        values = jnp.where(head == h, part[:, :value_width], values)
        values = jnp.where(head == h + 1, part[:, value_width:], values)
    out_ref[:rows, :] = values.astype(bf16)
    out_ref[rows:, :] = stat_rows(peak, weight_sum)


def merge_rows(parts, rows):
    tops = []
    sums = []
    for part in parts:
        stat = part[rows:, :rows].astype(f32)
        tops.append(stat[0:1] + stat[1:2] + stat[2:3])
        sums.append(stat[3:4] + stat[4:5])
    tops = jnp.concatenate(tops, axis=0)
    peak = jnp.max(tops, axis=0, keepdims=True)
    weights = jnp.exp2(tops - peak)
    weight_sum = jnp.sum(weights * jnp.concatenate(sums, axis=0), axis=0, keepdims=True)
    return weights, peak, weight_sum


def weigh(parts, weights, rows):
    spread = jnp.concatenate([weights, jnp.zeros((128 - len(parts), weights.shape[1]), f32)], axis=0).T
    return sum(part[:rows, :].astype(f32) * spread[:rows, i : i + 1] for i, part in enumerate(parts))


def middle_kernel(*refs):
    *parts, out_ref = refs
    parts = [part[...] for part in parts]
    rows = out_ref.shape[0] - 16
    weights, peak, weight_sum = merge_rows(parts, rows)
    out_ref[:rows, :] = weigh(parts, weights, rows).astype(bf16)
    out_ref[rows:, :] = stat_rows(peak, weight_sum)


def finish_kernel(*refs):
    *parts, out_ref = refs
    parts = [part[...] for part in parts]
    steps, half = out_ref.shape[:2]
    rows = steps * half * out_ref.shape[2]
    weights, _, weight_sum = merge_rows(parts, rows)
    result = weigh(parts, weights / weight_sum, rows)
    result = result.astype(bf16).reshape(half, steps, *out_ref.shape[2:])
    for b in range(half):
        out_ref[:, b] = result[b]


def place_kernel(info_ref, own_ref, other_ref, out_ref):
    half = own_ref.shape[1]
    first = info_ref[0]
    out_ref[:, pl.ds(first, half)] = own_ref[...]
    out_ref[:, pl.ds(half - first, half)] = other_ref[...]


def on_device(
    query_heads, up_keys, up_values, latent_cache, new_latent, context_lengths, positions
):
    steps, requests, heads, query_width = query_heads.shape
    nope = up_keys.shape[1]
    width = up_keys.shape[2]
    key_width = latent_cache.shape[2]
    rope = key_width - width
    value_width = up_values.shape[2]
    cached = latent_cache.shape[1]
    owners = lax.axis_size("head")
    plane = lax.axis_size("z") * lax.axis_size("x")
    pairs = steps * requests
    half = requests // 2
    scale = float(query_width) ** (-0.5) * log2_e

    core = lax.axis_index("core")
    slot = lax.axis_index(("z", "x", "core", "head"))

    vmem = pl.BlockSpec(memory_space=pltpu.VMEM)
    smem = pl.BlockSpec(memory_space=pltpu.SMEM)
    small = pltpu.CompilerParams(vmem_limit_bytes=12 * 2**20)
    anywhere = pl.BlockSpec(memory_space=pltpu.HBM)
    wide = 640
    in_hbm = functools.partial(pltpu.with_memory_space_constraint, memory_space=pltpu.HBM)
    core32 = core.astype(jnp.int32)
    own_first = (core32 * half).reshape(1)
    other_first = (half - core32 * half).reshape(1)
    first_row = (slot.astype(jnp.int32) * cached).reshape(1)
    place = lax.axis_index(("z", "x")).astype(jnp.int32).reshape(1)
    chunk = half * steps * heads
    own_queries, sent_queries, new_keys, limits = pl.pallas_call(
        functools.partial(queries_kernel, steps),
        in_specs=[smem] * 4 + [anywhere] * 5,
        out_specs=[vmem] * 4,
        out_shape=(
            jax.ShapeDtypeStruct((requests, steps * heads, wide), bf16),
            jax.ShapeDtypeStruct((steps * heads, half * key_width), bf16),
            jax.ShapeDtypeStruct((pairs, key_width), bf16),
            jax.ShapeDtypeStruct((8, 128), jnp.int32),
        ),
        scratch_shapes=[
            pltpu.SMEM((requests,), jnp.int32),
            pltpu.SMEM((requests,), jnp.int32),
            pltpu.VMEM((pairs, heads, query_width), bf16),
            pltpu.VMEM(up_keys.shape, bf16),
            pltpu.VMEM(new_latent.shape, bf16),
            pltpu.VMEM((pairs, heads, width), f32),
            pltpu.SemaphoreType.DMA((8,)),
        ],
        compiler_params=pltpu.CompilerParams(vmem_limit_bytes=24 * 2**20),
        name="queries",
    )(
        other_first,
        own_first,
        first_row,
        place,
        in_hbm(positions),
        in_hbm(context_lengths),
        in_hbm(query_heads.reshape(pairs, heads, query_width)),
        in_hbm(up_keys),
        in_hbm(new_latent),
    )

    def over_head(array, k):
        return lax.ppermute(array, "head", [(i, i ^ k) for i in range(owners)])

    swap = [(0, 1), (1, 0)]
    partners = (2, 3, 1)
    got = [over_head(sent_queries, k) for k in partners]
    fresh = pl.pallas_call(
        functools.partial(fresh_kernel, scale, steps, heads),
        in_specs=[smem, vmem, vmem, vmem],
        out_specs=vmem,
        out_shape=jax.ShapeDtypeStruct((chunk + 16, width), bf16),
        compiler_params=small,
        cost_estimate=pl.CostEstimate(flops=10**9, bytes_accessed=4 * 10**6, transcendentals=0),
        name="fresh",
    )(own_first, limits, own_queries, new_keys)
    cache = jnp.swapaxes(latent_cache, 1, 2)
    staged_shape = pltpu.VMEM((half, key_width, cached), bf16)
    in_vmem = functools.partial(pltpu.with_memory_space_constraint, memory_space=pltpu.VMEM)
    staged = pl.pallas_call(
        stage_kernel,
        in_specs=[smem, anywhere],
        out_specs=vmem,
        out_shape=staged_shape,
        scratch_shapes=[pltpu.SemaphoreType.DMA((half,))],
        compiler_params=small,
        cost_estimate=pl.CostEstimate(flops=0, bytes_accessed=2 * half * key_width * cached, transcendentals=0),
        name="stage",
    )(other_first, in_hbm(cache))
    got[0], staged = lax.optimization_barrier((got[0], staged))
    passed = [lax.ppermute(g, "core", swap) for g in got]

    rows = owners * steps * heads

    def attend(first, got, keys):
        return pl.pallas_call(
            functools.partial(attention_kernel, scale),
            in_specs=[smem] + [vmem] * 6,
            out_specs=vmem,
            scratch_shapes=[pltpu.VMEM((half, owners, steps * heads, wide), bf16)]
            + [pltpu.VMEM((rows, cached), f32)] * half,
            out_shape=jax.ShapeDtypeStruct((owners, chunk, width + 128), bf16),
            compiler_params=pltpu.CompilerParams(vmem_limit_bytes=18 * 2**20),
            cost_estimate=pl.CostEstimate(
                flops=20 * half * rows * cached * (key_width + width),
                bytes_accessed=half * cached * key_width * 2,
                transcendentals=half * rows * cached,
            ),
            name="attention",
        )(first, limits, own_queries, *got, keys)

    other_part = lax.ppermute(attend(other_first, got, in_vmem(staged)), "core", swap)
    own_part = attend(own_first, passed, cache)
    def pair(first, count):
        return pl.pallas_call(
            functools.partial(pair_kernel, first),
            in_specs=[vmem] * 2,
            out_specs=[vmem] * count,
            out_shape=[pltpu.VMEM((chunk + 16, width), bf16)] * count,
            compiler_params=small,
            name="pair_merge",
        )(other_part, own_part)

    sent = dict(zip(partners, pair(1, owners - 1)))
    arrived = [over_head(sent[k], k) for k in (2, 3, 1)]
    (kept,) = pair(0, 1)
    part = pl.pallas_call(
        functools.partial(project_kernel, heads),
        in_specs=[vmem] * 6,
        out_specs=vmem,
        out_shape=jax.ShapeDtypeStruct((chunk + 16, value_width), bf16),
        compiler_params=small,
        name="project",
    )(kept, *arrived, fresh, up_values)

    def crossing(array, axis):
        size = lax.axis_size(axis)
        sides = [(i, c) for i in range(size) for c in range(2)]
        got = [
            lax.ppermute(array, (axis, "core"), [(2 * i + c, 2 * (i ^ k) + 1 - c) for i, c in sides])
            for k in (2, 3, 1)
        ]
        return got + [lax.ppermute(array, "core", swap)]

    part = pl.pallas_call(
        middle_kernel,
        in_specs=[vmem] * 4,
        out_specs=vmem,
        out_shape=jax.ShapeDtypeStruct(part.shape, bf16),
        compiler_params=small,
        name="middle_merge",
    )(*crossing(part, "x"))
    own = pl.pallas_call(
        finish_kernel,
        in_specs=[vmem] * 4,
        out_specs=vmem,
        out_shape=jax.ShapeDtypeStruct((steps, half, heads, value_width), bf16),
        compiler_params=small,
        name="finish",
    )(*crossing(part, "z"))
    theirs = lax.ppermute(own, "core", swap)
    return pl.pallas_call(
        place_kernel,
        in_specs=[smem, vmem, vmem],
        out_specs=vmem,
        out_shape=jax.ShapeDtypeStruct((steps, requests, heads, value_width), bf16),
        compiler_params=small,
        name="place",
    )(own_first, own, theirs)


def solution(mesh):
    fine = Mesh(mesh.devices.reshape(4, 4, 2, 4), ("z", "x", "core", "head"))
    in_specs = (
        P(None, None, "head", None),
        P("head", None, None),
        P("head", None, None),
        P(None, ("z", "x", "core", "head"), None),
        P(),
        P(),
        P(),
    )
    out_specs = P(None, None, "head", None)
    return jax.shard_map(
        on_device, mesh=fine, in_specs=in_specs, out_specs=out_specs, check_vma=False
    )
```

```python
import functools

import jax
import jax.numpy as jnp
from jax import lax
from jax.experimental import pallas as pl
from jax.experimental.pallas import tpu as pltpu
from jax.sharding import Mesh, PartitionSpec as P

rope_base = 50000.0
masked_score = -1e30
lowest_max = -1e29
log2_e = 1.4426950408889634
bf16 = jnp.bfloat16
f32 = jnp.float32


def swap_halves(values):
    half = values.shape[-1] // 2
    return jnp.concatenate([values[..., half:], values[..., :half]], axis=-1)


def rope_tables(positions_ref, steps, width):
    requests = positions_ref.shape[0]
    pairs = steps * requests
    half = width // 2
    row = lax.broadcasted_iota(jnp.int32, (pairs, width), 0)
    lane = lax.broadcasted_iota(jnp.int32, (pairs, width), 1)
    where_at = row // requests
    for b in range(requests):
        where_at += jnp.where(row % requests == b, positions_ref[b], 0)
    counter = lax.broadcasted_iota(jnp.int32, (1, width), 1) % half
    inverse = jnp.zeros((1, width), f32)
    for i in range(half):
        inverse = jnp.where(counter == i, f32(rope_base ** (-2.0 * i / width)), inverse)
    angles = where_at.astype(f32) * inverse
    return jnp.cos(angles), jnp.where(lane < half, -1.0, 1.0) * jnp.sin(angles)


def queries_kernel(
    steps,
    info_ref,
    own_first_ref,
    row_ref,
    place_ref,
    positions_hbm,
    lengths_hbm,
    q_hbm,
    up_hbm,
    new_hbm,
    own_ref,
    sent_ref,
    keys_ref,
    limits_ref,
    positions,
    lengths,
    q,
    up,
    new,
    lat,
    sems,
):
    pairs, heads, _ = q.shape
    requests = pairs // steps
    nope, width = up.shape[1], up.shape[2]
    key_width = new.shape[2]
    fetches = [
        pltpu.make_async_copy(positions_hbm, positions, sems.at[0]),
        pltpu.make_async_copy(q_hbm, q, sems.at[1]),
        pltpu.make_async_copy(new_hbm, new, sems.at[2]),
        pltpu.make_async_copy(lengths_hbm, lengths, sems.at[3]),
    ]
    groups = 4
    share = heads // groups
    for g in range(groups):
        at = pl.ds(g * share, share)
        fetches.append(pltpu.make_async_copy(up_hbm.at[at], up.at[at], sems.at[4 + g]))
    for fetch in fetches:
        fetch.start()
    own_ref[:, :, key_width:] = jnp.zeros(own_ref.shape[:2] + (own_ref.shape[2] - key_width,), bf16)
    fetches[0].wait()
    cos, sin = rope_tables(positions, steps, key_width - width)
    fetches[1].wait()
    rope = q[:, :, nope:].astype(f32)
    rope = (rope * cos[:, None, :] + swap_halves(rope) * sin[:, None, :]).astype(bf16)
    for s in range(steps):
        for b in range(requests):
            own_ref[b, s * heads : (s + 1) * heads, width:key_width] = rope[s * requests + b]
    fetches[3].wait()
    line = lax.broadcasted_iota(jnp.int32, limits_ref.shape, 0)
    limits = jnp.zeros(limits_ref.shape, jnp.int32)
    for b in range(requests):
        limits = jnp.where(line == b, lengths[b] - row_ref[0], limits)
    limits_ref[...] = jnp.where(line == requests, place_ref[0], limits)
    fetches[2].wait()
    rows = jnp.concatenate([new[t].astype(f32) for t in range(steps)], axis=0)
    tail = rows[:, width:]
    tail = tail * cos + swap_halves(tail) * sin
    keys_ref[...] = jnp.concatenate([rows[:, :width], tail], axis=-1).astype(bf16)
    q_f32 = q[:, :, :nope].astype(f32)
    for h in range(heads):
        if h % share == 0:
            fetches[4 + h // share].wait()
        lat[:, h, :] = jnp.dot(q_f32[:, h, :].astype(bf16), up[h], preferred_element_type=f32)
    for s in range(steps):
        for b in range(requests):
            own_ref[b, s * heads : (s + 1) * heads, :width] = lat[s * requests + b].astype(bf16)
    packed = [own_ref[own_first_ref[0] + i] for i in range(sent_ref.shape[1] // key_width)]
    latents = [row[:, :width] for row in packed]
    sent_ref[...] = jnp.concatenate(latents + [row[:, width:key_width] for row in packed], axis=-1)


def split_stats(peak, weight_sum, rows):
    lane = lax.broadcasted_iota(jnp.int32, (rows, 128), 1)
    first = peak.astype(bf16).astype(f32)
    rest = peak - first
    second = rest.astype(bf16).astype(f32)
    third = rest - second
    sum_first = weight_sum.astype(bf16).astype(f32)
    sum_second = weight_sum - sum_first
    out = jnp.where(lane == 0, first, 0.0)
    out = jnp.where(lane == 1, second, out)
    out = jnp.where(lane == 2, third, out)
    out = jnp.where(lane == 3, sum_first, out)
    return jnp.where(lane == 4, sum_second, out)


def stage_kernel(info_ref, cache_hbm, out_ref, sems):
    copies = []
    for i in range(out_ref.shape[0]):
        copies.append(pltpu.make_async_copy(cache_hbm.at[info_ref[0] + i], out_ref.at[i], sems.at[i]))
    for copy in copies:
        copy.start()
    for copy in copies:
        copy.wait()


def stat_rows(peak, weight_sum):
    line = lax.broadcasted_iota(jnp.int32, (16, peak.shape[1]), 0)
    first = peak.astype(bf16).astype(f32)
    second = (peak - first).astype(bf16).astype(f32)
    sum_first = weight_sum.astype(bf16).astype(f32)
    stats = jnp.where(line == 0, first, 0.0)
    stats = jnp.where(line == 1, second, stats)
    stats = jnp.where(line == 2, peak - first - second, stats)
    stats = jnp.where(line == 3, sum_first, stats)
    return jnp.where(line == 4, weight_sum - sum_first, stats).astype(bf16)


def attention_kernel(scale, info_ref, limits_ref, own_ref, q1_ref, q2_ref, q3_ref, k_ref, out_ref, q_ref, *scores):
    count, owners, share, _ = q_ref.shape
    rows = owners * share
    key_width, cached = k_ref.shape[1:]
    width = out_ref.shape[2] - 128
    chunk = 1024
    first = info_ref[0]
    base = first if k_ref.shape[0] > count else 0
    q_ref[:, 0] = own_ref[pl.ds(first, count)]
    rope = key_width - width
    for k, packed_ref in enumerate((q1_ref, q2_ref, q3_ref)):
        for i in range(count):
            q_ref[i, 1 + k, :, :width] = packed_ref[:, i * width : (i + 1) * width]
            at = count * width + i * rope
            q_ref[i, 1 + k, :, width:key_width] = packed_ref[:, at : at + rope]

    tops = []
    for i in range(count):
        limit = limits_ref[pl.ds(first + i, 1), :1]
        queries = q_ref[i].reshape(rows, -1)[:, :key_width]
        top = jnp.full((rows, 128), lowest_max, f32)
        for c in range(0, cached, chunk):
            keys = k_ref[base + i, :, c : c + chunk]
            part = jnp.dot(queries, keys, preferred_element_type=f32) * scale
            column = lax.broadcasted_iota(jnp.int32, (1, chunk), 1) + c
            part = jnp.where(column < limit, part, masked_score)
            scores[i][:, c : c + chunk] = part
            for at in range(0, chunk, 128):
                top = jnp.maximum(top, part[:, at : at + 128])
        tops.append(jnp.max(top, axis=1, keepdims=True))

    for i in range(count):
        total = jnp.zeros((rows, 128), f32)
        for c in range(0, cached, chunk):
            weights = jnp.exp2(scores[i][:, c : c + chunk] - tops[i])
            for at in range(0, chunk, 128):
                total = total + weights[:, at : at + 128]
            part = lax.dot_general(
                weights.astype(bf16),
                k_ref[base + i, :width, c : c + chunk],
                (((1,), (1,)), ((), ())),
                preferred_element_type=f32,
            )
            mixed = part if c == 0 else mixed + part
        total = jnp.sum(total, axis=1, keepdims=True)
        at = slice(i * share, (i + 1) * share)
        out_ref[:, at, :width] = mixed.astype(bf16).reshape(owners, share, width)
        out_ref[:, at, width:] = split_stats(tops[i], total, rows).astype(bf16).reshape(owners, share, 128)


def fresh_kernel(scale, steps, heads, info_ref, limits_ref, own_ref, new_ref, out_ref):
    requests, share, _ = own_ref.shape
    key_width = new_ref.shape[1]
    width = out_ref.shape[1]
    requests_rows = out_ref.shape[0] - 16
    stats = []
    fresh = new_ref[...]
    shape = (share, fresh.shape[0])
    key = lax.broadcasted_iota(jnp.int32, shape, 1)
    step = (lax.broadcasted_iota(jnp.int32, shape, 0) // heads) % steps
    counted = limits_ref[requests : requests + 1, :1] == 0
    for i in range(requests_rows // share):
        request = info_ref[0] + i
        scores = (
            lax.dot_general(
                own_ref[request][:, :key_width], fresh, (((1,), (1,)), ((), ())), preferred_element_type=f32
            )
            * scale
        )
        visible = (key % requests == request) & (key // requests <= step) & counted
        scores = jnp.where(visible, scores, masked_score)
        top = jnp.maximum(jnp.max(scores, axis=1, keepdims=True), lowest_max)
        weights = jnp.exp2(scores - top)
        total = jnp.sum(weights, axis=1, keepdims=True)
        mixed = jnp.dot(weights.astype(bf16), fresh[:, :width], preferred_element_type=f32)
        out_ref[i * share : (i + 1) * share, :] = mixed.astype(bf16)
        stats.append(split_stats(top, total, share))
    out_ref[requests_rows:, :] = jnp.zeros((16, width), bf16)
    out_ref[requests_rows:, :requests_rows] = jnp.concatenate(stats, axis=0).T[:16].astype(bf16)


def merge_parts(parts, width):
    tops = []
    sums = []
    for part in parts:
        stat = part[:, width:].astype(f32)
        tops.append(stat[:, 0:1] + stat[:, 1:2] + stat[:, 2:3])
        sums.append(stat[:, 3:4] + stat[:, 4:5])
    peak = functools.reduce(jnp.maximum, tops)
    weights = [jnp.exp2(t - peak) for t in tops]
    weight_sum = sum(w * s for w, s in zip(weights, sums))
    merged = sum(w * part[:, :width].astype(f32) for w, part in zip(weights, parts))
    return merged, peak, weight_sum


def pair_kernel(first, a_ref, b_ref, *sent_refs):
    width = sent_refs[0].shape[1]
    rows = sent_refs[0].shape[0] - 16
    for owner, sent_ref in enumerate(sent_refs, first):
        merged, peak, weight_sum = merge_parts((a_ref[owner], b_ref[owner]), width)
        sent_ref[:rows, :] = merged.astype(bf16)
        sent_ref[rows:, :] = jnp.zeros((16, width), bf16)
        sent_ref[rows:, :rows] = split_stats(peak, weight_sum, rows).T[:16].astype(bf16)


def project_kernel(heads, *refs):
    *parts, up_ref, out_ref = refs
    parts = [part[...] for part in parts]
    rows = out_ref.shape[0] - 16
    weights, peak, weight_sum = merge_rows(parts, rows)
    mixed = weigh(parts, weights, rows)
    high = mixed.astype(bf16)
    both = jnp.concatenate([high, (mixed - high.astype(f32)).astype(bf16)], axis=0)
    value_width = out_ref.shape[1]
    head = lax.broadcasted_iota(jnp.int32, (rows, value_width), 0) % heads
    values = jnp.zeros((rows, value_width), f32)
    for h in range(0, heads, 2):
        two = jnp.concatenate([up_ref[h], up_ref[h + 1]], axis=1)
        part = jnp.dot(both, two, preferred_element_type=f32)
        part = part[:rows] + part[rows:]
        values = jnp.where(head == h, part[:, :value_width], values)
        values = jnp.where(head == h + 1, part[:, value_width:], values)
    out_ref[:rows, :] = values.astype(bf16)
    out_ref[rows:, :] = stat_rows(peak, weight_sum)


def merge_rows(parts, rows):
    tops = []
    sums = []
    for part in parts:
        stat = part[rows:, :rows].astype(f32)
        tops.append(stat[0:1] + stat[1:2] + stat[2:3])
        sums.append(stat[3:4] + stat[4:5])
    tops = jnp.concatenate(tops, axis=0)
    peak = jnp.max(tops, axis=0, keepdims=True)
    weights = jnp.exp2(tops - peak)
    weight_sum = jnp.sum(weights * jnp.concatenate(sums, axis=0), axis=0, keepdims=True)
    return weights, peak, weight_sum


def weigh(parts, weights, rows):
    spread = jnp.concatenate([weights, jnp.zeros((128 - len(parts), weights.shape[1]), f32)], axis=0).T
    return sum(part[:rows, :].astype(f32) * spread[:rows, i : i + 1] for i, part in enumerate(parts))


def middle_kernel(*refs):
    *parts, out_ref = refs
    parts = [part[...] for part in parts]
    rows = out_ref.shape[0] - 16
    weights, peak, weight_sum = merge_rows(parts, rows)
    out_ref[:rows, :] = weigh(parts, weights, rows).astype(bf16)
    out_ref[rows:, :] = stat_rows(peak, weight_sum)


def finish_kernel(*refs):
    *parts, out_ref = refs
    parts = [part[...] for part in parts]
    steps, half = out_ref.shape[:2]
    rows = steps * half * out_ref.shape[2]
    weights, _, weight_sum = merge_rows(parts, rows)
    result = weigh(parts, weights / weight_sum, rows)
    result = result.astype(bf16).reshape(half, steps, *out_ref.shape[2:])
    for b in range(half):
        out_ref[:, b] = result[b]


def place_kernel(info_ref, own_ref, other_ref, out_ref):
    half = own_ref.shape[1]
    first = info_ref[0]
    out_ref[:, pl.ds(first, half)] = own_ref[...]
    out_ref[:, pl.ds(half - first, half)] = other_ref[...]


def on_device(
    query_heads, up_keys, up_values, latent_cache, new_latent, context_lengths, positions
):
    steps, requests, heads, query_width = query_heads.shape
    nope = up_keys.shape[1]
    width = up_keys.shape[2]
    key_width = latent_cache.shape[2]
    rope = key_width - width
    value_width = up_values.shape[2]
    cached = latent_cache.shape[1]
    owners = lax.axis_size("head")
    plane = lax.axis_size("z") * lax.axis_size("x")
    pairs = steps * requests
    half = requests // 2
    scale = float(query_width) ** (-0.5) * log2_e

    core = lax.axis_index("core")
    slot = lax.axis_index(("z", "x", "core", "head"))

    vmem = pl.BlockSpec(memory_space=pltpu.VMEM)
    smem = pl.BlockSpec(memory_space=pltpu.SMEM)
    small = pltpu.CompilerParams(vmem_limit_bytes=12 * 2**20)
    anywhere = pl.BlockSpec(memory_space=pltpu.HBM)
    wide = 640
    in_hbm = functools.partial(pltpu.with_memory_space_constraint, memory_space=pltpu.HBM)
    core32 = core.astype(jnp.int32)
    own_first = (core32 * half).reshape(1)
    other_first = (half - core32 * half).reshape(1)
    first_row = (slot.astype(jnp.int32) * cached).reshape(1)
    place = lax.axis_index(("z", "x")).astype(jnp.int32).reshape(1)
    chunk = half * steps * heads
    own_queries, sent_queries, new_keys, limits = pl.pallas_call(
        functools.partial(queries_kernel, steps),
        in_specs=[smem] * 4 + [anywhere] * 5,
        out_specs=[vmem] * 4,
        out_shape=(
            jax.ShapeDtypeStruct((requests, steps * heads, wide), bf16),
            jax.ShapeDtypeStruct((steps * heads, half * key_width), bf16),
            jax.ShapeDtypeStruct((pairs, key_width), bf16),
            jax.ShapeDtypeStruct((8, 128), jnp.int32),
        ),
        scratch_shapes=[
            pltpu.SMEM((requests,), jnp.int32),
            pltpu.SMEM((requests,), jnp.int32),
            pltpu.VMEM((pairs, heads, query_width), bf16),
            pltpu.VMEM(up_keys.shape, bf16),
            pltpu.VMEM(new_latent.shape, bf16),
            pltpu.VMEM((pairs, heads, width), f32),
            pltpu.SemaphoreType.DMA((8,)),
        ],
        compiler_params=pltpu.CompilerParams(vmem_limit_bytes=24 * 2**20),
        name="queries",
    )(
        other_first,
        own_first,
        first_row,
        place,
        in_hbm(positions),
        in_hbm(context_lengths),
        in_hbm(query_heads.reshape(pairs, heads, query_width)),
        in_hbm(up_keys),
        in_hbm(new_latent),
    )

    def over_head(array, k):
        return lax.ppermute(array, "head", [(i, i ^ k) for i in range(owners)])

    swap = [(0, 1), (1, 0)]
    partners = (2, 3, 1)
    sides = [(c, i) for c in range(2) for i in range(owners)]
    got = [
        lax.ppermute(
            sent_queries, ("core", "head"), [(c * owners + i, (1 - c) * owners + (i ^ k)) for c, i in sides]
        )
        for k in partners
    ]
    fresh = pl.pallas_call(
        functools.partial(fresh_kernel, scale, steps, heads),
        in_specs=[smem, vmem, vmem, vmem],
        out_specs=vmem,
        out_shape=jax.ShapeDtypeStruct((chunk + 16, width), bf16),
        compiler_params=small,
        cost_estimate=pl.CostEstimate(flops=10**9, bytes_accessed=4 * 10**6, transcendentals=0),
        name="fresh",
    )(own_first, limits, own_queries, new_keys)
    cache = jnp.swapaxes(latent_cache, 1, 2)
    staged_shape = pltpu.VMEM((half, key_width, cached), bf16)
    in_vmem = functools.partial(pltpu.with_memory_space_constraint, memory_space=pltpu.VMEM)
    staged = pl.pallas_call(
        stage_kernel,
        in_specs=[smem, anywhere],
        out_specs=vmem,
        out_shape=staged_shape,
        scratch_shapes=[pltpu.SemaphoreType.DMA((half,))],
        compiler_params=small,
        cost_estimate=pl.CostEstimate(flops=0, bytes_accessed=2 * half * key_width * cached, transcendentals=0),
        name="stage",
    )(other_first, in_hbm(cache))
    got[0], staged = lax.optimization_barrier((got[0], staged))
    passed = [lax.ppermute(g, "core", swap) for g in got]

    rows = owners * steps * heads

    def attend(first, got, keys):
        return pl.pallas_call(
            functools.partial(attention_kernel, scale),
            in_specs=[smem] + [vmem] * 6,
            out_specs=vmem,
            scratch_shapes=[pltpu.VMEM((half, owners, steps * heads, wide), bf16)]
            + [pltpu.VMEM((rows, cached), f32)] * half,
            out_shape=jax.ShapeDtypeStruct((owners, chunk, width + 128), bf16),
            compiler_params=pltpu.CompilerParams(vmem_limit_bytes=18 * 2**20),
            cost_estimate=pl.CostEstimate(
                flops=20 * half * rows * cached * (key_width + width),
                bytes_accessed=half * cached * key_width * 2,
                transcendentals=half * rows * cached,
            ),
            name="attention",
        )(first, limits, own_queries, *got, keys)

    other_part = lax.ppermute(attend(other_first, got, in_vmem(staged)), "core", swap)
    own_part = attend(own_first, passed, cache)
    def pair(first, count):
        return pl.pallas_call(
            functools.partial(pair_kernel, first),
            in_specs=[vmem] * 2,
            out_specs=[vmem] * count,
            out_shape=[pltpu.VMEM((chunk + 16, width), bf16)] * count,
            compiler_params=small,
            name="pair_merge",
        )(other_part, own_part)

    sent = dict(zip(partners, pair(1, owners - 1)))
    arrived = [over_head(sent[k], k) for k in (2, 3, 1)]
    (kept,) = pair(0, 1)
    part = pl.pallas_call(
        functools.partial(project_kernel, heads),
        in_specs=[vmem] * 6,
        out_specs=vmem,
        out_shape=jax.ShapeDtypeStruct((chunk + 16, value_width), bf16),
        compiler_params=small,
        name="project",
    )(kept, *arrived, fresh, up_values)

    def crossing(array, axis):
        size = lax.axis_size(axis)
        sides = [(i, c) for i in range(size) for c in range(2)]
        got = [
            lax.ppermute(array, (axis, "core"), [(2 * i + c, 2 * (i ^ k) + 1 - c) for i, c in sides])
            for k in (2, 3, 1)
        ]
        return got + [lax.ppermute(array, "core", swap)]

    part = pl.pallas_call(
        middle_kernel,
        in_specs=[vmem] * 4,
        out_specs=vmem,
        out_shape=jax.ShapeDtypeStruct(part.shape, bf16),
        compiler_params=small,
        name="middle_merge",
    )(*crossing(part, "z"))
    own = pl.pallas_call(
        finish_kernel,
        in_specs=[vmem] * 4,
        out_specs=vmem,
        out_shape=jax.ShapeDtypeStruct((steps, half, heads, value_width), bf16),
        compiler_params=small,
        name="finish",
    )(*crossing(part, "x"))
    theirs = lax.ppermute(own, "core", swap)
    return pl.pallas_call(
        place_kernel,
        in_specs=[smem, vmem, vmem],
        out_specs=vmem,
        out_shape=jax.ShapeDtypeStruct((steps, requests, heads, value_width), bf16),
        compiler_params=small,
        name="place",
    )(own_first, own, theirs)


def solution(mesh):
    fine = Mesh(mesh.devices.reshape(4, 4, 2, 4), ("z", "x", "core", "head"))
    in_specs = (
        P(None, None, "head", None),
        P("head", None, None),
        P("head", None, None),
        P(None, ("z", "x", "core", "head"), None),
        P(),
        P(),
        P(),
    )
    out_specs = P(None, None, "head", None)
    return jax.shard_map(
        on_device, mesh=fine, in_specs=in_specs, out_specs=out_specs, check_vma=False
    )
```

```python
import functools

import jax
import jax.numpy as jnp
from jax import lax
from jax.experimental import pallas as pl
from jax.experimental.pallas import tpu as pltpu
from jax.sharding import Mesh, PartitionSpec as P

rope_base = 50000.0
masked_score = -1e30
lowest_max = -1e29
log2_e = 1.4426950408889634
bf16 = jnp.bfloat16
f32 = jnp.float32


def swap_halves(values):
    half = values.shape[-1] // 2
    return jnp.concatenate([values[..., half:], values[..., :half]], axis=-1)


def rope_tables(positions_ref, steps, width):
    requests = positions_ref.shape[0]
    pairs = steps * requests
    half = width // 2
    row = lax.broadcasted_iota(jnp.int32, (pairs, width), 0)
    lane = lax.broadcasted_iota(jnp.int32, (pairs, width), 1)
    where_at = row // requests
    for b in range(requests):
        where_at += jnp.where(row % requests == b, positions_ref[b], 0)
    counter = lax.broadcasted_iota(jnp.int32, (1, width), 1) % half
    inverse = jnp.zeros((1, width), f32)
    for i in range(half):
        inverse = jnp.where(counter == i, f32(rope_base ** (-2.0 * i / width)), inverse)
    angles = where_at.astype(f32) * inverse
    return jnp.cos(angles), jnp.where(lane < half, -1.0, 1.0) * jnp.sin(angles)


def queries_kernel(
    steps,
    info_ref,
    own_first_ref,
    row_ref,
    place_ref,
    positions_hbm,
    lengths_hbm,
    q_hbm,
    up_hbm,
    new_hbm,
    own_ref,
    sent_ref,
    keys_ref,
    limits_ref,
    positions,
    lengths,
    q,
    up,
    new,
    lat,
    sems,
):
    pairs, heads, _ = q.shape
    requests = pairs // steps
    nope, width = up.shape[1], up.shape[2]
    key_width = new.shape[2]
    fetches = [
        pltpu.make_async_copy(positions_hbm, positions, sems.at[0]),
        pltpu.make_async_copy(q_hbm, q, sems.at[1]),
        pltpu.make_async_copy(new_hbm, new, sems.at[2]),
        pltpu.make_async_copy(lengths_hbm, lengths, sems.at[3]),
    ]
    groups = 4
    share = heads // groups
    for g in range(groups):
        at = pl.ds(g * share, share)
        fetches.append(pltpu.make_async_copy(up_hbm.at[at], up.at[at], sems.at[4 + g]))
    for fetch in fetches:
        fetch.start()
    own_ref[:, :, key_width:] = jnp.zeros(own_ref.shape[:2] + (own_ref.shape[2] - key_width,), bf16)
    fetches[0].wait()
    cos, sin = rope_tables(positions, steps, key_width - width)
    fetches[1].wait()
    rope = q[:, :, nope:].astype(f32)
    rope = (rope * cos[:, None, :] + swap_halves(rope) * sin[:, None, :]).astype(bf16)
    for s in range(steps):
        for b in range(requests):
            own_ref[b, s * heads : (s + 1) * heads, width:key_width] = rope[s * requests + b]
    fetches[3].wait()
    line = lax.broadcasted_iota(jnp.int32, limits_ref.shape, 0)
    limits = jnp.zeros(limits_ref.shape, jnp.int32)
    for b in range(requests):
        limits = jnp.where(line == b, lengths[b] - row_ref[0], limits)
    limits_ref[...] = jnp.where(line == requests, place_ref[0], limits)
    fetches[2].wait()
    rows = jnp.concatenate([new[t].astype(f32) for t in range(steps)], axis=0)
    tail = rows[:, width:]
    tail = tail * cos + swap_halves(tail) * sin
    keys_ref[...] = jnp.concatenate([rows[:, :width], tail], axis=-1).astype(bf16)
    q_f32 = q[:, :, :nope].astype(f32)
    for h in range(heads):
        if h % share == 0:
            fetches[4 + h // share].wait()
        lat[:, h, :] = jnp.dot(q_f32[:, h, :].astype(bf16), up[h], preferred_element_type=f32)
    for s in range(steps):
        for b in range(requests):
            own_ref[b, s * heads : (s + 1) * heads, :width] = lat[s * requests + b].astype(bf16)
    packed = [own_ref[info_ref[0] + i] for i in range(sent_ref.shape[1] // key_width)]
    latents = [row[:, :width] for row in packed]
    sent_ref[...] = jnp.concatenate(latents + [row[:, width:key_width] for row in packed], axis=-1)


def split_stats(peak, weight_sum, rows):
    lane = lax.broadcasted_iota(jnp.int32, (rows, 128), 1)
    first = peak.astype(bf16).astype(f32)
    rest = peak - first
    second = rest.astype(bf16).astype(f32)
    third = rest - second
    sum_first = weight_sum.astype(bf16).astype(f32)
    sum_second = weight_sum - sum_first
    out = jnp.where(lane == 0, first, 0.0)
    out = jnp.where(lane == 1, second, out)
    out = jnp.where(lane == 2, third, out)
    out = jnp.where(lane == 3, sum_first, out)
    return jnp.where(lane == 4, sum_second, out)


def stage_kernel(info_ref, cache_hbm, out_ref, sems):
    copies = []
    for i in range(out_ref.shape[0]):
        copies.append(pltpu.make_async_copy(cache_hbm.at[info_ref[0] + i], out_ref.at[i], sems.at[i]))
    for copy in copies:
        copy.start()
    for copy in copies:
        copy.wait()


def stat_rows(peak, weight_sum):
    line = lax.broadcasted_iota(jnp.int32, (16, peak.shape[1]), 0)
    first = peak.astype(bf16).astype(f32)
    second = (peak - first).astype(bf16).astype(f32)
    sum_first = weight_sum.astype(bf16).astype(f32)
    stats = jnp.where(line == 0, first, 0.0)
    stats = jnp.where(line == 1, second, stats)
    stats = jnp.where(line == 2, peak - first - second, stats)
    stats = jnp.where(line == 3, sum_first, stats)
    return jnp.where(line == 4, weight_sum - sum_first, stats).astype(bf16)


def attention_kernel(scale, info_ref, limits_ref, own_ref, q1_ref, q2_ref, q3_ref, k_ref, out_ref, q_ref, *scores):
    count, owners, share, _ = q_ref.shape
    rows = owners * share
    key_width, cached = k_ref.shape[1:]
    width = out_ref.shape[2] - 128
    chunk = 1024
    first = info_ref[0]
    base = first if k_ref.shape[0] > count else 0
    q_ref[:, 0] = own_ref[pl.ds(first, count)]
    rope = key_width - width
    for k, packed_ref in enumerate((q1_ref, q2_ref, q3_ref)):
        for i in range(count):
            q_ref[i, 1 + k, :, :width] = packed_ref[:, i * width : (i + 1) * width]
            at = count * width + i * rope
            q_ref[i, 1 + k, :, width:key_width] = packed_ref[:, at : at + rope]

    tops = []
    for i in range(count):
        limit = limits_ref[pl.ds(first + i, 1), :1]
        queries = q_ref[i].reshape(rows, -1)[:, :key_width]
        top = jnp.full((rows, 128), lowest_max, f32)
        for c in range(0, cached, chunk):
            keys = k_ref[base + i, :, c : c + chunk]
            part = jnp.dot(queries, keys, preferred_element_type=f32) * scale
            column = lax.broadcasted_iota(jnp.int32, (1, chunk), 1) + c
            part = jnp.where(column < limit, part, masked_score)
            scores[i][:, c : c + chunk] = part
            for at in range(0, chunk, 128):
                top = jnp.maximum(top, part[:, at : at + 128])
        tops.append(jnp.max(top, axis=1, keepdims=True))

    for i in range(count):
        total = jnp.zeros((rows, 128), f32)
        for c in range(0, cached, chunk):
            weights = jnp.exp2(scores[i][:, c : c + chunk] - tops[i])
            for at in range(0, chunk, 128):
                total = total + weights[:, at : at + 128]
            part = lax.dot_general(
                weights.astype(bf16),
                k_ref[base + i, :width, c : c + chunk],
                (((1,), (1,)), ((), ())),
                preferred_element_type=f32,
            )
            mixed = part if c == 0 else mixed + part
        total = jnp.sum(total, axis=1, keepdims=True)
        at = slice(i * share, (i + 1) * share)
        out_ref[:, at, :width] = mixed.astype(bf16).reshape(owners, share, width)
        out_ref[:, at, width:] = split_stats(tops[i], total, rows).astype(bf16).reshape(owners, share, 128)


def fresh_kernel(scale, steps, heads, info_ref, limits_ref, own_ref, new_ref, out_ref):
    requests, share, _ = own_ref.shape
    key_width = new_ref.shape[1]
    width = out_ref.shape[1]
    requests_rows = out_ref.shape[0] - 16
    stats = []
    fresh = new_ref[...]
    shape = (share, fresh.shape[0])
    key = lax.broadcasted_iota(jnp.int32, shape, 1)
    step = (lax.broadcasted_iota(jnp.int32, shape, 0) // heads) % steps
    counted = limits_ref[requests : requests + 1, :1] == 0
    for i in range(requests_rows // share):
        request = info_ref[0] + i
        scores = (
            lax.dot_general(
                own_ref[request][:, :key_width], fresh, (((1,), (1,)), ((), ())), preferred_element_type=f32
            )
            * scale
        )
        visible = (key % requests == request) & (key // requests <= step) & counted
        scores = jnp.where(visible, scores, masked_score)
        top = jnp.maximum(jnp.max(scores, axis=1, keepdims=True), lowest_max)
        weights = jnp.exp2(scores - top)
        total = jnp.sum(weights, axis=1, keepdims=True)
        mixed = jnp.dot(weights.astype(bf16), fresh[:, :width], preferred_element_type=f32)
        out_ref[i * share : (i + 1) * share, :] = mixed.astype(bf16)
        stats.append(split_stats(top, total, share))
    out_ref[requests_rows:, :] = jnp.zeros((16, width), bf16)
    out_ref[requests_rows:, :requests_rows] = jnp.concatenate(stats, axis=0).T[:16].astype(bf16)


def merge_parts(parts, width):
    tops = []
    sums = []
    for part in parts:
        stat = part[:, width:].astype(f32)
        tops.append(stat[:, 0:1] + stat[:, 1:2] + stat[:, 2:3])
        sums.append(stat[:, 3:4] + stat[:, 4:5])
    peak = functools.reduce(jnp.maximum, tops)
    weights = [jnp.exp2(t - peak) for t in tops]
    weight_sum = sum(w * s for w, s in zip(weights, sums))
    merged = sum(w * part[:, :width].astype(f32) for w, part in zip(weights, parts))
    return merged, peak, weight_sum


def pair_kernel(first, a_ref, b_ref, *sent_refs):
    width = sent_refs[0].shape[1]
    rows = sent_refs[0].shape[0] - 16
    for owner, sent_ref in enumerate(sent_refs, first):
        merged, peak, weight_sum = merge_parts((a_ref[owner], b_ref[owner]), width)
        sent_ref[:rows, :] = merged.astype(bf16)
        sent_ref[rows:, :] = jnp.zeros((16, width), bf16)
        sent_ref[rows:, :rows] = split_stats(peak, weight_sum, rows).T[:16].astype(bf16)


def project_kernel(heads, *refs):
    *parts, up_ref, out_ref = refs
    parts = [part[...] for part in parts]
    rows = out_ref.shape[0] - 16
    weights, peak, weight_sum = merge_rows(parts, rows)
    mixed = weigh(parts, weights, rows)
    high = mixed.astype(bf16)
    both = jnp.concatenate([high, (mixed - high.astype(f32)).astype(bf16)], axis=0)
    value_width = out_ref.shape[1]
    head = lax.broadcasted_iota(jnp.int32, (rows, value_width), 0) % heads
    values = jnp.zeros((rows, value_width), f32)
    for h in range(0, heads, 2):
        two = jnp.concatenate([up_ref[h], up_ref[h + 1]], axis=1)
        part = jnp.dot(both, two, preferred_element_type=f32)
        part = part[:rows] + part[rows:]
        values = jnp.where(head == h, part[:, :value_width], values)
        values = jnp.where(head == h + 1, part[:, value_width:], values)
    out_ref[:rows, :] = values.astype(bf16)
    out_ref[rows:, :] = stat_rows(peak, weight_sum)


def merge_rows(parts, rows):
    tops = []
    sums = []
    for part in parts:
        stat = part[rows:, :rows].astype(f32)
        tops.append(stat[0:1] + stat[1:2] + stat[2:3])
        sums.append(stat[3:4] + stat[4:5])
    tops = jnp.concatenate(tops, axis=0)
    peak = jnp.max(tops, axis=0, keepdims=True)
    weights = jnp.exp2(tops - peak)
    weight_sum = jnp.sum(weights * jnp.concatenate(sums, axis=0), axis=0, keepdims=True)
    return weights, peak, weight_sum


def weigh(parts, weights, rows):
    spread = jnp.concatenate([weights, jnp.zeros((128 - len(parts), weights.shape[1]), f32)], axis=0).T
    return sum(part[:rows, :].astype(f32) * spread[:rows, i : i + 1] for i, part in enumerate(parts))


def middle_kernel(*refs):
    *parts, out_ref = refs
    parts = [part[...] for part in parts]
    rows = out_ref.shape[0] - 16
    weights, peak, weight_sum = merge_rows(parts, rows)
    out_ref[:rows, :] = weigh(parts, weights, rows).astype(bf16)
    out_ref[rows:, :] = stat_rows(peak, weight_sum)


def finish_kernel(*refs):
    *parts, out_ref = refs
    parts = [part[...] for part in parts]
    steps, half = out_ref.shape[:2]
    rows = steps * half * out_ref.shape[2]
    weights, _, weight_sum = merge_rows(parts, rows)
    result = weigh(parts, weights / weight_sum, rows)
    result = result.astype(bf16).reshape(half, steps, *out_ref.shape[2:])
    for b in range(half):
        out_ref[:, b] = result[b]


def place_kernel(info_ref, own_ref, other_ref, out_hbm, sems):
    half = own_ref.shape[1]
    first = info_ref[0]
    copies = [
        pltpu.make_async_copy(own_ref, out_hbm.at[:, pl.ds(first, half)], sems.at[0]),
        pltpu.make_async_copy(other_ref, out_hbm.at[:, pl.ds(half - first, half)], sems.at[1]),
    ]
    for copy in copies:
        copy.start()
    for copy in copies:
        copy.wait()


def on_device(
    query_heads, up_keys, up_values, latent_cache, new_latent, context_lengths, positions
):
    steps, requests, heads, query_width = query_heads.shape
    nope = up_keys.shape[1]
    width = up_keys.shape[2]
    key_width = latent_cache.shape[2]
    rope = key_width - width
    value_width = up_values.shape[2]
    cached = latent_cache.shape[1]
    owners = lax.axis_size("head")
    plane = lax.axis_size("z") * lax.axis_size("x")
    pairs = steps * requests
    half = requests // 2
    scale = float(query_width) ** (-0.5) * log2_e

    core = lax.axis_index("core")
    slot = lax.axis_index(("z", "x", "core", "head"))

    vmem = pl.BlockSpec(memory_space=pltpu.VMEM)
    smem = pl.BlockSpec(memory_space=pltpu.SMEM)
    small = pltpu.CompilerParams(vmem_limit_bytes=12 * 2**20)
    anywhere = pl.BlockSpec(memory_space=pltpu.HBM)
    wide = 640
    in_hbm = functools.partial(pltpu.with_memory_space_constraint, memory_space=pltpu.HBM)
    core32 = core.astype(jnp.int32)
    own_first = (core32 * half).reshape(1)
    other_first = (half - core32 * half).reshape(1)
    first_row = (slot.astype(jnp.int32) * cached).reshape(1)
    place = lax.axis_index(("z", "x")).astype(jnp.int32).reshape(1)
    chunk = half * steps * heads
    own_queries, sent_queries, new_keys, limits = pl.pallas_call(
        functools.partial(queries_kernel, steps),
        in_specs=[smem] * 4 + [anywhere] * 5,
        out_specs=[vmem] * 4,
        out_shape=(
            jax.ShapeDtypeStruct((requests, steps * heads, wide), bf16),
            jax.ShapeDtypeStruct((steps * heads, half * key_width), bf16),
            jax.ShapeDtypeStruct((pairs, key_width), bf16),
            jax.ShapeDtypeStruct((8, 128), jnp.int32),
        ),
        scratch_shapes=[
            pltpu.SMEM((requests,), jnp.int32),
            pltpu.SMEM((requests,), jnp.int32),
            pltpu.VMEM((pairs, heads, query_width), bf16),
            pltpu.VMEM(up_keys.shape, bf16),
            pltpu.VMEM(new_latent.shape, bf16),
            pltpu.VMEM((pairs, heads, width), f32),
            pltpu.SemaphoreType.DMA((8,)),
        ],
        compiler_params=pltpu.CompilerParams(vmem_limit_bytes=24 * 2**20),
        name="queries",
    )(
        other_first,
        own_first,
        first_row,
        place,
        in_hbm(positions),
        in_hbm(context_lengths),
        in_hbm(query_heads.reshape(pairs, heads, query_width)),
        in_hbm(up_keys),
        in_hbm(new_latent),
    )

    def over_head(array, k):
        return lax.ppermute(array, "head", [(i, i ^ k) for i in range(owners)])

    swap = [(0, 1), (1, 0)]
    partners = (2, 3, 1)
    got = [over_head(sent_queries, k) for k in partners]
    fresh = pl.pallas_call(
        functools.partial(fresh_kernel, scale, steps, heads),
        in_specs=[smem, vmem, vmem, vmem],
        out_specs=vmem,
        out_shape=jax.ShapeDtypeStruct((chunk + 16, width), bf16),
        compiler_params=small,
        cost_estimate=pl.CostEstimate(flops=10**9, bytes_accessed=4 * 10**6, transcendentals=0),
        name="fresh",
    )(own_first, limits, own_queries, new_keys)
    cache = jnp.swapaxes(latent_cache, 1, 2)
    staged_shape = pltpu.VMEM((half, key_width, cached), bf16)
    in_vmem = functools.partial(pltpu.with_memory_space_constraint, memory_space=pltpu.VMEM)
    staged = pl.pallas_call(
        stage_kernel,
        in_specs=[smem, anywhere],
        out_specs=vmem,
        out_shape=staged_shape,
        scratch_shapes=[pltpu.SemaphoreType.DMA((half,))],
        compiler_params=small,
        cost_estimate=pl.CostEstimate(flops=0, bytes_accessed=2 * half * key_width * cached, transcendentals=0),
        name="stage",
    )(other_first, in_hbm(cache))
    got[0], staged = lax.optimization_barrier((got[0], staged))
    passed = [lax.ppermute(g, "core", swap) for g in got]

    rows = owners * steps * heads

    def attend(first, got, keys):
        return pl.pallas_call(
            functools.partial(attention_kernel, scale),
            in_specs=[smem] + [vmem] * 6,
            out_specs=vmem,
            scratch_shapes=[pltpu.VMEM((half, owners, steps * heads, wide), bf16)]
            + [pltpu.VMEM((rows, cached), f32)] * half,
            out_shape=jax.ShapeDtypeStruct((owners, chunk, width + 128), bf16),
            compiler_params=pltpu.CompilerParams(vmem_limit_bytes=18 * 2**20),
            cost_estimate=pl.CostEstimate(
                flops=20 * half * rows * cached * (key_width + width),
                bytes_accessed=half * cached * key_width * 2,
                transcendentals=half * rows * cached,
            ),
            name="attention",
        )(first, limits, own_queries, *got, keys)

    other_part = lax.ppermute(attend(other_first, got, in_vmem(staged)), "core", swap)
    own_part = attend(own_first, passed, cache)
    def pair(first, count):
        return pl.pallas_call(
            functools.partial(pair_kernel, first),
            in_specs=[vmem] * 2,
            out_specs=[vmem] * count,
            out_shape=[pltpu.VMEM((chunk + 16, width), bf16)] * count,
            compiler_params=small,
            name="pair_merge",
        )(other_part, own_part)

    sent = dict(zip(partners, pair(1, owners - 1)))
    arrived = [over_head(sent[k], k) for k in (2, 3, 1)]
    (kept,) = pair(0, 1)
    part = pl.pallas_call(
        functools.partial(project_kernel, heads),
        in_specs=[vmem] * 6,
        out_specs=vmem,
        out_shape=jax.ShapeDtypeStruct((chunk + 16, value_width), bf16),
        compiler_params=small,
        name="project",
    )(kept, *arrived, fresh, up_values)

    def crossing(array, axis):
        size = lax.axis_size(axis)
        sides = [(i, c) for i in range(size) for c in range(2)]
        got = [
            lax.ppermute(array, (axis, "core"), [(2 * i + c, 2 * (i ^ k) + 1 - c) for i, c in sides])
            for k in (2, 3, 1)
        ]
        return got + [lax.ppermute(array, "core", swap)]

    part = pl.pallas_call(
        middle_kernel,
        in_specs=[vmem] * 4,
        out_specs=vmem,
        out_shape=jax.ShapeDtypeStruct(part.shape, bf16),
        compiler_params=small,
        name="middle_merge",
    )(*crossing(part, "z"))
    own = pl.pallas_call(
        finish_kernel,
        in_specs=[vmem] * 4,
        out_specs=vmem,
        out_shape=jax.ShapeDtypeStruct((steps, half, heads, value_width), bf16),
        compiler_params=small,
        name="finish",
    )(*crossing(part, "x"))
    theirs = lax.ppermute(own, "core", swap)
    return pl.pallas_call(
        place_kernel,
        in_specs=[smem, vmem, vmem],
        out_specs=anywhere,
        scratch_shapes=[pltpu.SemaphoreType.DMA((2,))],
        out_shape=jax.ShapeDtypeStruct((steps, requests, heads, value_width), bf16),
        compiler_params=small,
        name="place",
    )(own_first, own, theirs)


def solution(mesh):
    fine = Mesh(mesh.devices.reshape(4, 4, 2, 4), ("z", "x", "core", "head"))
    in_specs = (
        P(None, None, "head", None),
        P("head", None, None),
        P("head", None, None),
        P(None, ("z", "x", "core", "head"), None),
        P(),
        P(),
        P(),
    )
    out_specs = P(None, None, "head", None)
    return jax.shard_map(
        on_device, mesh=fine, in_specs=in_specs, out_specs=out_specs, check_vma=False
    )
```

```python
import functools

import jax
import jax.numpy as jnp
from jax import lax
from jax.experimental import pallas as pl
from jax.experimental.pallas import tpu as pltpu
from jax.sharding import Mesh, PartitionSpec as P

rope_base = 50000.0
masked_score = -1e30
lowest_max = -1e29
log2_e = 1.4426950408889634
bf16 = jnp.bfloat16
f32 = jnp.float32


def swap_halves(values):
    half = values.shape[-1] // 2
    return jnp.concatenate([values[..., half:], values[..., :half]], axis=-1)


def rope_tables(positions_ref, steps, width):
    requests = positions_ref.shape[0]
    pairs = steps * requests
    half = width // 2
    row = lax.broadcasted_iota(jnp.int32, (pairs, width), 0)
    lane = lax.broadcasted_iota(jnp.int32, (pairs, width), 1)
    where_at = row // requests
    for b in range(requests):
        where_at += jnp.where(row % requests == b, positions_ref[b], 0)
    counter = lax.broadcasted_iota(jnp.int32, (1, width), 1) % half
    inverse = jnp.zeros((1, width), f32)
    for i in range(half):
        inverse = jnp.where(counter == i, f32(rope_base ** (-2.0 * i / width)), inverse)
    angles = where_at.astype(f32) * inverse
    return jnp.cos(angles), jnp.where(lane < half, -1.0, 1.0) * jnp.sin(angles)


def queries_kernel(
    steps,
    info_ref,
    own_first_ref,
    row_ref,
    place_ref,
    positions_hbm,
    lengths_hbm,
    q_hbm,
    up_hbm,
    new_hbm,
    own_ref,
    sent_ref,
    keys_ref,
    limits_ref,
    positions,
    lengths,
    q,
    up,
    new,
    lat,
    sems,
):
    pairs, heads, _ = q.shape
    requests = pairs // steps
    nope, width = up.shape[1], up.shape[2]
    key_width = new.shape[2]
    fetches = [
        pltpu.make_async_copy(positions_hbm, positions, sems.at[0]),
        pltpu.make_async_copy(q_hbm, q, sems.at[1]),
        pltpu.make_async_copy(new_hbm, new, sems.at[2]),
        pltpu.make_async_copy(lengths_hbm, lengths, sems.at[3]),
    ]
    groups = 4
    share = heads // groups
    for g in range(groups):
        at = pl.ds(g * share, share)
        fetches.append(pltpu.make_async_copy(up_hbm.at[at], up.at[at], sems.at[4 + g]))
    for fetch in fetches:
        fetch.start()
    own_ref[:, :, key_width:] = jnp.zeros(own_ref.shape[:2] + (own_ref.shape[2] - key_width,), bf16)
    fetches[0].wait()
    cos, sin = rope_tables(positions, steps, key_width - width)
    fetches[1].wait()
    rope = q[:, :, nope:].astype(f32)
    rope = (rope * cos[:, None, :] + swap_halves(rope) * sin[:, None, :]).astype(bf16)
    for s in range(steps):
        for b in range(requests):
            own_ref[b, s * heads : (s + 1) * heads, width:key_width] = rope[s * requests + b]
    fetches[3].wait()
    line = lax.broadcasted_iota(jnp.int32, limits_ref.shape, 0)
    limits = jnp.zeros(limits_ref.shape, jnp.int32)
    for b in range(requests):
        limits = jnp.where(line == b, lengths[b] - row_ref[0], limits)
    limits_ref[...] = jnp.where(line == requests, place_ref[0], limits)
    fetches[2].wait()
    rows = jnp.concatenate([new[t].astype(f32) for t in range(steps)], axis=0)
    tail = rows[:, width:]
    tail = tail * cos + swap_halves(tail) * sin
    keys_ref[...] = jnp.concatenate([rows[:, :width], tail], axis=-1).astype(bf16)
    q_f32 = q[:, :, :nope].astype(f32)
    for h in range(heads):
        if h % share == 0:
            fetches[4 + h // share].wait()
        lat[:, h, :] = jnp.dot(q_f32[:, h, :].astype(bf16), up[h], preferred_element_type=f32)
    for s in range(steps):
        for b in range(requests):
            own_ref[b, s * heads : (s + 1) * heads, :width] = lat[s * requests + b].astype(bf16)
    packed = [own_ref[info_ref[0] + i] for i in range(sent_ref.shape[1] // key_width)]
    latents = [row[:, :width] for row in packed]
    sent_ref[...] = jnp.concatenate(latents + [row[:, width:key_width] for row in packed], axis=-1)


def split_stats(peak, weight_sum, rows):
    lane = lax.broadcasted_iota(jnp.int32, (rows, 128), 1)
    first = peak.astype(bf16).astype(f32)
    rest = peak - first
    second = rest.astype(bf16).astype(f32)
    third = rest - second
    sum_first = weight_sum.astype(bf16).astype(f32)
    sum_second = weight_sum - sum_first
    out = jnp.where(lane == 0, first, 0.0)
    out = jnp.where(lane == 1, second, out)
    out = jnp.where(lane == 2, third, out)
    out = jnp.where(lane == 3, sum_first, out)
    return jnp.where(lane == 4, sum_second, out)


def stage_kernel(info_ref, cache_hbm, out_ref, sems):
    copies = []
    for i in range(out_ref.shape[0]):
        copies.append(pltpu.make_async_copy(cache_hbm.at[info_ref[0] + i], out_ref.at[i], sems.at[i]))
    for copy in copies:
        copy.start()
    for copy in copies:
        copy.wait()


def stat_rows(peak, weight_sum):
    line = lax.broadcasted_iota(jnp.int32, (16, peak.shape[1]), 0)
    first = peak.astype(bf16).astype(f32)
    second = (peak - first).astype(bf16).astype(f32)
    sum_first = weight_sum.astype(bf16).astype(f32)
    stats = jnp.where(line == 0, first, 0.0)
    stats = jnp.where(line == 1, second, stats)
    stats = jnp.where(line == 2, peak - first - second, stats)
    stats = jnp.where(line == 3, sum_first, stats)
    return jnp.where(line == 4, weight_sum - sum_first, stats).astype(bf16)


def attention_kernel(scale, info_ref, limits_ref, own_ref, q1_ref, q2_ref, q3_ref, k_ref, out_ref, q_ref, *scores):
    count, owners, share, _ = q_ref.shape
    rows = owners * share
    key_width, cached = k_ref.shape[1:]
    width = out_ref.shape[2] - 128
    chunk = 1024
    first = info_ref[0]
    base = first if k_ref.shape[0] > count else 0
    q_ref[:, 0] = own_ref[pl.ds(first, count)]
    rope = key_width - width
    for k, packed_ref in enumerate((q1_ref, q2_ref, q3_ref)):
        for i in range(count):
            q_ref[i, 1 + k, :, :width] = packed_ref[:, i * width : (i + 1) * width]
            at = count * width + i * rope
            q_ref[i, 1 + k, :, width:key_width] = packed_ref[:, at : at + rope]

    tops = []
    for i in range(count):
        limit = limits_ref[pl.ds(first + i, 1), :1]
        queries = q_ref[i].reshape(rows, -1)[:, :key_width]
        top = jnp.full((rows, 128), lowest_max, f32)
        for c in range(0, cached, chunk):
            keys = k_ref[base + i, :, c : c + chunk]
            part = jnp.dot(queries, keys, preferred_element_type=f32) * scale
            column = lax.broadcasted_iota(jnp.int32, (1, chunk), 1) + c
            part = jnp.where(column < limit, part, masked_score)
            scores[i][:, c : c + chunk] = part
            for at in range(0, chunk, 128):
                top = jnp.maximum(top, part[:, at : at + 128])
        tops.append(jnp.max(top, axis=1, keepdims=True))

    for i in range(count):
        total = jnp.zeros((rows, 128), f32)
        for c in range(0, cached, chunk):
            weights = jnp.exp2(scores[i][:, c : c + chunk] - tops[i])
            for at in range(0, chunk, 128):
                total = total + weights[:, at : at + 128]
            part = lax.dot_general(
                weights.astype(bf16),
                k_ref[base + i, :width, c : c + chunk],
                (((1,), (1,)), ((), ())),
                preferred_element_type=f32,
            )
            mixed = part if c == 0 else mixed + part
        total = jnp.sum(total, axis=1, keepdims=True)
        at = slice(i * share, (i + 1) * share)
        out_ref[:, at, :width] = mixed.astype(bf16).reshape(owners, share, width)
        out_ref[:, at, width:] = split_stats(tops[i], total, rows).astype(bf16).reshape(owners, share, 128)


def fresh_kernel(scale, steps, heads, info_ref, limits_ref, own_ref, new_ref, out_ref):
    requests, share, _ = own_ref.shape
    key_width = new_ref.shape[1]
    width = out_ref.shape[1]
    requests_rows = out_ref.shape[0] - 16
    stats = []
    fresh = new_ref[...]
    shape = (share, fresh.shape[0])
    key = lax.broadcasted_iota(jnp.int32, shape, 1)
    step = (lax.broadcasted_iota(jnp.int32, shape, 0) // heads) % steps
    counted = limits_ref[requests : requests + 1, :1] == 0
    for i in range(requests_rows // share):
        request = info_ref[0] + i
        scores = (
            lax.dot_general(
                own_ref[request][:, :key_width], fresh, (((1,), (1,)), ((), ())), preferred_element_type=f32
            )
            * scale
        )
        visible = (key % requests == request) & (key // requests <= step) & counted
        scores = jnp.where(visible, scores, masked_score)
        top = jnp.maximum(jnp.max(scores, axis=1, keepdims=True), lowest_max)
        weights = jnp.exp2(scores - top)
        total = jnp.sum(weights, axis=1, keepdims=True)
        mixed = jnp.dot(weights.astype(bf16), fresh[:, :width], preferred_element_type=f32)
        out_ref[i * share : (i + 1) * share, :] = mixed.astype(bf16)
        stats.append(split_stats(top, total, share))
    out_ref[requests_rows:, :] = jnp.zeros((16, width), bf16)
    out_ref[requests_rows:, :requests_rows] = jnp.concatenate(stats, axis=0).T[:16].astype(bf16)


def merge_parts(parts, width):
    tops = []
    sums = []
    for part in parts:
        stat = part[:, width:].astype(f32)
        tops.append(stat[:, 0:1] + stat[:, 1:2] + stat[:, 2:3])
        sums.append(stat[:, 3:4] + stat[:, 4:5])
    peak = functools.reduce(jnp.maximum, tops)
    weights = [jnp.exp2(t - peak) for t in tops]
    weight_sum = sum(w * s for w, s in zip(weights, sums))
    merged = sum(w * part[:, :width].astype(f32) for w, part in zip(weights, parts))
    return merged, peak, weight_sum


def pair_kernel(first, a_ref, b_ref, *sent_refs):
    width = sent_refs[0].shape[1]
    rows = sent_refs[0].shape[0] - 16
    for owner, sent_ref in enumerate(sent_refs, first):
        merged, peak, weight_sum = merge_parts((a_ref[owner], b_ref[owner]), width)
        sent_ref[:rows, :] = merged.astype(bf16)
        sent_ref[rows:, :] = jnp.zeros((16, width), bf16)
        sent_ref[rows:, :rows] = split_stats(peak, weight_sum, rows).T[:16].astype(bf16)


def project_kernel(heads, *refs):
    *parts, up_ref, out_ref = refs
    parts = [part[...] for part in parts]
    rows = out_ref.shape[0] - 16
    weights, peak, weight_sum = merge_rows(parts, rows)
    mixed = weigh(parts, weights, rows)
    high = mixed.astype(bf16)
    both = jnp.concatenate([high, (mixed - high.astype(f32)).astype(bf16)], axis=0)
    value_width = out_ref.shape[1]
    head = lax.broadcasted_iota(jnp.int32, (rows, value_width), 0) % heads
    values = jnp.zeros((rows, value_width), f32)
    for h in range(0, heads, 2):
        two = jnp.concatenate([up_ref[h], up_ref[h + 1]], axis=1)
        part = jnp.dot(both, two, preferred_element_type=f32)
        part = part[:rows] + part[rows:]
        values = jnp.where(head == h, part[:, :value_width], values)
        values = jnp.where(head == h + 1, part[:, value_width:], values)
    out_ref[:rows, :] = values.astype(bf16)
    out_ref[rows:, :] = stat_rows(peak, weight_sum)


def merge_rows(parts, rows):
    tops = []
    sums = []
    for part in parts:
        stat = part[rows:, :rows].astype(f32)
        tops.append(stat[0:1] + stat[1:2] + stat[2:3])
        sums.append(stat[3:4] + stat[4:5])
    tops = jnp.concatenate(tops, axis=0)
    peak = jnp.max(tops, axis=0, keepdims=True)
    weights = jnp.exp2(tops - peak)
    weight_sum = jnp.sum(weights * jnp.concatenate(sums, axis=0), axis=0, keepdims=True)
    return weights, peak, weight_sum


def weigh(parts, weights, rows):
    spread = jnp.concatenate([weights, jnp.zeros((128 - len(parts), weights.shape[1]), f32)], axis=0).T
    return sum(part[:rows, :].astype(f32) * spread[:rows, i : i + 1] for i, part in enumerate(parts))


def middle_kernel(*refs):
    *parts, out_ref = refs
    parts = [part[...] for part in parts]
    rows = out_ref.shape[0] - 16
    weights, peak, weight_sum = merge_rows(parts, rows)
    out_ref[:rows, :] = weigh(parts, weights, rows).astype(bf16)
    out_ref[rows:, :] = stat_rows(peak, weight_sum)


def finish_kernel(*refs):
    *parts, out_ref = refs
    parts = [part[...] for part in parts]
    steps, half = out_ref.shape[:2]
    rows = steps * half * out_ref.shape[2]
    weights, _, weight_sum = merge_rows(parts, rows)
    result = weigh(parts, weights / weight_sum, rows)
    result = result.astype(bf16).reshape(half, steps, *out_ref.shape[2:])
    for b in range(half):
        out_ref[:, b] = result[b]


def place_kernel(info_ref, own_ref, other_ref, out_ref):
    half = own_ref.shape[1]
    first = info_ref[0]
    out_ref[:, pl.ds(first, half)] = own_ref[...]
    out_ref[:, pl.ds(half - first, half)] = other_ref[...]


def on_device(
    query_heads, up_keys, up_values, latent_cache, new_latent, context_lengths, positions
):
    steps, requests, heads, query_width = query_heads.shape
    nope = up_keys.shape[1]
    width = up_keys.shape[2]
    key_width = latent_cache.shape[2]
    rope = key_width - width
    value_width = up_values.shape[2]
    cached = latent_cache.shape[1]
    owners = lax.axis_size("head")
    plane = lax.axis_size("z") * lax.axis_size("x")
    pairs = steps * requests
    half = requests // 2
    scale = float(query_width) ** (-0.5) * log2_e

    core = lax.axis_index("core")
    slot = lax.axis_index(("z", "x", "core", "head"))

    vmem = pl.BlockSpec(memory_space=pltpu.VMEM)
    smem = pl.BlockSpec(memory_space=pltpu.SMEM)
    small = pltpu.CompilerParams(vmem_limit_bytes=12 * 2**20)
    anywhere = pl.BlockSpec(memory_space=pltpu.HBM)
    wide = 640
    in_hbm = functools.partial(pltpu.with_memory_space_constraint, memory_space=pltpu.HBM)
    core32 = core.astype(jnp.int32)
    own_first = (core32 * half).reshape(1)
    other_first = (half - core32 * half).reshape(1)
    first_row = (slot.astype(jnp.int32) * cached).reshape(1)
    place = lax.axis_index(("z", "x")).astype(jnp.int32).reshape(1)
    chunk = half * steps * heads
    own_queries, sent_queries, new_keys, limits = pl.pallas_call(
        functools.partial(queries_kernel, steps),
        in_specs=[smem] * 4 + [anywhere] * 5,
        out_specs=[vmem] * 4,
        out_shape=(
            jax.ShapeDtypeStruct((requests, steps * heads, wide), bf16),
            jax.ShapeDtypeStruct((steps * heads, half * key_width), bf16),
            jax.ShapeDtypeStruct((pairs, key_width), bf16),
            jax.ShapeDtypeStruct((8, 128), jnp.int32),
        ),
        scratch_shapes=[
            pltpu.SMEM((requests,), jnp.int32),
            pltpu.SMEM((requests,), jnp.int32),
            pltpu.VMEM((pairs, heads, query_width), bf16),
            pltpu.VMEM(up_keys.shape, bf16),
            pltpu.VMEM(new_latent.shape, bf16),
            pltpu.VMEM((pairs, heads, width), f32),
            pltpu.SemaphoreType.DMA((8,)),
        ],
        compiler_params=pltpu.CompilerParams(vmem_limit_bytes=24 * 2**20),
        name="queries",
    )(
        other_first,
        own_first,
        first_row,
        place,
        in_hbm(positions),
        in_hbm(context_lengths),
        in_hbm(query_heads.reshape(pairs, heads, query_width)),
        in_hbm(up_keys),
        in_hbm(new_latent),
    )

    def over_head(array, k):
        return lax.ppermute(array, "head", [(i, i ^ k) for i in range(owners)])

    swap = [(0, 1), (1, 0)]
    partners = (2, 3, 1)
    got = [over_head(sent_queries, k) for k in partners]
    fresh = pl.pallas_call(
        functools.partial(fresh_kernel, scale, steps, heads),
        in_specs=[smem, vmem, vmem, vmem],
        out_specs=vmem,
        out_shape=jax.ShapeDtypeStruct((chunk + 16, width), bf16),
        compiler_params=small,
        cost_estimate=pl.CostEstimate(flops=10**9, bytes_accessed=4 * 10**6, transcendentals=0),
        name="fresh",
    )(own_first, limits, own_queries, new_keys)
    cache = jnp.swapaxes(latent_cache, 1, 2)
    staged_shape = pltpu.VMEM((half, key_width, cached), bf16)
    in_vmem = functools.partial(pltpu.with_memory_space_constraint, memory_space=pltpu.VMEM)
    staged = pl.pallas_call(
        stage_kernel,
        in_specs=[smem, anywhere],
        out_specs=vmem,
        out_shape=staged_shape,
        scratch_shapes=[pltpu.SemaphoreType.DMA((half,))],
        compiler_params=small,
        cost_estimate=pl.CostEstimate(flops=0, bytes_accessed=2 * half * key_width * cached, transcendentals=0),
        name="stage",
    )(other_first, in_hbm(cache))
    got[0], staged = lax.optimization_barrier((got[0], staged))
    passed = [lax.ppermute(g, "core", swap) for g in got]

    rows = owners * steps * heads

    def attend(first, got, keys):
        return pl.pallas_call(
            functools.partial(attention_kernel, scale),
            in_specs=[smem] + [vmem] * 6,
            out_specs=vmem,
            scratch_shapes=[pltpu.VMEM((half, owners, steps * heads, wide), bf16)]
            + [pltpu.VMEM((rows, cached), f32)] * half,
            out_shape=jax.ShapeDtypeStruct((owners, chunk, width + 128), bf16),
            compiler_params=pltpu.CompilerParams(vmem_limit_bytes=18 * 2**20),
            cost_estimate=pl.CostEstimate(
                flops=20 * half * rows * cached * (key_width + width),
                bytes_accessed=half * cached * key_width * 2,
                transcendentals=half * rows * cached,
            ),
            name="attention",
        )(first, limits, own_queries, *got, keys)

    other_part = lax.ppermute(attend(other_first, got, in_vmem(staged)), "core", swap)
    own_part = attend(own_first, passed, cache)
    def pair(first, count):
        return pl.pallas_call(
            functools.partial(pair_kernel, first),
            in_specs=[vmem] * 2,
            out_specs=[vmem] * count,
            out_shape=[pltpu.VMEM((chunk + 16, width), bf16)] * count,
            compiler_params=small,
            name="pair_merge",
        )(other_part, own_part)

    sent = dict(zip(partners, pair(1, owners - 1)))
    arrived = [over_head(sent[k], k) for k in (2, 3, 1)]
    (kept,) = pair(0, 1)
    part = pl.pallas_call(
        functools.partial(project_kernel, heads),
        in_specs=[vmem] * 6,
        out_specs=vmem,
        out_shape=jax.ShapeDtypeStruct((chunk + 16, value_width), bf16),
        compiler_params=small,
        name="project",
    )(kept, *arrived, fresh, up_values)

    def crossing(array, axis):
        size = lax.axis_size(axis)
        sides = [(i, c) for i in range(size) for c in range(2)]
        sibling = [lax.ppermute(array, "core", swap)]
        got = [
            lax.ppermute(array, (axis, "core"), [(2 * i + c, 2 * (i ^ k) + 1 - c) for i, c in sides])
            for k in (2, 3, 1)
        ]
        return sibling + got

    part = pl.pallas_call(
        middle_kernel,
        in_specs=[vmem] * 4,
        out_specs=vmem,
        out_shape=jax.ShapeDtypeStruct(part.shape, bf16),
        compiler_params=small,
        name="middle_merge",
    )(*crossing(part, "z"))
    own = pl.pallas_call(
        finish_kernel,
        in_specs=[vmem] * 4,
        out_specs=vmem,
        out_shape=jax.ShapeDtypeStruct((steps, half, heads, value_width), bf16),
        compiler_params=small,
        name="finish",
    )(*crossing(part, "x"))
    theirs = lax.ppermute(own, "core", swap)
    return pl.pallas_call(
        place_kernel,
        in_specs=[smem, vmem, vmem],
        out_specs=vmem,
        out_shape=jax.ShapeDtypeStruct((steps, requests, heads, value_width), bf16),
        compiler_params=small,
        name="place",
    )(own_first, own, theirs)


def solution(mesh):
    fine = Mesh(mesh.devices.reshape(4, 4, 2, 4), ("z", "x", "core", "head"))
    in_specs = (
        P(None, None, "head", None),
        P("head", None, None),
        P("head", None, None),
        P(None, ("z", "x", "core", "head"), None),
        P(),
        P(),
        P(),
    )
    out_specs = P(None, None, "head", None)
    return jax.shard_map(
        on_device, mesh=fine, in_specs=in_specs, out_specs=out_specs, check_vma=False
    )
```
